32 devices in a mesh: dp: 4 (over y, x), blk: 8 (over z, core).
Axes of the slice: x: 2, y: 2, z: 4, core: 2. Of those that a mesh axis runs over, the one named last changes fastest.
Arguments:
- visual_inputs: bfloat16 [4, 512, 1152], P('dp', 'blk'), may hold values from -0.38301617 to 0.38301617
- sentence_vectors: bfloat16 [4, 2048, 1152], P('dp', 'blk'), may hold values from -0.38301617 to 0.38301617
- paired_picture_index: int32 [4, 2048], P('dp', 'blk'), may hold values from 0 to 511, as said below
- visual_head_linear_map: bfloat16 [1152, 1152], replicated, may hold values from -3 to 3
- score_multiplier: float32 [], replicated, may hold values from 8 to 16
- score_offset: float32 [], replicated, may hold values from -6 to -3
Outputs:
- grad_features: float32 [4, 512, 1152], P('dp', 'blk')
- sentence_vector_adjoint: float32 [4, 2048, 1152], P('dp', 'blk')
- grad_weight: float32 [1152, 1152], replicated
The draws below stay inside these ranges and needn't reach their ends.
Inputs may be any that keep to these rules, and one draw needn't show every extreme that they name: `paired_picture_index`: within each loss group, every image index appears exactly 4 times among the labels.
All inputs are finite; a program needn't handle non-finite values.
Results may differ from the reference program's by a relative error of at most 0.0032.
Values may be sent and summed in bfloat16 or wider, within the bound.
No kernel may reach another device: no remote copies, remote signals or barrier semaphores. Data moves between devices by JAX's collectives and lax.ppermute only.
A program may use at most 128 MiB of HBM per device.

```python
import math
import jax
import jax.numpy as jnp
from jax import lax

D = 1152
IMG_GROUP = 512
TXT_GROUP = 2048
GROUPS = 4


topic_count = 128


col_norm = 4.6


def normal_table(key, shape):
    return jax.random.truncated_normal(key, -3.0, 3.0, shape, jnp.float32) * D ** (-0.5)


def pick_rows(table, chosen):
    return jax.vmap(lambda rows_table, rows_chosen: rows_table[rows_chosen])(table, chosen)


def common_parts(key):
    topics = jax.random.randint(jax.random.fold_in(key, 101), (GROUPS, IMG_GROUP), 0, topic_count)
    centers = normal_table(jax.random.fold_in(key, 102), (GROUPS, topic_count, D))
    own_parts = normal_table(jax.random.fold_in(key, 103), (GROUPS, IMG_GROUP, D))
    subkeys = jax.random.split(jax.random.fold_in(key, 105), GROUPS)
    shuffled = jax.vmap(lambda subkey: jax.random.permutation(subkey, TXT_GROUP))(subkeys)
    sentence_label_signs = (shuffled % IMG_GROUP).astype(jnp.int32)
    columns = jnp.exp(jax.random.uniform(jax.random.fold_in(key, 106), (D,), jnp.float32, 0.0, math.log(10.0)))
    image_centers = pick_rows(centers, topics)
    return (image_centers, own_parts, sentence_label_signs, columns)


def draw_visual_inputs(key, part):
    image_centers, own_parts, sentence_label_signs, columns = common_parts(key)
    key = jax.random.fold_in(key, 1)
    mixture = 0.7 * image_centers + 0.7 * own_parts
    lowest, highest = (0.3, 3.0)
    scales = jnp.exp(jax.random.uniform(key, (GROUPS, IMG_GROUP, 1), jnp.float32, math.log(lowest), math.log(highest)))
    return (mixture * scales).astype(jnp.bfloat16)


def draw_sentence_vectors(key, part):
    image_centers, own_parts, sentence_label_signs, columns = common_parts(key)
    key = jax.random.fold_in(key, 2)
    picked_centers = pick_rows(image_centers, sentence_label_signs)
    picked_own = pick_rows(own_parts, sentence_label_signs)
    caption_noise = normal_table(key, (GROUPS, TXT_GROUP, D))
    mixture = 0.6 * picked_centers + 0.6 * picked_own + 0.5 * caption_noise
    return (mixture * columns / col_norm).astype(jnp.bfloat16)


def draw_paired_picture_index(key, part):
    image_centers, own_parts, sentence_label_signs, columns = common_parts(key)
    return sentence_label_signs


def draw_visual_head_linear_map(key, part):
    image_centers, own_parts, sentence_label_signs, columns = common_parts(key)
    key = jax.random.fold_in(key, 4)
    mixing = jax.random.truncated_normal(key, -3.0, 3.0, (D, D), jnp.float32) * (0.7 * D ** (-0.5))
    identity = jnp.eye(D, dtype=jnp.float32)
    return ((identity + mixing) * columns[None, :] / col_norm).astype(jnp.bfloat16)


def setup_inputs(seed: int = 0) -> dict:
    streams_of = jax.random.split(jax.random.key(seed), 7)
    visual_inputs = draw_visual_inputs(jax.random.fold_in(streams_of[6], 71), 0)
    sentence_vectors = draw_sentence_vectors(jax.random.fold_in(streams_of[6], 71), 0)
    paired_picture_index = draw_paired_picture_index(jax.random.fold_in(streams_of[6], 71), 0)
    visual_head_linear_map = draw_visual_head_linear_map(jax.random.fold_in(streams_of[6], 71), 0)
    score_multiplier = jnp.clip(jnp.exp(jax.random.uniform(streams_of[4], (), jnp.float32, math.log(8.0), math.log(16.0))), 8.0, 16.0)
    score_offset = jnp.clip(jax.random.uniform(streams_of[5], (), jnp.float32, -6.0, -3.0), -6.0, -3.0)
    return dict(visual_inputs=visual_inputs, sentence_vectors=sentence_vectors, paired_picture_index=paired_picture_index, visual_head_linear_map=visual_head_linear_map, score_multiplier=score_multiplier, score_offset=score_offset)


def whole_batch_case(picture_tile_slice, sentence_tile_slice, sentence_label_signs, visual_head_linear_map, score_multiplier, score_offset):
    embedding = jnp.dot(picture_tile_slice, visual_head_linear_map, preferred_element_type=jnp.float32)
    inv_norm = lax.rsqrt(lax.optimization_barrier(jnp.sum(embedding * embedding, axis=1, keepdims=True)) + 1e-06)
    unit_f = embedding * inv_norm
    unitlength_brainfloat = unit_f.astype(jnp.bfloat16)
    pairwise_scores = score_multiplier * jnp.dot(unitlength_brainfloat, sentence_tile_slice.T, preferred_element_type=jnp.float32) + score_offset
    picture_indices = jnp.arange(IMG_GROUP, dtype=jnp.int32)
    pair_sign = jnp.where(sentence_label_signs[None, :] == picture_indices[:, None], 1.0, -1.0).astype(jnp.float32)
    score_adjoint = (-pair_sign * jax.nn.sigmoid(-pair_sign * pairwise_scores)).astype(jnp.bfloat16)
    unitlength_adjoint = score_multiplier * jnp.dot(score_adjoint, sentence_tile_slice, preferred_element_type=jnp.float32)
    sentence_vector_adjoint = score_multiplier * jnp.dot(score_adjoint.T, unitlength_brainfloat, preferred_element_type=jnp.float32)
    radial = lax.optimization_barrier(jnp.sum(unit_f * unitlength_adjoint, axis=1, keepdims=True))
    grad_embed = ((unitlength_adjoint - unit_f * radial) * inv_norm).astype(jnp.bfloat16)
    grad_features = jnp.dot(grad_embed, visual_head_linear_map.T, preferred_element_type=jnp.float32)
    weight_term = jnp.dot(picture_tile_slice.T, grad_embed, preferred_element_type=jnp.float32)
    return (grad_features, sentence_vector_adjoint, weight_term)

def reference(visual_inputs, sentence_vectors, paired_picture_index, visual_head_linear_map, score_multiplier, score_offset):

    def per_group(batch_partners):
        return whole_batch_case(batch_partners[0], batch_partners[1], batch_partners[2], visual_head_linear_map, score_multiplier, score_offset)
    grad_features, sentence_vector_adjoint, weight_terms = lax.map(per_group, (visual_inputs, sentence_vectors, paired_picture_index))
    grad_weight = lax.optimization_barrier(jnp.sum(weight_terms, axis=0)) / GROUPS
    return (grad_features, sentence_vector_adjoint, grad_weight)
```

```python
import jax
import jax.numpy as jnp
from jax import lax
from jax.sharding import PartitionSpec as P

FIRST = (((0,), (0,)), ((), ()))
LAST = (((1,), (1,)), ((), ()))
F32 = jnp.float32
BF16 = jnp.bfloat16


def dot(a, b, dims=(((1,), (0,)), ((), ()))):
    return lax.dot_general(a, b, dims, preferred_element_type=F32)


def on_device(x, captions, labels, weight, scale, offset):
    x, captions, labels = x[0], captions[0], labels[0]
    n_img, depth = x.shape
    n_cap = captions.shape[0]
    nd, nb = lax.axis_size("dp"), lax.axis_size("blk")
    nz = nb // 2
    d, b = lax.axis_index("dp"), lax.axis_index("blk")
    z, c = b // 2, b % 2

    def along_z(v, k):
        return lax.ppermute(
            v, "blk", [(i, ((i // 2 + k) % nz) * 2 + i % 2) for i in range(nb)]
        )

    def swap(v):
        return lax.ppermute(v, "blk", [(i, i ^ 1) for i in range(nb)])

    def in_plane(v, kd, kc):
        perm = []
        for i in range(nd):
            for j in range(nb):
                perm.append((i * nb + j, ((i + kd) % nd) * nb + (j ^ kc)))
        return lax.ppermute(v, ("dp", "blk"), perm)

    xs = jnp.concatenate([x] + [along_z(x, k) for k in range(1, nz)])
    caps = jnp.concatenate([captions, swap(captions)])
    labs = jnp.concatenate([labels, swap(labels)])
    ids = jnp.concatenate(
        [
            (((z - k + nz) % nz) * 2 + c) * n_img + jnp.arange(n_img, dtype=jnp.int32)
            for k in range(nz)
        ]
    )
    embed = dot(xs, weight)
    inv_norm = lax.rsqrt(jnp.sum(embed * embed, axis=1, keepdims=True) + 1e-06)
    unit_f = embed * inv_norm
    unit = unit_f.astype(BF16)
    logits = scale * dot(unit, caps, LAST) + offset
    sign = jnp.where(labs[None, :] == ids[:, None], 1.0, -1.0).astype(F32)
    dlogit = (-sign * jax.nn.sigmoid(-sign * logits)).astype(BF16)

    part = scale * dot(dlogit, caps)
    own = part[:n_img]
    for k in range(1, nz):
        back = along_z(part[k * n_img : (k + 1) * n_img].astype(BF16), nz - k)
        own = own + back.astype(F32)

    adjoint = scale * dot(dlogit, unit, FIRST)
    adjoint = adjoint[:n_cap] + swap(adjoint[n_cap:])

    u = unit_f[:n_img]
    radial = jnp.sum(u * own, axis=1, keepdims=True)
    ge = ((own - u * radial) * inv_norm[:n_img]).astype(BF16)
    grad_features = dot(ge, weight, LAST)

    cols = depth // nz
    blocks = []
    for k in range(nz):
        v = lax.dynamic_slice_in_dim(ge, ((z + k) % nz) * cols, cols, 1)
        blocks.append(along_z(v, k) if k else v)
    wpart = dot(xs, jnp.concatenate(blocks), FIRST)
    rows = depth // (nd * 2)
    piece = None
    for kc in range(2):
        for kd in range(nd):
            to = ((d + kd) % nd) * 2 + (c ^ kc)
            v = lax.dynamic_slice_in_dim(wpart, to * rows, rows, 0)
            if kd or kc:
                v = in_plane(v.astype(BF16), kd, kc).astype(F32)
            piece = v if piece is None else piece + v
    piece = (piece / nd).astype(BF16)
    whole = lax.all_gather(piece, ("dp", "blk"), axis=0)
    whole = whole.reshape(nd, nz, 2, rows, cols).transpose(0, 2, 3, 1, 4)
    grad_weight = whole.reshape(depth, depth).astype(F32)
    return (grad_features[None], adjoint[None], grad_weight)


def solution(mesh):
    placed = (P("dp", "blk", None), P("dp", "blk", None), P("dp", "blk"), P(), P(), P())
    return jax.shard_map(
        on_device,
        mesh=mesh,
        in_specs=placed,
        out_specs=(P("dp", "blk", None), P("dp", "blk", None), P()),
        check_vma=False,
    )
```

```python
import functools

import jax
import jax.numpy as jnp
from jax import lax
from jax.experimental import pallas as pl
from jax.experimental.pallas import tpu as pltpu
from jax.sharding import PartitionSpec as P

FIRST = (((0,), (0,)), ((), ()))
LAST = (((1,), (1,)), ((), ()))
F32 = jnp.float32
BF16 = jnp.bfloat16


def dot(a, b, dims=(((1,), (0,)), ((), ()))):
    return lax.dot_general(a, b, dims, preferred_element_type=F32)


def weight_kernel(n_x, n_img, lanes, factor, has_acc, *refs):
    out = refs[-1]
    acc = refs[0] if has_acc else None
    refs = refs[has_acc:-1]
    depth, width = out.shape[0], out.shape[1] // 3
    xs, gs = refs[:n_x], refs[n_x:]

    def columns(j, carry):
        tile = pl.ds(pl.multiple_of(j * width, width), width)
        x_t, g = [], []
        for x_ref, g_ref in zip(xs, gs):
            for at in range(x_ref.shape[0] // depth):
                x_t.append(x_ref[at * depth : (at + 1) * depth, lanes])
                g.append(g_ref[at * n_img : (at + 1) * n_img, tile])
        total = dot(jnp.concatenate(x_t, axis=1), jnp.concatenate(g))
        if has_acc:
            total = total + acc[:, tile]
        out[:, tile] = total * factor
        return carry

    lax.fori_loop(0, 3, columns, 0)


def weight_sum(acc, xs, gs, first, n_img, factor):
    depth = gs[0].shape[1]
    images = 2 * sum(g.shape[0] for g in gs)
    if images > 2048:
        for x, g in zip(xs, gs):
            for at in range(g.shape[0] // n_img):
                x_t = x[at * depth : (at + 1) * depth, first : first + n_img]
                term = dot(x_t, g[at * n_img : (at + 1) * n_img])
                acc = term if acc is None else acc + term
        return acc
    has_acc = acc is not None
    operands = ([acc] if has_acc else []) + xs + gs
    return pl.pallas_call(
        functools.partial(
            weight_kernel,
            len(xs),
            n_img,
            slice(first, first + n_img),
            factor,
            int(has_acc),
        ),
        out_shape=jax.ShapeDtypeStruct((depth, depth), F32),
        in_specs=[pl.BlockSpec(memory_space=pltpu.VMEM)] * len(operands),
        out_specs=pl.BlockSpec(memory_space=pltpu.VMEM),
        compiler_params=pltpu.CompilerParams(vmem_limit_bytes=48 * 2**20),
        cost_estimate=pl.CostEstimate(
            flops=2 * images * depth * depth,
            bytes_accessed=4 * images * depth + 4 * depth * depth,
            transcendentals=0,
        ),
    )(*operands)


def on_device(x, captions, labels, weight, scale, offset):
    x, captions, labels = x[0], captions[0], labels[0]
    n_img, depth = x.shape
    n_cap = captions.shape[0]
    nd, nb = lax.axis_size("dp"), lax.axis_size("blk")
    nz = nb // 2
    b = lax.axis_index("blk")
    z, c = b // 2, b % 2

    def along_z(v, k):
        return lax.ppermute(v, "blk", [(i, i ^ (2 * k)) for i in range(nb)])

    def along_d(v, k):
        return lax.ppermute(v, "dp", [(i, i ^ k) for i in range(nd)])

    def swap(v):
        return lax.ppermute(v, "blk", [(i, i ^ 1) for i in range(nb)])

    xs = jnp.concatenate([x] + [along_z(x, k) for k in range(1, nz)])
    caps = jnp.concatenate([captions, swap(captions)])
    labs = jnp.concatenate([labels, swap(labels)])
    ids = jnp.concatenate(
        [
            ((z ^ k) * 2 + c) * n_img + jnp.arange(n_img, dtype=jnp.int32)
            for k in range(nz)
        ]
    )
    bits = nd.bit_length() - 1

    def over_d(v):
        for i in range(bits):
            perm = []
            for j in range(nd):
                for m in range(nb):
                    to = j ^ (1 << ((i + m % 2) % bits))
                    perm.append((j * nb + m, to * nb + m))
            v = jnp.concatenate(v) if i else v[0]
            v = [v, lax.ppermute(v, ("dp", "blk"), perm)]
        return v

    x_t = over_d([xs.T])

    embed = dot(xs, weight)
    inv_norm = lax.rsqrt(jnp.sum(embed * embed, axis=1, keepdims=True) + 1e-06)
    unit_f = embed * inv_norm
    unit = unit_f.astype(BF16)
    logits = scale * dot(unit, caps, LAST) + offset
    sign = jnp.where(labs[None, :] == ids[:, None], 1.0, -1.0).astype(F32)
    dlogit = (-sign * jax.nn.sigmoid(-sign * logits)).astype(BF16)

    part = scale * dot(dlogit, caps)
    own = part[:n_img]
    back = [
        along_z(part[k * n_img : (k + 1) * n_img].astype(BF16), k)
        for k in range(1, nz)
    ]
    back, x_t = lax.optimization_barrier((back, x_t))
    for v in back:
        own = own + v.astype(F32)

    adjoint = scale * dot(dlogit, unit, FIRST)
    adjoint = adjoint[:n_cap] + swap(adjoint[n_cap:])

    u = unit_f[:n_img]
    radial = jnp.sum(u * own, axis=1, keepdims=True)
    ge = ((own - u * radial) * inv_norm[:n_img]).astype(BF16)
    grad_features = dot(ge, weight, LAST)

    near = [ge] + [along_z(ge, k) for k in range(1, nz // 2)]
    far = [along_z(ge, k) for k in range(nz // 2, nz)]
    n_near = n_img * (nz // 2)
    near, far = over_d([jnp.concatenate(near)]), over_d([jnp.concatenate(far)])
    small = nd * nb * n_img <= 2048
    if small:
        x_t, near, far = (v + [swap(p) for p in v] for v in (x_t, near, far))
    grad_weight = weight_sum(None, x_t, near, 0, n_near, 1.0)
    grad_weight = weight_sum(grad_weight, x_t, far, n_near, n_near, 1.0 / nd)
    if not small:
        grad_weight = (grad_weight + swap(grad_weight)) / nd
    return (grad_features[None], adjoint[None], grad_weight)


def solution(mesh):
    placed = (P("dp", "blk", None), P("dp", "blk", None), P("dp", "blk"), P(), P(), P())
    return jax.shard_map(
        on_device,
        mesh=mesh,
        in_specs=placed,
        out_specs=(P("dp", "blk", None), P("dp", "blk", None), P()),
        check_vma=False,
    )
```

```python
import functools

import jax
import jax.numpy as jnp
from jax import lax
from jax.experimental import pallas as pl
from jax.experimental.pallas import tpu as pltpu
from jax.sharding import PartitionSpec as P

FIRST = (((0,), (0,)), ((), ()))
LAST = (((1,), (1,)), ((), ()))
F32 = jnp.float32
BF16 = jnp.bfloat16


def dot(a, b, dims=(((1,), (0,)), ((), ()))):
    return lax.dot_general(a, b, dims, preferred_element_type=F32)


def turn_kernel(sizes, n_chunk, *refs):
    out, refs = refs[-1], refs[:-1]
    half = len(refs) // 2
    per = n_chunk // half
    step = refs[0].shape[0] // per
    col = 0
    for core in range(2):
        first = 0
        for size in sizes:
            rows = []
            for chunk in range(n_chunk):
                at = (chunk % per) * step + first
                rows.append(refs[core * half + chunk // per][at : at + size, :])
            rows = jnp.concatenate(rows)
            out[:, col : col + rows.shape[0]] = rows.T
            col += rows.shape[0]
            first += size


def turned(xs, sizes, n_chunk):
    images = sum(v.shape[0] for v in xs)
    depth = xs[0].shape[1]
    return pl.pallas_call(
        functools.partial(turn_kernel, sizes, n_chunk),
        out_shape=jax.ShapeDtypeStruct((depth, images), BF16),
        in_specs=[pl.BlockSpec(memory_space=pltpu.VMEM)] * len(xs),
        out_specs=pl.BlockSpec(memory_space=pltpu.VMEM),
        compiler_params=pltpu.CompilerParams(vmem_limit_bytes=24 * 2**20),
        cost_estimate=pl.CostEstimate(
            flops=0, bytes_accessed=4 * images * depth, transcendentals=0
        ),
    )(*xs)


def weight_kernel(factor, x_t, *refs):
    gs, (out, stacked, tiles, sems) = refs[:-4], refs[-4:]
    at = 0
    for g in gs:
        stacked[at : at + g.shape[0], :] = g[...]
        at += g.shape[0]
    n, rows = tiles.shape[:2]
    copies = []
    for i in range(n):
        here = slice(i * rows, (i + 1) * rows)
        tiles[i] = dot(x_t[here, :], stacked[...]) * factor
        copies.append(pltpu.make_async_copy(tiles.at[i], out.at[here, :], sems.at[i]))
        copies[-1].start()
    for copy in copies:
        copy.wait()


def weight_sum(x_t, gs, factor):
    depth, images = x_t.shape
    n = 3
    return pl.pallas_call(
        functools.partial(weight_kernel, factor),
        out_shape=jax.ShapeDtypeStruct((depth, depth), F32),
        in_specs=[pl.BlockSpec(memory_space=pltpu.VMEM)] * (1 + len(gs)),
        out_specs=pl.BlockSpec(memory_space=pl.ANY),
        scratch_shapes=[
            pltpu.VMEM((images, depth), BF16),
            pltpu.VMEM((n, depth // n, depth), F32),
            pltpu.SemaphoreType.DMA((n,)),
        ],
        compiler_params=pltpu.CompilerParams(vmem_limit_bytes=28 * 2**20),
        cost_estimate=pl.CostEstimate(
            flops=2 * images * depth * depth,
            bytes_accessed=4 * images * depth + 4 * depth * depth,
            transcendentals=0,
        ),
    )(x_t, *gs)


def on_device(x, captions, labels, weight, scale, offset):
    x, captions, labels = x[0], captions[0], labels[0]
    n_img, depth = x.shape
    n_cap = captions.shape[0]
    nd, nb = lax.axis_size("dp"), lax.axis_size("blk")
    nz = nb // 2
    b = lax.axis_index("blk")
    z, c = b // 2, b % 2

    def along_z(v, k):
        return lax.ppermute(v, "blk", [(i, i ^ (2 * k)) for i in range(nb)])

    def swap(v):
        return lax.ppermute(v, "blk", [(i, i ^ 1) for i in range(nb)])

    xs = jnp.concatenate([x] + [along_z(x, k) for k in range(1, nz)])
    caps = jnp.concatenate([captions, swap(captions)])
    labs = jnp.concatenate([labels, swap(labels)])
    ids = jnp.concatenate(
        [
            ((z ^ k) * 2 + c) * n_img + jnp.arange(n_img, dtype=jnp.int32)
            for k in range(nz)
        ]
    )
    bits = nd.bit_length() - 1

    def step_d(v, i):
        perm = []
        for j in range(nd):
            for m in range(nb):
                to = j ^ (1 << ((i + m % 2) % bits))
                perm.append((j * nb + m, to * nb + m))
        return lax.ppermute(v, ("dp", "blk"), perm)

    def over_d(v, first=None):
        v = [v]
        for i in range(bits):
            if i:
                v = [jnp.concatenate(v)]
            v.append(step_d(v[0], i) if i or first is None else first)
        return v

    x_first = step_d(xs, 0)
    embed = dot(xs, weight)
    inv_norm = lax.rsqrt(jnp.sum(embed * embed, axis=1, keepdims=True) + 1e-06)
    unit_f = embed * inv_norm
    unit = unit_f.astype(BF16)
    logits = scale * dot(unit, caps, LAST) + offset
    sign = jnp.where(labs[None, :] == ids[:, None], 1.0, -1.0).astype(F32)
    dlogit = (-sign * jax.nn.sigmoid(-sign * logits)).astype(BF16)

    part = scale * dot(dlogit, caps)
    own = part[:n_img]
    sent = [part[k * n_img : (k + 1) * n_img].astype(BF16) for k in range(1, nz)]
    back = [along_z(v, k + 1) for k, v in enumerate(sent)]
    x_first = lax.optimization_barrier((x_first, sent))[0]
    x_own = over_d(xs, x_first)
    back = lax.optimization_barrier((back, x_own[0]))[0]
    for v in back:
        own = own + v.astype(F32)

    dlogit = lax.optimization_barrier((dlogit, sent))[0]
    adjoint = scale * dot(dlogit, unit, FIRST)
    adjoint_other = swap(adjoint[n_cap:])
    adjoint = adjoint[:n_cap] + adjoint_other

    u = unit_f[:n_img]
    radial = jnp.sum(u * own, axis=1, keepdims=True)
    ge = ((own - u * radial) * inv_norm[:n_img]).astype(BF16)
    ge = lax.optimization_barrier((ge, adjoint_other))[0]
    grad_features = dot(ge, weight, LAST)

    half = nz // 2
    blocks = [ge] + [along_z(ge, k) for k in range(1, nz)]
    groups = [blocks[:1], blocks[1:half], blocks[half:]]
    sizes = [n_img * len(g) for g in groups]
    g_own = [over_d(jnp.concatenate(g)) for g in groups]
    if nd * nb * n_img <= 2048:
        for i in range(2):
            g_own[i] = [jnp.concatenate(g_own[i])]
        g_own = [v for g in g_own for v in g]
        x_t = turned(x_own + [swap(v) for v in x_own], sizes, nd)
        g_own[-1] = lax.optimization_barrier((g_own[-1], x_t))[0]
        grad_weight = weight_sum(x_t, g_own + [swap(v) for v in g_own], 1.0 / nd)
    else:
        grad_weight = 0.0
        n_own = nz * n_img
        for i, x_part in enumerate(x_own):
            for at in range(nd // 2):
                g_part = [g[i][at * m : (at + 1) * m] for m, g in zip(sizes, g_own)]
                grad_weight = grad_weight + dot(
                    x_part[at * n_own : (at + 1) * n_own],
                    jnp.concatenate(g_part),
                    FIRST,
                )
        grad_weight = (grad_weight + swap(grad_weight)) / nd
    return (grad_features[None], adjoint[None], grad_weight)


def solution(mesh):
    placed = (P("dp", "blk", None), P("dp", "blk", None), P("dp", "blk"), P(), P(), P())
    return jax.shard_map(
        on_device,
        mesh=mesh,
        in_specs=placed,
        out_specs=(P("dp", "blk", None), P("dp", "blk", None), P()),
        check_vma=False,
    )
```

```python
import functools

import jax
import jax.numpy as jnp
from jax import lax
from jax.experimental import pallas as pl
from jax.experimental.pallas import tpu as pltpu
from jax.sharding import PartitionSpec as P

FIRST = (((0,), (0,)), ((), ()))
LAST = (((1,), (1,)), ((), ()))
F32 = jnp.float32
BF16 = jnp.bfloat16


def dot(a, b, dims=(((1,), (0,)), ((), ()))):
    return lax.dot_general(a, b, dims, preferred_element_type=F32)


def after(v, *others):
    return lax.optimization_barrier((v, others))[0]


def score_kernel(nz, scale, offset, index, embed, *refs):
    labels, captions, refs = refs[:2], refs[2:4], refs[4:]
    own, unit_own, inv_own, unit, dlogit = refs[:5]
    sent, (caps, sems) = refs[5:-2], refs[-2:]
    n_img, n_cap = embed.shape[0] // nz, captions[0].shape[0]
    copies = []
    for i in range(2):
        here = caps.at[i * n_cap : (i + 1) * n_cap, :]
        copies.append(pltpu.make_async_copy(captions[i], here, sems.at[i]))
        copies[-1].start()
    embed = embed[...]
    inv_norm = lax.rsqrt(jnp.sum(embed * embed, axis=1, keepdims=True) + 1e-06)
    unit_f = embed * inv_norm
    unit_own[...] = unit_f[:n_img]
    inv_own[...] = inv_norm[:n_img]
    u = unit_f.astype(BF16)
    unit[...] = u
    ids = []
    for k in range(nz):
        first = (index[0] ^ (2 * k)) * n_img
        ids.append(first + lax.broadcasted_iota(jnp.int32, (n_img, 1), 0))
    ids = jnp.concatenate(ids)
    labs = jnp.concatenate([v[...] for v in labels], axis=1)
    sign = jnp.where(labs == ids, 1.0, -1.0).astype(F32)
    for copy in copies:
        copy.wait()
    logits = scale[0] * dot(u, caps[...], LAST) + offset[0]
    d = (-sign * jax.nn.sigmoid(-sign * logits)).astype(BF16)
    dlogit[...] = d
    part = scale[0] * dot(d, caps[...])
    own[...] = part[:n_img]
    for k in range(1, nz):
        sent[k - 1][...] = part[k * n_img : (k + 1) * n_img].astype(BF16)


def scores(nz, scale, offset, index, embed, labels, captions):
    images, depth = embed.shape
    n_img, n_cap = images // nz, captions[0].shape[0]
    caps = 2 * n_cap
    smem = pl.BlockSpec(memory_space=pltpu.SMEM)
    vmem = pl.BlockSpec(memory_space=pltpu.VMEM)
    block = jax.ShapeDtypeStruct((n_img, depth), F32)
    outs = [
        block,
        block,
        jax.ShapeDtypeStruct((n_img, 1), F32),
        jax.ShapeDtypeStruct((images, depth), BF16),
        jax.ShapeDtypeStruct((images, caps), BF16),
    ] + [jax.ShapeDtypeStruct((n_img, depth), BF16)] * (nz - 1)
    return pl.pallas_call(
        functools.partial(score_kernel, nz),
        out_shape=outs,
        in_specs=[smem] * 3
        + [vmem] * 3
        + [pl.BlockSpec(memory_space=pl.ANY)] * 2,
        out_specs=[vmem] * len(outs),
        scratch_shapes=[pltpu.VMEM((caps, depth), BF16), pltpu.SemaphoreType.DMA((2,))],
        compiler_params=pltpu.CompilerParams(
            vmem_limit_bytes=12 * 2**20 + 24 * images * depth
        ),
        cost_estimate=pl.CostEstimate(
            flops=4 * images * depth * caps,
            bytes_accessed=2 * depth * (caps + 6 * images),
            transcendentals=images * caps,
        ),
    )(scale, offset, index, embed, *labels, *captions)


def turn_kernel(plan, *refs):
    ins, outs = refs[: -len(plan)], refs[-len(plan) :]
    for out, pieces in zip(outs, plan):
        col = 0
        for runs in pieces:
            rows = [ins[i][at : at + size, :] for i, at, size in runs]
            rows = jnp.concatenate(rows)
            out[:, col : col + rows.shape[0]] = rows.T
            col += rows.shape[0]


def turned(xs, plan):
    depth = xs[0].shape[1]
    images = [sum(size for runs in pieces for _, _, size in runs) for pieces in plan]
    return pl.pallas_call(
        functools.partial(turn_kernel, plan),
        out_shape=[jax.ShapeDtypeStruct((depth, n), BF16) for n in images],
        in_specs=[pl.BlockSpec(memory_space=pltpu.VMEM)] * len(xs),
        out_specs=[pl.BlockSpec(memory_space=pltpu.VMEM)] * len(plan),
        compiler_params=pltpu.CompilerParams(vmem_limit_bytes=16 * 2**20),
        cost_estimate=pl.CostEstimate(
            flops=0, bytes_accessed=4 * sum(images) * depth, transcendentals=0
        ),
    )(*xs)


def weight_kernel(factor, has_acc, x_t, *refs):
    gs, (out, stacked, tiles, sems) = refs[has_acc:-4], refs[-4:]
    n, rows = tiles.shape[:2]
    here = [slice(i * rows, (i + 1) * rows) for i in range(n)]
    held, copies = [], []
    for i in range(n if has_acc else 0):
        held.append(
            pltpu.make_async_copy(refs[0].at[here[i], :], tiles.at[i], sems.at[n + i])
        )
        held[-1].start()
    at = 0
    for g in gs:
        stacked[at : at + g.shape[0], :] = g[...]
        at += g.shape[0]
    for i in range(n):
        total = dot(x_t[here[i], :], stacked[...])
        if has_acc:
            held[i].wait()
            total = tiles[i] + total
        tiles[i] = total * factor
        copies.append(
            pltpu.make_async_copy(tiles.at[i], out.at[here[i], :], sems.at[i])
        )
        copies[-1].start()
    for copy in copies:
        copy.wait()


def weight_sum(acc, x_t, gs, factor):
    depth, images = x_t.shape
    n = 3
    has_acc = acc is not None
    vmem = pl.BlockSpec(memory_space=pltpu.VMEM)
    anywhere = pl.BlockSpec(memory_space=pl.ANY)
    return pl.pallas_call(
        functools.partial(weight_kernel, factor, int(has_acc)),
        out_shape=jax.ShapeDtypeStruct((depth, depth), F32),
        in_specs=[vmem] + [anywhere] * has_acc + [vmem] * len(gs),
        out_specs=anywhere,
        scratch_shapes=[
            pltpu.VMEM((images, depth), BF16),
            pltpu.VMEM((n, depth // n, depth), F32),
            pltpu.SemaphoreType.DMA((2 * n,)),
        ],
        compiler_params=pltpu.CompilerParams(vmem_limit_bytes=20 * 2**20),
        cost_estimate=pl.CostEstimate(
            flops=2 * images * depth * depth,
            bytes_accessed=4 * images * depth + 4 * depth * depth * (1 + has_acc),
            transcendentals=0,
        ),
    )(x_t, *([acc] if has_acc else []), *gs)


def on_device(x, captions, labels, weight, scale, offset):
    x, captions = x[0], captions[0]
    n_img, depth = x.shape
    n_cap = captions.shape[0]
    nd, nb = lax.axis_size("dp"), lax.axis_size("blk")
    nz = nb // 2
    index = lax.axis_index("blk")
    bits = nd.bit_length() - 1

    def along_z(v, k):
        return lax.ppermute(v, "blk", [(i, i ^ (2 * k)) for i in range(nb)])

    def swap(v):
        return lax.ppermute(v, "blk", [(i, i ^ 1) for i in range(nb)])

    def step_d(v, i):
        perm = []
        for j in range(nd):
            for m in range(nb):
                to = j ^ (1 << ((i + m % 2) % bits))
                perm.append((j * nb + m, to * nb + m))
        return lax.ppermute(v, ("dp", "blk"), perm)

    xs = [x] + [along_z(x, k) for k in range(1, nz)]
    embed = dot(jnp.concatenate(xs), weight)
    own, u, inv_norm, unit, dlogit, *sent = scores(
        nz,
        scale.reshape(1),
        offset.reshape(1),
        index.reshape(1),
        embed,
        [labels, swap(labels)],
        [captions, swap(captions)],
    )
    back = [along_z(v, k + 1) for k, v in enumerate(sent)]

    xs, dlogit = after((xs, dlogit), back[0])
    x_own = jnp.concatenate(xs)
    for i in range(bits):
        x_own = [x_own, step_d(x_own, i)]
        if i < bits - 1:
            x_own = jnp.concatenate(x_own)

    adjoint = scale * dot(dlogit, unit, FIRST)
    adjoint_other = swap(adjoint[n_cap:])
    adjoint = adjoint[:n_cap] + adjoint_other

    back = after(back, x_own[0])
    for v in back:
        own = own + v.astype(F32)
    radial = jnp.sum(u * own, axis=1, keepdims=True)
    ge = ((own - u * radial) * inv_norm).astype(BF16)
    grad_features = dot(ge, weight, LAST)
    ge = after(ge, adjoint_other)

    half = nz // 2
    near = [along_z(ge, k) for k in range(1, half)]
    own_first = step_d(ge, 0)
    far = [along_z(ge, k) for k in range(half, nz)]

    def over_d(v, first, *before):
        v = [v, first]
        for i in range(1, bits):
            v = after(jnp.concatenate(v), before)
            v = [v, step_d(v, i)]
        return v

    g_own = over_d(ge, own_first)
    near = after(jnp.concatenate(near), g_own[0])
    near_first = step_d(near, 0)
    g_near = over_d(near, near_first)
    far = after(jnp.concatenate(far), near)
    small = nd * nb * n_img <= 2048
    before = []
    if small:
        g_own = jnp.concatenate(g_own)
        x_other = [swap(after(v, near)) for v in x_own]
        before = x_other + [swap(g_own)]
    g_far = over_d(far, step_d(far, 0), before)
    sizes = [n_img, n_img * (half - 1), n_img * half]
    firsts = [0, n_img, n_img * half]
    n_own = nz * n_img
    per = nd // 2
    if small:
        plan = [[], []]
        for core in range(2):
            for g in range(3):
                runs = [
                    (2 * core + i // per, (i % per) * n_own + firsts[g], sizes[g])
                    for i in range(nd)
                ]
                if g < 2:
                    plan[0].append(runs)
                else:
                    plan[0].append(runs[:per])
                    plan[1].append(runs[per:])
        early = [g_own, jnp.concatenate(g_near), g_far[0]]
        x_early, x_late = turned(x_own + x_other, plan)
        others = [before[2], swap(early[1]), swap(after(early[2], g_near[1]))]
        acc = weight_sum(None, x_early, early + others, 1.0)
        late = after(g_far[1], acc)
        grad_weight = weight_sum(acc, x_late, [late, swap(late)], 1.0 / nd)
    else:
        grad_weight = 0.0
        for i, x_part in enumerate(x_own):
            for at in range(per):
                g_part = [
                    g[i][at * m : (at + 1) * m]
                    for m, g in zip(sizes, (g_own, g_near, g_far))
                ]
                grad_weight = grad_weight + dot(
                    x_part[at * n_own : (at + 1) * n_own],
                    jnp.concatenate(g_part),
                    FIRST,
                )
        grad_weight = (grad_weight + swap(grad_weight)) / nd
    return (grad_features[None], adjoint[None], grad_weight)


def solution(mesh):
    placed = (P("dp", "blk", None), P("dp", "blk", None), P("dp", "blk"), P(), P(), P())
    return jax.shard_map(
        on_device,
        mesh=mesh,
        in_specs=placed,
        out_specs=(P("dp", "blk", None), P("dp", "blk", None), P()),
        check_vma=False,
    )
```

```python
import functools

import jax
import jax.numpy as jnp
from jax import lax
from jax.experimental import pallas as pl
from jax.experimental.pallas import tpu as pltpu
from jax.sharding import PartitionSpec as P

FIRST = (((0,), (0,)), ((), ()))
LAST = (((1,), (1,)), ((), ()))
F32 = jnp.float32
BF16 = jnp.bfloat16


def dot(a, b, dims=(((1,), (0,)), ((), ()))):
    return lax.dot_general(a, b, dims, preferred_element_type=F32)


def after(v, *others):
    return lax.optimization_barrier((v, others))[0]


def score_kernel(nz, both, embed, *refs):
    scale, offset = both[0:1, 0:1], both[8:9, 0:1]
    labels, captions, refs = refs[:2], refs[2:4], refs[4:]
    own, unit_own, inv_own, unit, dlogit = refs[:5]
    sent, (caps, sems) = refs[5:-2], refs[-2:]
    n_img, n_cap = embed.shape[0] // nz, captions[0].shape[0]
    copies = []
    for i in range(2):
        here = caps.at[i * n_cap : (i + 1) * n_cap, :]
        copies.append(pltpu.make_async_copy(captions[i], here, sems.at[i]))
        copies[-1].start()
    embed = embed[...]
    inv_norm = lax.rsqrt(jnp.sum(embed * embed, axis=1, keepdims=True) + 1e-06)
    unit_f = embed * inv_norm
    unit_own[...] = unit_f[:n_img]
    inv_own[...] = jnp.broadcast_to(inv_norm[:n_img], inv_own.shape)
    u = unit_f.astype(BF16)
    unit[...] = u
    index = lax.axis_index("blk")
    ids = []
    for k in range(nz):
        first = (index ^ (2 * k)) * n_img
        ids.append(first + lax.broadcasted_iota(jnp.int32, (n_img, 1), 0))
    ids = jnp.concatenate(ids)
    labs = jnp.concatenate([v[...] for v in labels], axis=1)
    sign = jnp.where(labs == ids, 1.0, -1.0).astype(F32)
    for copy in copies:
        copy.wait()
    logits = scale * dot(u, caps[...], LAST) + offset
    d = (-sign * jax.nn.sigmoid(-sign * logits)).astype(BF16)
    dlogit[...] = d
    part = scale * dot(d, caps[...])
    own[...] = part[:n_img]
    for k in range(1, nz):
        sent[k - 1][...] = part[k * n_img : (k + 1) * n_img].astype(BF16)


def scores(nz, both, embed, labels, captions):
    images, depth = embed.shape
    n_img, n_cap = images // nz, captions[0].shape[0]
    caps = 2 * n_cap
    vmem = pl.BlockSpec(memory_space=pltpu.VMEM)
    block = jax.ShapeDtypeStruct((n_img, depth), F32)
    outs = [
        block,
        block,
        jax.ShapeDtypeStruct((n_img, 128), F32),
        jax.ShapeDtypeStruct((images, depth), BF16),
        jax.ShapeDtypeStruct((images, caps), BF16),
    ] + [jax.ShapeDtypeStruct((n_img, depth), BF16)] * (nz - 1)
    return pl.pallas_call(
        functools.partial(score_kernel, nz),
        out_shape=outs,
        in_specs=[vmem] * 4
        + [pl.BlockSpec(memory_space=pl.ANY)] * 2,
        out_specs=[vmem] * len(outs),
        scratch_shapes=[pltpu.VMEM((caps, depth), BF16), pltpu.SemaphoreType.DMA((2,))],
        compiler_params=pltpu.CompilerParams(
            vmem_limit_bytes=12 * 2**20 + 24 * images * depth
        ),
        cost_estimate=pl.CostEstimate(
            flops=4 * images * depth * caps,
            bytes_accessed=2 * depth * (caps + 6 * images),
            transcendentals=images * caps,
        ),
    )(both, embed, *labels, *captions)


def caption_kernel(both, dlogit, unit, own, other):
    scale = both[0:1, 0:1]
    n_cap = own.shape[0]
    own[...] = scale * dot(dlogit[:, :n_cap], unit[...], FIRST)
    other[...] = scale * dot(dlogit[:, n_cap:], unit[...], FIRST)


def caption_sums(both, dlogit, unit):
    images, caps = dlogit.shape
    depth = unit.shape[1]
    vmem = pl.BlockSpec(memory_space=pltpu.VMEM)
    return pl.pallas_call(
        caption_kernel,
        out_shape=[jax.ShapeDtypeStruct((caps // 2, depth), F32)] * 2,
        in_specs=[vmem] * 3,
        out_specs=[vmem] * 2,
        compiler_params=pltpu.CompilerParams(
            vmem_limit_bytes=10 * 2**20 + 8 * images * depth
        ),
        cost_estimate=pl.CostEstimate(
            flops=2 * images * caps * depth,
            bytes_accessed=4 * caps * depth + 2 * images * (depth + caps),
            transcendentals=0,
        ),
    )(both, dlogit, unit)


def embed_grad_kernel(own, unit, inv_norm, *refs):
    back, out = refs[:-1], refs[-1]
    total = own[...]
    for v in back:
        total = total + v[...].astype(F32)
    u = unit[...]
    radial = jnp.sum(u * total, axis=1, keepdims=True)
    out[...] = ((total - u * radial) * inv_norm[:, :1]).astype(BF16)


def embed_grad(own, unit, inv_norm, back):
    vmem = pl.BlockSpec(memory_space=pltpu.VMEM)
    return pl.pallas_call(
        embed_grad_kernel,
        out_shape=jax.ShapeDtypeStruct(own.shape, BF16),
        in_specs=[vmem] * (3 + len(back)),
        out_specs=vmem,
        compiler_params=pltpu.CompilerParams(vmem_limit_bytes=8 * 2**20),
        cost_estimate=pl.CostEstimate(
            flops=8 * own.size, bytes_accessed=12 * own.size, transcendentals=0
        ),
    )(own, unit, inv_norm, *back)


def turn_kernel(plan, *refs):
    ins, outs = refs[: -len(plan)], refs[-len(plan) :]
    for out, pieces in zip(outs, plan):
        col = 0
        for runs in pieces:
            rows = [ins[i][at : at + size, :] for i, at, size in runs]
            rows = jnp.concatenate(rows)
            out[:, col : col + rows.shape[0]] = rows.T
            col += rows.shape[0]


def turned(xs, plan):
    depth = xs[0].shape[1]
    images = [sum(size for runs in pieces for _, _, size in runs) for pieces in plan]
    return pl.pallas_call(
        functools.partial(turn_kernel, plan),
        out_shape=[jax.ShapeDtypeStruct((depth, n), BF16) for n in images],
        in_specs=[pl.BlockSpec(memory_space=pltpu.VMEM)] * len(xs),
        out_specs=[pl.BlockSpec(memory_space=pltpu.VMEM)] * len(plan),
        compiler_params=pltpu.CompilerParams(vmem_limit_bytes=16 * 2**20),
        cost_estimate=pl.CostEstimate(
            flops=0, bytes_accessed=4 * sum(images) * depth, transcendentals=0
        ),
    )(*xs)


def stack(stacked, gs):
    at = 0
    for g in gs:
        stacked[at : at + g.shape[0], :] = g[...]
        at += g.shape[0]


def early_kernel(n, x_t, *refs):
    gs, (out, stacked) = refs[:-2], refs[-2:]
    stack(stacked, gs)
    rows = out.shape[0] // n
    for i in range(n):
        here = slice(i * rows, (i + 1) * rows)
        out[here, :] = dot(x_t[here, :], stacked[...])


def late_kernel(factor, x_t, acc, *refs):
    gs, (out, stacked, tiles, sems) = refs[:-4], refs[-4:]
    stack(stacked, gs)
    n, rows = tiles.shape[:2]
    copies = []
    for i in range(n):
        here = slice(i * rows, (i + 1) * rows)
        tiles[i] = (acc[here, :] + dot(x_t[here, :], stacked[...])) * factor
        copies.append(pltpu.make_async_copy(tiles.at[i], out.at[here, :], sems.at[i]))
        copies[-1].start()
    for copy in copies:
        copy.wait()


def weight_sum(acc, x_t, gs, factor):
    depth, images = x_t.shape
    n = 3
    early = acc is None
    vmem = pl.BlockSpec(memory_space=pltpu.VMEM)
    scratch = [pltpu.VMEM((images, depth), BF16)]
    if early:
        kernel = functools.partial(early_kernel, n)
    else:
        kernel = functools.partial(late_kernel, factor)
        scratch.append(pltpu.VMEM((n, depth // n, depth), F32))
        scratch.append(pltpu.SemaphoreType.DMA((n,)))
    operands = [x_t] + ([] if early else [acc]) + gs
    return pl.pallas_call(
        kernel,
        out_shape=jax.ShapeDtypeStruct((depth, depth), F32),
        in_specs=[vmem] * len(operands),
        out_specs=vmem if early else pl.BlockSpec(memory_space=pl.ANY),
        scratch_shapes=scratch,
        compiler_params=pltpu.CompilerParams(vmem_limit_bytes=24 * 2**20),
        cost_estimate=pl.CostEstimate(
            flops=2 * images * depth * depth,
            bytes_accessed=4 * images * depth + 4 * depth * depth * (2 - early),
            transcendentals=0,
        ),
    )(*operands)


def on_device(x, captions, labels, weight, scale, offset):
    x, captions = x[0], captions[0]
    n_img, depth = x.shape
    n_cap = captions.shape[0]
    nd, nb = lax.axis_size("dp"), lax.axis_size("blk")
    nz = nb // 2
    bits = nd.bit_length() - 1

    def along_z(v, k):
        return lax.ppermute(v, "blk", [(i, i ^ (2 * k)) for i in range(nb)])

    def swap(v):
        return lax.ppermute(v, "blk", [(i, i ^ 1) for i in range(nb)])

    def step_d(v, i):
        perm = []
        for j in range(nd):
            for m in range(nb):
                to = j ^ (1 << ((i + m % 2) % bits))
                perm.append((j * nb + m, to * nb + m))
        return lax.ppermute(v, ("dp", "blk"), perm)

    xs = [x] + [along_z(x, k) for k in range(1, nz)]
    x_own = jnp.concatenate(xs)
    x_first = step_d(x_own, 0)
    embed = dot(jnp.concatenate(xs), weight)
    row = lax.broadcasted_iota(jnp.int32, (16, 128), 0)
    both = jnp.where(row < 8, scale, offset)
    own, u, inv_norm, unit, dlogit, *sent = scores(
        nz,
        both,
        embed,
        [labels, swap(labels)],
        [captions, swap(captions)],
    )
    back = [along_z(v, k + 1) for k, v in enumerate(sent)]

    x_first = after(x_first, back)
    x_own = [x_own, x_first]
    for i in range(1, bits):
        x_own = jnp.concatenate(x_own)
        x_own = [x_own, step_d(x_own, i)]
    small = nd * nb * n_img <= 2048

    adjoint, adjoint_other = caption_sums(both, after(dlogit, x_first), unit)

    ge = embed_grad(own, u, inv_norm, back)
    grad_features = dot(ge, weight, LAST)

    half = nz // 2
    near = [along_z(ge, k) for k in range(1, half)]
    own_first = step_d(ge, 0)
    far = [along_z(ge, k) for k in range(half, nz)]

    def over_d(v, first, *before):
        v = [v, first]
        for i in range(1, bits):
            v = after(jnp.concatenate(v), before)
            v = [v, step_d(v, i)]
        return v

    g_own = over_d(ge, own_first)
    near = after(jnp.concatenate(near), g_own[0])
    near_first = step_d(near, 0)
    g_near = over_d(near, near_first)
    far = after(jnp.concatenate(far), near_first, g_own[1])
    far_first = step_d(far, 0)
    adjoint = adjoint + swap(after(adjoint_other, far_first))
    sizes = [n_img, n_img * (half - 1), n_img * half]
    firsts = [0, n_img, n_img * half]
    n_own = nz * n_img
    per = nd // 2
    if small:
        plan = [[], []]
        for core in range(2):
            for g in range(3):
                runs = [(core, i * n_own + firsts[g], sizes[g]) for i in range(nd)]
                if g < 2:
                    plan[0].append(runs)
                else:
                    plan[0].append(runs[:per])
                    plan[1].append(runs[per:])
        x_own = jnp.concatenate(x_own)
        x_early, x_late = turned([x_own, swap(after(x_own, far))], plan)
        g_own = jnp.concatenate(g_own)
        own_swapped = swap(g_own)
        g_far = over_d(far, far_first, own_swapped, g_near[1])
        early = [g_own, jnp.concatenate(g_near), g_far[0]]
        others = [own_swapped, swap(early[1]), swap(after(early[2], g_near[1]))]
        acc = weight_sum(None, x_early, early + others, 1.0)
        late = after(g_far[1], acc)
        grad_weight = weight_sum(acc, x_late, [late, swap(late)], 1.0 / nd)
    else:
        g_far = over_d(far, far_first)
        grad_weight = 0.0
        for i, x_part in enumerate(x_own):
            for at in range(per):
                g_part = [
                    g[i][at * m : (at + 1) * m]
                    for m, g in zip(sizes, (g_own, g_near, g_far))
                ]
                grad_weight = grad_weight + dot(
                    x_part[at * n_own : (at + 1) * n_own],
                    jnp.concatenate(g_part),
                    FIRST,
                )
        grad_weight = (grad_weight + swap(grad_weight)) / nd
    return (grad_features[None], adjoint[None], grad_weight)


def solution(mesh):
    placed = (P("dp", "blk", None), P("dp", "blk", None), P("dp", "blk"), P(), P(), P())
    return jax.shard_map(
        on_device,
        mesh=mesh,
        in_specs=placed,
        out_specs=(P("dp", "blk", None), P("dp", "blk", None), P()),
        check_vma=False,
    )
```

```python
import functools

import jax
import jax.numpy as jnp
from jax import lax
from jax.experimental import pallas as pl
from jax.experimental.pallas import tpu as pltpu
from jax.sharding import PartitionSpec as P

FIRST = (((0,), (0,)), ((), ()))
LAST = (((1,), (1,)), ((), ()))
F32 = jnp.float32
BF16 = jnp.bfloat16


def dot(a, b, dims=(((1,), (0,)), ((), ()))):
    return lax.dot_general(a, b, dims, preferred_element_type=F32)


def after(v, *others):
    return lax.optimization_barrier((v, others))[0]


def score_kernel(nz, both, embed, *refs):
    scale, offset = both[0:1, 0:1], both[8:9, 0:1]
    labels, captions, refs = refs[:2], refs[2:4], refs[4:]
    own, unit_own, inv_own, unit, dlogit = refs[:5]
    sent, (caps, sems) = refs[5:-2], refs[-2:]
    n_img, n_cap = embed.shape[0] // nz, captions[0].shape[0]
    copies = []
    for i in range(2):
        here = caps.at[i * n_cap : (i + 1) * n_cap, :]
        copies.append(pltpu.make_async_copy(captions[i], here, sems.at[i]))
        copies[-1].start()
    embed = embed[...]
    inv_norm = lax.rsqrt(jnp.sum(embed * embed, axis=1, keepdims=True) + 1e-06)
    unit_f = embed * inv_norm
    unit_own[...] = unit_f[:n_img]
    inv_own[...] = jnp.broadcast_to(inv_norm[:n_img], inv_own.shape)
    u = unit_f.astype(BF16)
    unit[...] = u
    index = lax.axis_index("blk")
    ids = []
    for k in range(nz):
        first = (index ^ (2 * k)) * n_img
        ids.append(first + lax.broadcasted_iota(jnp.int32, (n_img, 1), 0))
    ids = jnp.concatenate(ids)
    labs = jnp.concatenate([v[...] for v in labels], axis=1)
    sign = jnp.where(labs == ids, 1.0, -1.0).astype(F32)
    for copy in copies:
        copy.wait()
    logits = scale * dot(u, caps[...], LAST) + offset
    d = (-sign * jax.nn.sigmoid(-sign * logits)).astype(BF16)
    dlogit[...] = d
    part = scale * dot(d, caps[...])
    own[...] = part[:n_img]
    for k in range(1, nz):
        sent[k - 1][...] = part[k * n_img : (k + 1) * n_img].astype(BF16)


def scores(nz, both, embed, labels, captions):
    images, depth = embed.shape
    n_img, n_cap = images // nz, captions[0].shape[0]
    caps = 2 * n_cap
    vmem = pl.BlockSpec(memory_space=pltpu.VMEM)
    block = jax.ShapeDtypeStruct((n_img, depth), F32)
    outs = [
        block,
        block,
        jax.ShapeDtypeStruct((n_img, 128), F32),
        jax.ShapeDtypeStruct((images, depth), BF16),
        jax.ShapeDtypeStruct((images, caps), BF16),
    ] + [jax.ShapeDtypeStruct((n_img, depth), BF16)] * (nz - 1)
    return pl.pallas_call(
        functools.partial(score_kernel, nz),
        out_shape=outs,
        in_specs=[vmem] * 4
        + [pl.BlockSpec(memory_space=pl.ANY)] * 2,
        out_specs=[vmem] * len(outs),
        scratch_shapes=[pltpu.VMEM((caps, depth), BF16), pltpu.SemaphoreType.DMA((2,))],
        compiler_params=pltpu.CompilerParams(
            vmem_limit_bytes=12 * 2**20 + 24 * images * depth
        ),
        cost_estimate=pl.CostEstimate(
            flops=4 * images * depth * caps,
            bytes_accessed=2 * depth * (caps + 6 * images),
            transcendentals=images * caps,
        ),
    )(both, embed, *labels, *captions)


def join_kernel(*refs):
    at = 0
    for v in refs[:-1]:
        refs[-1][at : at + v.shape[0], :] = v[...]
        at += v.shape[0]


def joined(vs):
    rows = sum(v.shape[0] for v in vs)
    depth = vs[0].shape[1]
    vmem = pl.BlockSpec(memory_space=pltpu.VMEM)
    return pl.pallas_call(
        join_kernel,
        out_shape=jax.ShapeDtypeStruct((rows, depth), vs[0].dtype),
        in_specs=[vmem] * len(vs),
        out_specs=vmem,
        compiler_params=pltpu.CompilerParams(vmem_limit_bytes=12 * 2**20),
        cost_estimate=pl.CostEstimate(
            flops=0, bytes_accessed=4 * rows * depth, transcendentals=0
        ),
    )(*vs)


def caption_kernel(both, dlogit, unit, own, other):
    scale = both[0:1, 0:1]
    n_cap = own.shape[0]
    own[...] = scale * dot(dlogit[:, :n_cap], unit[...], FIRST)
    other[...] = scale * dot(dlogit[:, n_cap:], unit[...], FIRST)


def caption_sums(both, dlogit, unit):
    images, caps = dlogit.shape
    depth = unit.shape[1]
    vmem = pl.BlockSpec(memory_space=pltpu.VMEM)
    return pl.pallas_call(
        caption_kernel,
        out_shape=[jax.ShapeDtypeStruct((caps // 2, depth), F32)] * 2,
        in_specs=[vmem] * 3,
        out_specs=[vmem] * 2,
        compiler_params=pltpu.CompilerParams(
            vmem_limit_bytes=10 * 2**20 + 8 * images * depth
        ),
        cost_estimate=pl.CostEstimate(
            flops=2 * images * caps * depth,
            bytes_accessed=4 * caps * depth + 2 * images * (depth + caps),
            transcendentals=0,
        ),
    )(both, dlogit, unit)


def embed_grad_kernel(own, unit, inv_norm, *refs):
    back, out = refs[:-1], refs[-1]
    total = own[...]
    for v in back:
        total = total + v[...].astype(F32)
    u = unit[...]
    radial = jnp.sum(u * total, axis=1, keepdims=True)
    out[...] = ((total - u * radial) * inv_norm[:, :1]).astype(BF16)


def embed_grad(own, unit, inv_norm, back):
    vmem = pl.BlockSpec(memory_space=pltpu.VMEM)
    return pl.pallas_call(
        embed_grad_kernel,
        out_shape=jax.ShapeDtypeStruct(own.shape, BF16),
        in_specs=[vmem] * (3 + len(back)),
        out_specs=vmem,
        compiler_params=pltpu.CompilerParams(vmem_limit_bytes=8 * 2**20),
        cost_estimate=pl.CostEstimate(
            flops=8 * own.size, bytes_accessed=12 * own.size, transcendentals=0
        ),
    )(own, unit, inv_norm, *back)


def turn_kernel(plan, *refs):
    ins, outs = refs[: -len(plan)], refs[-len(plan) :]
    for out, runs in zip(outs, plan):
        col = 0
        for i, at, size in runs:
            out[:, col : col + size] = ins[i][at : at + size, :].T
            col += size


def turned(xs, plan):
    depth = xs[0].shape[1]
    images = [sum(size for _, _, size in runs) for runs in plan]
    return pl.pallas_call(
        functools.partial(turn_kernel, plan),
        out_shape=[jax.ShapeDtypeStruct((depth, n), BF16) for n in images],
        in_specs=[pl.BlockSpec(memory_space=pltpu.VMEM)] * len(xs),
        out_specs=[pl.BlockSpec(memory_space=pltpu.VMEM)] * len(plan),
        compiler_params=pltpu.CompilerParams(vmem_limit_bytes=16 * 2**20),
        cost_estimate=pl.CostEstimate(
            flops=0, bytes_accessed=4 * sum(images) * depth, transcendentals=0
        ),
    )(*xs)


def stack(stacked, gs):
    at = 0
    for g in gs:
        stacked[at : at + g.shape[0], :] = g[...]
        at += g.shape[0]


def early_kernel(n, x_t, *refs):
    gs, (out, stacked) = refs[:-2], refs[-2:]
    stack(stacked, gs)
    rows = out.shape[0] // n
    for i in range(n):
        here = slice(i * rows, (i + 1) * rows)
        out[here, :] = dot(x_t[here, :], stacked[...])


def late_kernel(factor, x_t, acc, *refs):
    gs, (out, stacked, tiles, sems) = refs[:-4], refs[-4:]
    stack(stacked, gs)
    n, rows = tiles.shape[:2]
    copies = []
    for i in range(n):
        here = slice(i * rows, (i + 1) * rows)
        tiles[i] = (acc[here, :] + dot(x_t[here, :], stacked[...])) * factor
        copies.append(pltpu.make_async_copy(tiles.at[i], out.at[here, :], sems.at[i]))
        copies[-1].start()
    for copy in copies:
        copy.wait()


def weight_sum(acc, x_t, gs, factor):
    depth, images = x_t.shape
    n = 3
    early = acc is None
    vmem = pl.BlockSpec(memory_space=pltpu.VMEM)
    scratch = [pltpu.VMEM((images, depth), BF16)]
    if early:
        kernel = functools.partial(early_kernel, n)
    else:
        kernel = functools.partial(late_kernel, factor)
        scratch.append(pltpu.VMEM((n, depth // n, depth), F32))
        scratch.append(pltpu.SemaphoreType.DMA((n,)))
    operands = [x_t] + ([] if early else [acc]) + gs
    return pl.pallas_call(
        kernel,
        out_shape=jax.ShapeDtypeStruct((depth, depth), F32),
        in_specs=[vmem] * len(operands),
        out_specs=vmem if early else pl.BlockSpec(memory_space=pl.ANY),
        scratch_shapes=scratch,
        compiler_params=pltpu.CompilerParams(vmem_limit_bytes=24 * 2**20),
        cost_estimate=pl.CostEstimate(
            flops=2 * images * depth * depth,
            bytes_accessed=4 * images * depth + 4 * depth * depth * (2 - early),
            transcendentals=0,
        ),
    )(*operands)


def on_device(x, captions, labels, weight, scale, offset):
    x, captions = x[0], captions[0]
    n_img, depth = x.shape
    n_cap = captions.shape[0]
    nd, nb = lax.axis_size("dp"), lax.axis_size("blk")
    nz = nb // 2
    bits = nd.bit_length() - 1

    def along_z(v, k):
        return lax.ppermute(v, "blk", [(i, i ^ (2 * k)) for i in range(nb)])

    def swap(v):
        return lax.ppermute(v, "blk", [(i, i ^ 1) for i in range(nb)])

    def step_d(v, i):
        perm = []
        for j in range(nd):
            for m in range(nb):
                to = j ^ (1 << ((i + m % 2) % bits))
                perm.append((j * nb + m, to * nb + m))
        return lax.ppermute(v, ("dp", "blk"), perm)

    def over_d(v, first, *before):
        v = [v, first]
        for i in range(1, bits):
            v = after(jnp.concatenate(v), before)
            v = [v, step_d(v, i)]
        return v

    half = nz // 2
    xs = [x] + [along_z(x, k) for k in range(1, nz)]
    x_near, x_far = jnp.concatenate(xs[1:half]), jnp.concatenate(xs[half:])
    x_own = over_d(x, step_d(x, 0))
    x_near_first = step_d(x_near, 0)
    x_far_first = step_d(x_far, 0)
    embed = dot(jnp.concatenate(xs), weight)
    row = lax.broadcasted_iota(jnp.int32, (16, 128), 0)
    both = jnp.where(row < 8, scale, offset)
    own, u, inv_norm, unit, dlogit, *sent = scores(
        nz,
        both,
        embed,
        [labels, swap(labels)],
        [captions, swap(captions)],
    )
    sent = after(sent, x_own)
    back = [along_z(v, k + 1) for k, v in enumerate(sent)]

    x_near = over_d(x_near, after(x_near_first, sent))
    x_far = over_d(x_far, after(x_far_first, sent))
    back = after(back, x_far, x_near)
    ge = embed_grad(own, u, inv_norm, back)
    grad_features = dot(ge, weight, LAST)

    near = [along_z(ge, k) for k in range(1, half)]
    own_first = step_d(ge, 0)
    far = [along_z(ge, k) for k in range(half, nz)]

    g_own = over_d(ge, own_first)
    near = after(jnp.concatenate(near), g_own[0])
    near_first = step_d(near, 0)
    g_near = over_d(near, near_first)
    far = after(jnp.concatenate(far), near)
    far_first = step_d(far, 0)
    dlogit = after(dlogit, far_first)
    adjoint, adjoint_other = caption_sums(both, dlogit, unit)
    adjoint = adjoint + swap(adjoint_other)
    if nd * nb * n_img <= 2048:
        x_all = [joined(x_own + x_near), joined(x_far)]
        x_all += [swap(after(v, near)) for v in x_all]
        n = n_img * nd
        plan = [[], []]
        for core in (0, 2):
            plan[0] += [(core, 0, n), (core, n, n), (core + 1, 0, n)]
            plan[1] += [(core + 1, n, n)]
        x_early, x_late = turned(x_all, plan)
        g_own = jnp.concatenate(g_own)
        own_swapped = swap(g_own)
        g_far = over_d(far, far_first, own_swapped)
        early = [g_own, jnp.concatenate(g_near), g_far[0]]
        others = [own_swapped, swap(early[1]), swap(after(early[2], g_near[1]))]
        acc = weight_sum(None, x_early, early + others, 1.0)
        late = after(g_far[1], acc)
        grad_weight = weight_sum(acc, x_late, [late, swap(late)], 1.0 / nd)
    else:
        g_far = over_d(far, far_first)
        grad_weight = 0.0
        for v, g in zip(x_own + x_near + x_far, g_own + g_near + g_far):
            grad_weight = grad_weight + dot(v, g, FIRST)
        grad_weight = (grad_weight + swap(grad_weight)) / nd
    return (grad_features[None], adjoint[None], grad_weight)


def solution(mesh):
    placed = (P("dp", "blk", None), P("dp", "blk", None), P("dp", "blk"), P(), P(), P())
    return jax.shard_map(
        on_device,
        mesh=mesh,
        in_specs=placed,
        out_specs=(P("dp", "blk", None), P("dp", "blk", None), P()),
        check_vma=False,
    )
```

```python
import functools

import jax
import jax.numpy as jnp
from jax import lax
from jax.experimental import pallas as pl
from jax.experimental.pallas import tpu as pltpu
from jax.sharding import PartitionSpec as P

FIRST = (((0,), (0,)), ((), ()))
LAST = (((1,), (1,)), ((), ()))
F32 = jnp.float32
BF16 = jnp.bfloat16


def dot(a, b, dims=(((1,), (0,)), ((), ()))):
    return lax.dot_general(a, b, dims, preferred_element_type=F32)


def after(v, *others):
    return lax.optimization_barrier((v, others))[0]


def score_kernel(nz, both, embed, *refs):
    scale, offset = both[0:1, 0:1], both[8:9, 0:1]
    labels, captions, refs = refs[:2], refs[2:4], refs[4:]
    own, unit_own, inv_own, unit, dlogit = refs[:5]
    sent, caps, sems = refs[5:]
    n_img, n_cap = embed.shape[0] // nz, captions[0].shape[0]
    copies = []
    for i in range(2):
        here = caps.at[i * n_cap : (i + 1) * n_cap, :]
        copies.append(pltpu.make_async_copy(captions[i], here, sems.at[i]))
        copies[-1].start()
    embed = embed[...]
    inv_norm = lax.rsqrt(jnp.sum(embed * embed, axis=1, keepdims=True) + 1e-06)
    unit_f = embed * inv_norm
    unit_own[...] = unit_f[:n_img]
    inv_own[...] = jnp.broadcast_to(inv_norm[:n_img], inv_own.shape)
    u = unit_f.astype(BF16)
    unit[...] = u
    index = lax.axis_index("blk")
    ids = []
    for k in range(nz):
        first = (index ^ (2 * k)) * n_img
        ids.append(first + lax.broadcasted_iota(jnp.int32, (n_img, 1), 0))
    ids = jnp.concatenate(ids)
    labs = jnp.concatenate([v[...] for v in labels], axis=1)
    sign = jnp.where(labs == ids, 1.0, -1.0).astype(F32)
    for copy in copies:
        copy.wait()
    logits = scale * dot(u, caps[...], LAST) + offset
    d = (-sign * jax.nn.sigmoid(-sign * logits)).astype(BF16)
    dlogit[...] = d
    part = scale * dot(d, caps[...])
    own[...] = part[:n_img]
    for k in range(nz):
        row = pl.multiple_of(((index // 2) ^ k) * n_img, n_img)
        block = part[k * n_img : (k + 1) * n_img]
        sent[pl.ds(row, n_img), :] = block.astype(BF16)


def scores(nz, both, embed, labels, captions):
    images, depth = embed.shape
    n_img, n_cap = images // nz, captions[0].shape[0]
    caps = 2 * n_cap
    vmem = pl.BlockSpec(memory_space=pltpu.VMEM)
    block = jax.ShapeDtypeStruct((n_img, depth), F32)
    outs = [
        block,
        block,
        jax.ShapeDtypeStruct((n_img, 128), F32),
        jax.ShapeDtypeStruct((images, depth), BF16),
        jax.ShapeDtypeStruct((images, caps), BF16),
        jax.ShapeDtypeStruct((images, depth), BF16),
    ]
    return pl.pallas_call(
        functools.partial(score_kernel, nz),
        out_shape=outs,
        in_specs=[vmem] * 4
        + [pl.BlockSpec(memory_space=pl.ANY)] * 2,
        out_specs=[vmem] * len(outs),
        scratch_shapes=[pltpu.VMEM((caps, depth), BF16), pltpu.SemaphoreType.DMA((2,))],
        compiler_params=pltpu.CompilerParams(
            vmem_limit_bytes=12 * 2**20 + 24 * images * depth
        ),
        cost_estimate=pl.CostEstimate(
            flops=4 * images * depth * caps,
            bytes_accessed=2 * depth * (caps + 6 * images),
            transcendentals=images * caps,
        ),
    )(both, embed, *labels, *captions)


def join_kernel(*refs):
    at = 0
    for v in refs[:-1]:
        refs[-1][at : at + v.shape[0], :] = v[...]
        at += v.shape[0]


def joined(vs):
    rows = sum(v.shape[0] for v in vs)
    depth = vs[0].shape[1]
    vmem = pl.BlockSpec(memory_space=pltpu.VMEM)
    return pl.pallas_call(
        join_kernel,
        out_shape=jax.ShapeDtypeStruct((rows, depth), vs[0].dtype),
        in_specs=[vmem] * len(vs),
        out_specs=vmem,
        compiler_params=pltpu.CompilerParams(vmem_limit_bytes=12 * 2**20),
        cost_estimate=pl.CostEstimate(
            flops=0, bytes_accessed=4 * rows * depth, transcendentals=0
        ),
    )(*vs)


def caption_kernel(both, dlogit, unit, own, other):
    scale = both[0:1, 0:1]
    n_cap = own.shape[0]
    own[...] = scale * dot(dlogit[:, :n_cap], unit[...], FIRST)
    other[...] = scale * dot(dlogit[:, n_cap:], unit[...], FIRST)


def caption_sums(both, dlogit, unit):
    images, caps = dlogit.shape
    depth = unit.shape[1]
    vmem = pl.BlockSpec(memory_space=pltpu.VMEM)
    return pl.pallas_call(
        caption_kernel,
        out_shape=[jax.ShapeDtypeStruct((caps // 2, depth), F32)] * 2,
        in_specs=[vmem] * 3,
        out_specs=[vmem] * 2,
        compiler_params=pltpu.CompilerParams(
            vmem_limit_bytes=10 * 2**20 + 8 * images * depth
        ),
        cost_estimate=pl.CostEstimate(
            flops=2 * images * caps * depth,
            bytes_accessed=4 * caps * depth + 2 * images * (depth + caps),
            transcendentals=0,
        ),
    )(both, dlogit, unit)


def embed_grad_kernel(own, unit, inv_norm, back, out):
    n_img = own.shape[0]
    nz = back.shape[0] // n_img
    z = lax.axis_index("blk") // 2
    total = own[...]
    for k in range(1, nz):
        row = pl.multiple_of((z ^ k) * n_img, n_img)
        total = total + back[pl.ds(row, n_img), :].astype(F32)
    u = unit[...]
    radial = jnp.sum(u * total, axis=1, keepdims=True)
    out[...] = ((total - u * radial) * inv_norm[:, :1]).astype(BF16)


def embed_grad(own, unit, inv_norm, back):
    vmem = pl.BlockSpec(memory_space=pltpu.VMEM)
    return pl.pallas_call(
        embed_grad_kernel,
        out_shape=jax.ShapeDtypeStruct(own.shape, BF16),
        in_specs=[vmem] * 4,
        out_specs=vmem,
        compiler_params=pltpu.CompilerParams(vmem_limit_bytes=12 * 2**20),
        cost_estimate=pl.CostEstimate(
            flops=8 * own.size, bytes_accessed=12 * own.size, transcendentals=0
        ),
    )(own, unit, inv_norm, back)


def turn_kernel(plan, *refs):
    ins, outs = refs[: -len(plan)], refs[-len(plan) :]
    for out, pieces in zip(outs, plan):
        col = 0
        for runs in pieces:
            rows = [ins[i][at : at + size, :] for i, at, size in runs]
            rows = jnp.concatenate(rows)
            out[:, col : col + rows.shape[0]] = rows.T
            col += rows.shape[0]


def turned(xs, plan):
    depth = xs[0].shape[1]
    images = [sum(size for runs in pieces for _, _, size in runs) for pieces in plan]
    return pl.pallas_call(
        functools.partial(turn_kernel, plan),
        out_shape=[jax.ShapeDtypeStruct((depth, n), BF16) for n in images],
        in_specs=[pl.BlockSpec(memory_space=pltpu.VMEM)] * len(xs),
        out_specs=[pl.BlockSpec(memory_space=pltpu.VMEM)] * len(plan),
        compiler_params=pltpu.CompilerParams(vmem_limit_bytes=16 * 2**20),
        cost_estimate=pl.CostEstimate(
            flops=0, bytes_accessed=4 * sum(images) * depth, transcendentals=0
        ),
    )(*xs)


def stack(stacked, gs):
    at = 0
    for g in gs:
        stacked[at : at + g.shape[0], :] = g[...]
        at += g.shape[0]


def early_kernel(n, has_acc, x_t, *refs):
    gs, (out, stacked) = refs[has_acc:-2], refs[-2:]
    stack(stacked, gs)
    rows = out.shape[0] // n
    for i in range(n):
        here = slice(i * rows, (i + 1) * rows)
        total = dot(x_t[here, :], stacked[...])
        out[here, :] = refs[0][here, :] + total if has_acc else total


def late_kernel(factor, x_t, acc, *refs):
    gs, (out, stacked, tiles, sems) = refs[:-4], refs[-4:]
    stack(stacked, gs)
    n, rows = tiles.shape[:2]
    copies = []
    for i in range(n):
        here = slice(i * rows, (i + 1) * rows)
        tiles[i] = (acc[here, :] + dot(x_t[here, :], stacked[...])) * factor
        copies.append(pltpu.make_async_copy(tiles.at[i], out.at[here, :], sems.at[i]))
        copies[-1].start()
    for copy in copies:
        copy.wait()


def weight_sum(acc, x_t, gs, factor=None):
    depth, images = x_t.shape
    n = 3
    early, has_acc = factor is None, int(acc is not None)
    vmem = pl.BlockSpec(memory_space=pltpu.VMEM)
    scratch = [pltpu.VMEM((images, depth), BF16)]
    if early:
        kernel = functools.partial(early_kernel, n, has_acc)
    else:
        kernel = functools.partial(late_kernel, factor)
        scratch.append(pltpu.VMEM((n, depth // n, depth), F32))
        scratch.append(pltpu.SemaphoreType.DMA((n,)))
    operands = [x_t] + [acc] * has_acc + gs
    return pl.pallas_call(
        kernel,
        out_shape=jax.ShapeDtypeStruct((depth, depth), F32),
        in_specs=[vmem] * len(operands),
        out_specs=vmem if early else pl.BlockSpec(memory_space=pl.ANY),
        scratch_shapes=scratch,
        compiler_params=pltpu.CompilerParams(vmem_limit_bytes=24 * 2**20),
        cost_estimate=pl.CostEstimate(
            flops=2 * images * depth * depth,
            bytes_accessed=4 * images * depth + 4 * depth * depth * (1 + has_acc),
            transcendentals=0,
        ),
    )(*operands)


def on_device(x, captions, labels, weight, scale, offset):
    x, captions = x[0], captions[0]
    n_img, depth = x.shape
    n_cap = captions.shape[0]
    nd, nb = lax.axis_size("dp"), lax.axis_size("blk")
    nz = nb // 2
    bits = nd.bit_length() - 1

    def along_z(v, k):
        return lax.ppermute(v, "blk", [(i, i ^ (2 * k)) for i in range(nb)])

    def swap(v):
        return lax.ppermute(v, "blk", [(i, i ^ 1) for i in range(nb)])

    def step_d(v, i):
        perm = []
        for j in range(nd):
            for m in range(nb):
                to = j ^ (1 << ((i + m % 2) % bits))
                perm.append((j * nb + m, to * nb + m))
        return lax.ppermute(v, ("dp", "blk"), perm)

    def over_d(v, first, *before):
        v = [v, first]
        for i in range(1, bits):
            v = after(jnp.concatenate(v), before)
            v = [v, step_d(v, i)]
        return v

    half = nz // 2
    xs = [x] + [along_z(x, k) for k in range(1, nz)]
    x_own = over_d(x, step_d(after(x, xs[1]), 0))
    x_rest = jnp.concatenate(xs[1:])
    x_rest_first = step_d(x_rest, 0)
    embed = dot(joined(xs), weight)
    row = lax.broadcasted_iota(jnp.int32, (16, 128), 0)
    both = jnp.where(row < 8, scale, offset)
    own, u, inv_norm, unit, dlogit, sent = scores(
        nz,
        both,
        embed,
        [labels, swap(labels)],
        [captions, swap(captions)],
    )
    x_rest = over_d(x_rest, after(x_rest_first, sent))
    adjoint, adjoint_other = caption_sums(both, after(dlogit, sent), unit)
    adjoint_other = swap(adjoint_other)
    adjoint = adjoint + adjoint_other
    chips = [list(range(c, nb, 2)) for c in range(2)]
    sent = after(sent, x_own, x_rest[0])
    back = lax.all_to_all(sent, "blk", 0, 0, axis_index_groups=chips, tiled=True)
    back = after(back, x_rest, adjoint_other)
    small = nd * nb * n_img <= 2048
    if small:
        x_all = joined(x_own + x_rest)
        x_other = swap(after(x_all, back))
    ge = embed_grad(own, u, inv_norm, back)
    grad_features = dot(ge, weight, LAST)

    near = [along_z(ge, k) for k in range(1, half)]
    own_first = step_d(ge, 0)
    far = [along_z(ge, k) for k in range(half, nz)]
    g_own = over_d(ge, own_first)
    near = after(jnp.concatenate(near), g_own[0], g_own[0])
    near_first = step_d(near, 0)
    g_near = over_d(near, near_first)
    far = after(jnp.concatenate(far), near_first, g_own[1])
    far_first = step_d(far, 0)
    sizes = [n_img, n_img * (half - 1), n_img * half]
    n_rest = sizes[1] + sizes[2]
    per = nd // 2
    if small:
        plan = [[], [], []]
        for core in range(2):
            rest = [n_img * nd + i * n_rest for i in range(nd)]
            far_runs = [(core, at + sizes[1], sizes[2]) for at in rest]
            plan[0] += [[(core, 0, n_img * nd)]]
            plan[1] += [[(core, at, sizes[1]) for at in rest], far_runs[:per]]
            plan[2] += [far_runs[per:]]
        x_first, x_mid, x_late = turned([x_all, x_other], plan)
        g_own, g_near = jnp.concatenate(g_own), jnp.concatenate(g_near)
        own_swapped = swap(g_own)
        acc = weight_sum(None, x_first, [g_own, own_swapped])
        near_swapped = swap(g_near)
        g_far = over_d(far, far_first, )
        mid = [g_near, g_far[0], near_swapped, swap(g_far[0])]
        before_late = (acc, grad_features)
        acc = weight_sum(acc, x_mid, mid)
        late = after(g_far[1], before_late, adjoint)
        grad_weight = weight_sum(acc, x_late, [late, swap(late)], 1.0 / nd)
    else:
        g_far = over_d(far, far_first)
        grad_weight = 0.0
        for v, g in zip(x_own, g_own):
            grad_weight = grad_weight + dot(v, g, FIRST)
        for v, g, h in zip(x_rest, g_near, g_far):
            for i in range(per):
                g_part = [
                    g[i * sizes[1] : (i + 1) * sizes[1]],
                    h[i * sizes[2] : (i + 1) * sizes[2]],
                ]
                grad_weight = grad_weight + dot(
                    v[i * n_rest : (i + 1) * n_rest], jnp.concatenate(g_part), FIRST
                )
        grad_weight = (grad_weight + swap(grad_weight)) / nd
    return (grad_features[None], adjoint[None], grad_weight)


def solution(mesh):
    placed = (P("dp", "blk", None), P("dp", "blk", None), P("dp", "blk"), P(), P(), P())
    return jax.shard_map(
        on_device,
        mesh=mesh,
        in_specs=placed,
        out_specs=(P("dp", "blk", None), P("dp", "blk", None), P()),
        check_vma=False,
    )
```

```python
import functools

import jax
import jax.numpy as jnp
from jax import lax
from jax.experimental import pallas as pl
from jax.experimental.pallas import tpu as pltpu
from jax.sharding import PartitionSpec as P

FIRST = (((0,), (0,)), ((), ()))
LAST = (((1,), (1,)), ((), ()))
F32 = jnp.float32
BF16 = jnp.bfloat16


def dot(a, b, dims=(((1,), (0,)), ((), ()))):
    return lax.dot_general(a, b, dims, preferred_element_type=F32)


def after(v, *others):
    return lax.optimization_barrier((v, others))[0]


def score_kernel(nz, both, embed, *refs):
    scale, offset = both[0:1, 0:1], both[8:9, 0:1]
    labels, captions, refs = refs[:2], refs[2:4], refs[4:]
    own, unit_own, inv_own, unit, dlogit = refs[:5]
    sent, (caps, sems) = refs[5:-2], refs[-2:]
    n_img, n_cap = embed.shape[0] // nz, captions[0].shape[0]
    copies = []
    for i in range(2):
        here = caps.at[i * n_cap : (i + 1) * n_cap, :]
        copies.append(pltpu.make_async_copy(captions[i], here, sems.at[i]))
        copies[-1].start()
    embed = embed[...]
    inv_norm = lax.rsqrt(jnp.sum(embed * embed, axis=1, keepdims=True) + 1e-06)
    unit_f = embed * inv_norm
    unit_own[...] = unit_f[:n_img]
    inv_own[...] = jnp.broadcast_to(inv_norm[:n_img], inv_own.shape)
    u = unit_f.astype(BF16)
    unit[...] = u
    index = lax.axis_index("blk")
    ids = []
    for k in range(nz):
        first = (index ^ (2 * k)) * n_img
        ids.append(first + lax.broadcasted_iota(jnp.int32, (n_img, 1), 0))
    ids = jnp.concatenate(ids)
    labs = jnp.concatenate([v[...] for v in labels], axis=1)
    sign = jnp.where(labs == ids, 1.0, -1.0).astype(F32)
    for copy in copies:
        copy.wait()
    logits = scale * dot(u, caps[...], LAST) + offset
    d = (-sign * jax.nn.sigmoid(-sign * logits)).astype(BF16)
    dlogit[...] = d
    part = scale * dot(d, caps[...])
    own[...] = part[:n_img]
    for k in range(1, nz):
        sent[k - 1][...] = part[k * n_img : (k + 1) * n_img].astype(BF16)


def scores(nz, both, embed, labels, captions):
    images, depth = embed.shape
    n_img, n_cap = images // nz, captions[0].shape[0]
    caps = 2 * n_cap
    vmem = pl.BlockSpec(memory_space=pltpu.VMEM)
    block = jax.ShapeDtypeStruct((n_img, depth), F32)
    outs = [
        block,
        block,
        jax.ShapeDtypeStruct((n_img, 128), F32),
        jax.ShapeDtypeStruct((images, depth), BF16),
        jax.ShapeDtypeStruct((images, caps), BF16),
    ] + [jax.ShapeDtypeStruct((n_img, depth), BF16)] * (nz - 1)
    return pl.pallas_call(
        functools.partial(score_kernel, nz),
        out_shape=outs,
        in_specs=[vmem] * 4
        + [pl.BlockSpec(memory_space=pl.ANY)] * 2,
        out_specs=[vmem] * len(outs),
        scratch_shapes=[pltpu.VMEM((caps, depth), BF16), pltpu.SemaphoreType.DMA((2,))],
        compiler_params=pltpu.CompilerParams(
            vmem_limit_bytes=12 * 2**20 + 24 * images * depth
        ),
        cost_estimate=pl.CostEstimate(
            flops=4 * images * depth * caps,
            bytes_accessed=2 * depth * (caps + 6 * images),
            transcendentals=images * caps,
        ),
    )(both, embed, *labels, *captions)


def join_kernel(*refs):
    at = 0
    for v in refs[:-1]:
        refs[-1][at : at + v.shape[0], :] = v[...]
        at += v.shape[0]


def joined(vs):
    rows = sum(v.shape[0] for v in vs)
    depth = vs[0].shape[1]
    vmem = pl.BlockSpec(memory_space=pltpu.VMEM)
    return pl.pallas_call(
        join_kernel,
        out_shape=jax.ShapeDtypeStruct((rows, depth), vs[0].dtype),
        in_specs=[vmem] * len(vs),
        out_specs=vmem,
        compiler_params=pltpu.CompilerParams(vmem_limit_bytes=12 * 2**20),
        cost_estimate=pl.CostEstimate(
            flops=0, bytes_accessed=4 * rows * depth, transcendentals=0
        ),
    )(*vs)


def caption_kernel(both, dlogit, unit, own, other):
    scale = both[0:1, 0:1]
    n_cap = own.shape[0]
    own[...] = scale * dot(dlogit[:, :n_cap], unit[...], FIRST)
    other[...] = scale * dot(dlogit[:, n_cap:], unit[...], FIRST)


def caption_sums(both, dlogit, unit):
    images, caps = dlogit.shape
    depth = unit.shape[1]
    vmem = pl.BlockSpec(memory_space=pltpu.VMEM)
    return pl.pallas_call(
        caption_kernel,
        out_shape=[jax.ShapeDtypeStruct((caps // 2, depth), F32)] * 2,
        in_specs=[vmem] * 3,
        out_specs=[vmem] * 2,
        compiler_params=pltpu.CompilerParams(
            vmem_limit_bytes=10 * 2**20 + 8 * images * depth
        ),
        cost_estimate=pl.CostEstimate(
            flops=2 * images * caps * depth,
            bytes_accessed=4 * caps * depth + 2 * images * (depth + caps),
            transcendentals=0,
        ),
    )(both, dlogit, unit)


def embed_grad_kernel(own, unit, inv_norm, *refs):
    back, out = refs[:-1], refs[-1]
    total = own[...]
    for v in back:
        total = total + v[...].astype(F32)
    u = unit[...]
    radial = jnp.sum(u * total, axis=1, keepdims=True)
    out[...] = ((total - u * radial) * inv_norm[:, :1]).astype(BF16)


def embed_grad(own, unit, inv_norm, back):
    vmem = pl.BlockSpec(memory_space=pltpu.VMEM)
    return pl.pallas_call(
        embed_grad_kernel,
        out_shape=jax.ShapeDtypeStruct(own.shape, BF16),
        in_specs=[vmem] * (3 + len(back)),
        out_specs=vmem,
        compiler_params=pltpu.CompilerParams(vmem_limit_bytes=8 * 2**20),
        cost_estimate=pl.CostEstimate(
            flops=8 * own.size, bytes_accessed=12 * own.size, transcendentals=0
        ),
    )(own, unit, inv_norm, *back)


def turn_kernel(plan, *refs):
    ins, outs = refs[: -len(plan)], refs[-len(plan) :]
    for out, pieces in zip(outs, plan):
        col = 0
        for runs in pieces:
            rows = [ins[i][at : at + size, :] for i, at, size in runs]
            rows = jnp.concatenate(rows)
            out[:, col : col + rows.shape[0]] = rows.T
            col += rows.shape[0]


def turned(xs, plan):
    depth = xs[0].shape[1]
    images = [sum(size for runs in pieces for _, _, size in runs) for pieces in plan]
    return pl.pallas_call(
        functools.partial(turn_kernel, plan),
        out_shape=[jax.ShapeDtypeStruct((depth, n), BF16) for n in images],
        in_specs=[pl.BlockSpec(memory_space=pltpu.VMEM)] * len(xs),
        out_specs=[pl.BlockSpec(memory_space=pltpu.VMEM)] * len(plan),
        compiler_params=pltpu.CompilerParams(vmem_limit_bytes=16 * 2**20),
        cost_estimate=pl.CostEstimate(
            flops=0, bytes_accessed=4 * sum(images) * depth, transcendentals=0
        ),
    )(*xs)


def stack(stacked, gs):
    at = 0
    for g in gs:
        stacked[at : at + g.shape[0], :] = g[...]
        at += g.shape[0]


def early_kernel(n, has_acc, x_t, *refs):
    gs, (out, stacked) = refs[has_acc:-2], refs[-2:]
    stack(stacked, gs)
    rows = out.shape[0] // n
    for i in range(n):
        here = slice(i * rows, (i + 1) * rows)
        total = dot(x_t[here, :], stacked[...])
        out[here, :] = refs[0][here, :] + total if has_acc else total


def late_kernel(factor, x_t, acc, *refs):
    gs, (out, stacked, tiles, sems) = refs[:-4], refs[-4:]
    stack(stacked, gs)
    n, rows = tiles.shape[:2]
    copies = []
    for i in range(n):
        here = slice(i * rows, (i + 1) * rows)
        tiles[i] = (acc[here, :] + dot(x_t[here, :], stacked[...])) * factor
        copies.append(pltpu.make_async_copy(tiles.at[i], out.at[here, :], sems.at[i]))
        copies[-1].start()
    for copy in copies:
        copy.wait()


def weight_sum(acc, x_t, gs, factor=None):
    depth, images = x_t.shape
    n = 3
    early, has_acc = factor is None, int(acc is not None)
    vmem = pl.BlockSpec(memory_space=pltpu.VMEM)
    scratch = [pltpu.VMEM((images, depth), BF16)]
    if early:
        kernel = functools.partial(early_kernel, n, has_acc)
    else:
        kernel = functools.partial(late_kernel, factor)
        scratch.append(pltpu.VMEM((n, depth // n, depth), F32))
        scratch.append(pltpu.SemaphoreType.DMA((n,)))
    operands = [x_t] + [acc] * has_acc + gs
    return pl.pallas_call(
        kernel,
        out_shape=jax.ShapeDtypeStruct((depth, depth), F32),
        in_specs=[vmem] * len(operands),
        out_specs=vmem if early else pl.BlockSpec(memory_space=pl.ANY),
        scratch_shapes=scratch,
        compiler_params=pltpu.CompilerParams(vmem_limit_bytes=24 * 2**20),
        cost_estimate=pl.CostEstimate(
            flops=2 * images * depth * depth,
            bytes_accessed=4 * images * depth + 4 * depth * depth * (1 + has_acc),
            transcendentals=0,
        ),
    )(*operands)


def on_device(x, captions, labels, weight, scale, offset):
    x, captions = x[0], captions[0]
    n_img, depth = x.shape
    n_cap = captions.shape[0]
    nd, nb = lax.axis_size("dp"), lax.axis_size("blk")
    nz = nb // 2
    bits = nd.bit_length() - 1

    def along_z(v, k):
        return lax.ppermute(v, "blk", [(i, i ^ (2 * k)) for i in range(nb)])

    def swap(v):
        return lax.ppermute(v, "blk", [(i, i ^ 1) for i in range(nb)])

    def step_d(v, i):
        perm = []
        for j in range(nd):
            for m in range(nb):
                to = j ^ (1 << ((i + m % 2) % bits))
                perm.append((j * nb + m, to * nb + m))
        return lax.ppermute(v, ("dp", "blk"), perm)

    def direct_d(v, chunk):
        perm = []
        for j in range(nd):
            for m in range(nb):
                to = j
                for i in range(bits):
                    if chunk >> i & 1:
                        to ^= 1 << ((i + m % 2) % bits)
                perm.append((j * nb + m, to * nb + m))
        return lax.ppermute(v, ("dp", "blk"), perm)

    def over_d(v, first, *before):
        v = [v, first]
        for i in range(1, bits):
            v = after(jnp.concatenate(v), before)
            v = [v, step_d(v, i)]
        return v

    half = nz // 2
    xs = [x] + [along_z(x, k) for k in range(1, nz)]
    x_own = over_d(x, step_d(after(x, xs[1]), 0))
    x_rest = jnp.concatenate(xs[1:])
    embed = dot(joined(after(xs, x)), weight)
    row = lax.broadcasted_iota(jnp.int32, (16, 128), 0)
    both = jnp.where(row < 8, scale, offset)
    own, u, inv_norm, unit, dlogit, *sent = scores(
        nz,
        both,
        embed,
        [labels, swap(labels)],
        [captions, swap(captions)],
    )
    sent = after(sent, x_own)
    back = [along_z(v, k + 1) for k, v in enumerate(sent)]
    x_rest = after(x_rest, x)
    x_rest = over_d(x_rest, after(step_d(x_rest, 0), sent))
    adjoint, adjoint_other = caption_sums(both, after(dlogit, sent), unit)
    adjoint_other = swap(adjoint_other)
    adjoint = adjoint + adjoint_other
    back = after(back, x_rest, adjoint_other)
    ge = embed_grad(own, u, inv_norm, back)
    grad_features = dot(ge, weight, LAST)

    small = nd * nb * n_img <= 2048
    x_other = []
    if small:
        x_all = joined(x_own + x_rest)
        x_other = swap(after(x_all, ge))

    near = [along_z(ge, k) for k in range(1, half)]
    own_first = step_d(ge, 0)
    far = [along_z(ge, k) for k in range(half, nz)]
    g_own = over_d(ge, own_first)
    near = after(jnp.concatenate(near), g_own[0], ge)
    near_first = step_d(near, 0)
    g_near = over_d(near, near_first)
    far = after(jnp.concatenate(far), g_own[1], near_first, grad_features, adjoint, x_other)
    g_far = [far] + [direct_d(far, i) for i in range(1, nd)]
    sizes = [n_img, n_img * (half - 1), n_img * half]
    n_rest = sizes[1] + sizes[2]
    per = nd // 2
    if small:
        plan = [[], []]
        for core in range(2):
            rest = [n_img * nd + i * n_rest for i in range(nd)]
            far_runs = [(core, at + sizes[1], sizes[2]) for at in rest]
            plan[0] += [[(core, 0, n_img * nd)], far_runs[:1]]
            plan[1] += [[(core, at, sizes[1]) for at in rest], far_runs[1:]]
        x_early, x_late = turned([x_all, x_other], plan)
        early = jnp.concatenate(g_own + g_far[:1])
        early_swapped = swap(early)
        acc = weight_sum(None, x_early, [early, early_swapped])
        before_late = (x_early, grad_features, adjoint)
        late = [after(v, acc) for v in g_far[1:]]
        g_near = jnp.concatenate(g_near)
        late = [g_near] + late + [swap(g_near)] + [swap(v) for v in late]
        grad_weight = weight_sum(acc, x_late, late, 1.0 / nd)
    else:
        g_far = [jnp.concatenate(g_far[:per]), jnp.concatenate(g_far[per:])]
        grad_weight = 0.0
        for v, g in zip(x_own, g_own):
            grad_weight = grad_weight + dot(v, g, FIRST)
        for v, g, h in zip(x_rest, g_near, g_far):
            for i in range(per):
                g_part = [
                    g[i * sizes[1] : (i + 1) * sizes[1]],
                    h[i * sizes[2] : (i + 1) * sizes[2]],
                ]
                grad_weight = grad_weight + dot(
                    v[i * n_rest : (i + 1) * n_rest], jnp.concatenate(g_part), FIRST
                )
        grad_weight = (grad_weight + swap(grad_weight)) / nd
    return (grad_features[None], adjoint[None], grad_weight)


def solution(mesh):
    placed = (P("dp", "blk", None), P("dp", "blk", None), P("dp", "blk"), P(), P(), P())
    return jax.shard_map(
        on_device,
        mesh=mesh,
        in_specs=placed,
        out_specs=(P("dp", "blk", None), P("dp", "blk", None), P()),
        check_vma=False,
    )
```

```python
import functools

import jax
import jax.numpy as jnp
from jax import lax
from jax.experimental import pallas as pl
from jax.experimental.pallas import tpu as pltpu
from jax.sharding import PartitionSpec as P

FIRST = (((0,), (0,)), ((), ()))
LAST = (((1,), (1,)), ((), ()))
F32 = jnp.float32
BF16 = jnp.bfloat16


def dot(a, b, dims=(((1,), (0,)), ((), ()))):
    return lax.dot_general(a, b, dims, preferred_element_type=F32)


def after(v, *others):
    return lax.optimization_barrier((v, others))[0]


def score_kernel(nz, both, embed, *refs):
    scale, offset = both[0:1, 0:1], both[8:9, 0:1]
    labels, captions, refs = refs[:2], refs[2:4], refs[4:]
    own, unit_own, inv_own, unit, dlogit = refs[:5]
    sent, (caps, sems) = refs[5:-2], refs[-2:]
    n_img, n_cap = embed.shape[0] // nz, captions[0].shape[0]
    copies = []
    for i in range(2):
        here = caps.at[i * n_cap : (i + 1) * n_cap, :]
        copies.append(pltpu.make_async_copy(captions[i], here, sems.at[i]))
        copies[-1].start()
    embed = embed[...]
    inv_norm = lax.rsqrt(jnp.sum(embed * embed, axis=1, keepdims=True) + 1e-06)
    unit_f = embed * inv_norm
    unit_own[...] = unit_f[:n_img]
    inv_own[...] = jnp.broadcast_to(inv_norm[:n_img], inv_own.shape)
    u = unit_f.astype(BF16)
    unit[...] = u
    index = lax.axis_index("blk")
    ids = []
    for k in range(nz):
        first = (index ^ (2 * k)) * n_img
        ids.append(first + lax.broadcasted_iota(jnp.int32, (n_img, 1), 0))
    ids = jnp.concatenate(ids)
    labs = jnp.concatenate([v[...] for v in labels], axis=1)
    sign = jnp.where(labs == ids, 1.0, -1.0).astype(F32)
    for copy in copies:
        copy.wait()
    logits = scale * dot(u, caps[...], LAST) + offset
    d = (-sign * jax.nn.sigmoid(-sign * logits)).astype(BF16)
    dlogit[...] = d
    part = scale * dot(d, caps[...])
    own[...] = part[:n_img]
    for k in range(1, nz):
        sent[k - 1][...] = part[k * n_img : (k + 1) * n_img].astype(BF16)


def scores(nz, both, embed, labels, captions):
    images, depth = embed.shape
    n_img, n_cap = images // nz, captions[0].shape[0]
    caps = 2 * n_cap
    vmem = pl.BlockSpec(memory_space=pltpu.VMEM)
    block = jax.ShapeDtypeStruct((n_img, depth), F32)
    outs = [
        block,
        block,
        jax.ShapeDtypeStruct((n_img, 128), F32),
        jax.ShapeDtypeStruct((images, depth), BF16),
        jax.ShapeDtypeStruct((images, caps), BF16),
    ] + [jax.ShapeDtypeStruct((n_img, depth), BF16)] * (nz - 1)
    return pl.pallas_call(
        functools.partial(score_kernel, nz),
        out_shape=outs,
        in_specs=[vmem] * 4
        + [pl.BlockSpec(memory_space=pl.ANY)] * 2,
        out_specs=[vmem] * len(outs),
        scratch_shapes=[pltpu.VMEM((caps, depth), BF16), pltpu.SemaphoreType.DMA((2,))],
        compiler_params=pltpu.CompilerParams(
            vmem_limit_bytes=12 * 2**20 + 24 * images * depth
        ),
        cost_estimate=pl.CostEstimate(
            flops=4 * images * depth * caps,
            bytes_accessed=2 * depth * (caps + 6 * images),
            transcendentals=images * caps,
        ),
    )(both, embed, *labels, *captions)


def join_kernel(*refs):
    at = 0
    for v in refs[:-1]:
        refs[-1][at : at + v.shape[0], :] = v[...]
        at += v.shape[0]


def joined(vs):
    rows = sum(v.shape[0] for v in vs)
    depth = vs[0].shape[1]
    vmem = pl.BlockSpec(memory_space=pltpu.VMEM)
    return pl.pallas_call(
        join_kernel,
        out_shape=jax.ShapeDtypeStruct((rows, depth), vs[0].dtype),
        in_specs=[vmem] * len(vs),
        out_specs=vmem,
        compiler_params=pltpu.CompilerParams(vmem_limit_bytes=12 * 2**20),
        cost_estimate=pl.CostEstimate(
            flops=0, bytes_accessed=4 * rows * depth, transcendentals=0
        ),
    )(*vs)


def caption_kernel(both, dlogit, unit, own, other):
    scale = both[0:1, 0:1]
    n_cap = own.shape[0]
    own[...] = scale * dot(dlogit[:, :n_cap], unit[...], FIRST)
    other[...] = scale * dot(dlogit[:, n_cap:], unit[...], FIRST)


def caption_sums(both, dlogit, unit):
    images, caps = dlogit.shape
    depth = unit.shape[1]
    vmem = pl.BlockSpec(memory_space=pltpu.VMEM)
    return pl.pallas_call(
        caption_kernel,
        out_shape=[jax.ShapeDtypeStruct((caps // 2, depth), F32)] * 2,
        in_specs=[vmem] * 3,
        out_specs=[vmem] * 2,
        compiler_params=pltpu.CompilerParams(
            vmem_limit_bytes=10 * 2**20 + 8 * images * depth
        ),
        cost_estimate=pl.CostEstimate(
            flops=2 * images * caps * depth,
            bytes_accessed=4 * caps * depth + 2 * images * (depth + caps),
            transcendentals=0,
        ),
    )(both, dlogit, unit)


def embed_grad_kernel(own, unit, inv_norm, *refs):
    back, out = refs[:-1], refs[-1]
    total = own[...]
    for v in back:
        total = total + v[...].astype(F32)
    u = unit[...]
    radial = jnp.sum(u * total, axis=1, keepdims=True)
    out[...] = ((total - u * radial) * inv_norm[:, :1]).astype(BF16)


def embed_grad(own, unit, inv_norm, back):
    vmem = pl.BlockSpec(memory_space=pltpu.VMEM)
    return pl.pallas_call(
        embed_grad_kernel,
        out_shape=jax.ShapeDtypeStruct(own.shape, BF16),
        in_specs=[vmem] * (3 + len(back)),
        out_specs=vmem,
        compiler_params=pltpu.CompilerParams(vmem_limit_bytes=8 * 2**20),
        cost_estimate=pl.CostEstimate(
            flops=8 * own.size, bytes_accessed=12 * own.size, transcendentals=0
        ),
    )(own, unit, inv_norm, *back)


def turn_kernel(plan, *refs):
    ins, outs = refs[: -len(plan)], refs[-len(plan) :]
    for out, pieces in zip(outs, plan):
        col = 0
        for runs in pieces:
            rows = [ins[i][at : at + size, :] for i, at, size in runs]
            rows = jnp.concatenate(rows)
            out[:, col : col + rows.shape[0]] = rows.T
            col += rows.shape[0]


def turned(xs, plan):
    depth = xs[0].shape[1]
    images = [sum(size for runs in pieces for _, _, size in runs) for pieces in plan]
    return pl.pallas_call(
        functools.partial(turn_kernel, plan),
        out_shape=[jax.ShapeDtypeStruct((depth, n), BF16) for n in images],
        in_specs=[pl.BlockSpec(memory_space=pltpu.VMEM)] * len(xs),
        out_specs=[pl.BlockSpec(memory_space=pltpu.VMEM)] * len(plan),
        compiler_params=pltpu.CompilerParams(vmem_limit_bytes=16 * 2**20),
        cost_estimate=pl.CostEstimate(
            flops=0, bytes_accessed=4 * sum(images) * depth, transcendentals=0
        ),
    )(*xs)


def stack(stacked, gs):
    at = 0
    for g in gs:
        stacked[at : at + g.shape[0], :] = g[...]
        at += g.shape[0]


def early_kernel(n, has_acc, x_t, *refs):
    gs, (out, stacked) = refs[has_acc:-2], refs[-2:]
    stack(stacked, gs)
    rows = out.shape[0] // n
    for i in range(n):
        here = slice(i * rows, (i + 1) * rows)
        total = dot(x_t[here, :], stacked[...])
        out[here, :] = refs[0][here, :] + total if has_acc else total


def late_kernel(factor, x_t, acc, *refs):
    gs, (out, stacked, tiles, sems) = refs[:-4], refs[-4:]
    stack(stacked, gs)
    n, rows = tiles.shape[:2]
    copies = []
    for i in range(n):
        here = slice(i * rows, (i + 1) * rows)
        tiles[i] = (acc[here, :] + dot(x_t[here, :], stacked[...])) * factor
        copies.append(pltpu.make_async_copy(tiles.at[i], out.at[here, :], sems.at[i]))
        copies[-1].start()
    for copy in copies:
        copy.wait()


def weight_sum(acc, x_t, gs, factor=None):
    depth, images = x_t.shape
    n = 3
    early, has_acc = factor is None, int(acc is not None)
    vmem = pl.BlockSpec(memory_space=pltpu.VMEM)
    scratch = [pltpu.VMEM((images, depth), BF16)]
    if early:
        kernel = functools.partial(early_kernel, n, has_acc)
    else:
        kernel = functools.partial(late_kernel, factor)
        scratch.append(pltpu.VMEM((n, depth // n, depth), F32))
        scratch.append(pltpu.SemaphoreType.DMA((n,)))
    operands = [x_t] + [acc] * has_acc + gs
    return pl.pallas_call(
        kernel,
        out_shape=jax.ShapeDtypeStruct((depth, depth), F32),
        in_specs=[vmem] * len(operands),
        out_specs=vmem if early else pl.BlockSpec(memory_space=pl.ANY),
        scratch_shapes=scratch,
        compiler_params=pltpu.CompilerParams(vmem_limit_bytes=24 * 2**20),
        cost_estimate=pl.CostEstimate(
            flops=2 * images * depth * depth,
            bytes_accessed=4 * images * depth + 4 * depth * depth * (1 + has_acc),
            transcendentals=0,
        ),
    )(*operands)


def on_device(x, captions, labels, weight, scale, offset):
    x, captions = x[0], captions[0]
    n_img, depth = x.shape
    n_cap = captions.shape[0]
    nd, nb = lax.axis_size("dp"), lax.axis_size("blk")
    nz = nb // 2
    bits = nd.bit_length() - 1

    def along_z(v, k):
        return lax.ppermute(v, "blk", [(i, i ^ (2 * k)) for i in range(nb)])

    def swap(v):
        return lax.ppermute(v, "blk", [(i, i ^ 1) for i in range(nb)])

    def step_d(v, i):
        perm = []
        for j in range(nd):
            for m in range(nb):
                to = j ^ (1 << ((i + m % 2) % bits))
                perm.append((j * nb + m, to * nb + m))
        return lax.ppermute(v, ("dp", "blk"), perm)

    def over_d(v, first, *before):
        v = [v, first]
        for i in range(1, bits):
            v = after(jnp.concatenate(v), before)
            v = [v, step_d(v, i)]
        return v

    half = nz // 2
    xs = [x] + [along_z(x, k) for k in range(1, nz)]
    x_own = joined(xs)
    x_first = step_d(x_own, 0)
    embed = dot(x_own, weight)
    row = lax.broadcasted_iota(jnp.int32, (16, 128), 0)
    both = jnp.where(row < 8, scale, offset)
    own, u, inv_norm, unit, dlogit, *sent = scores(
        nz,
        both,
        embed,
        [labels, swap(labels)],
        [captions, swap(captions)],
    )
    x_own = [x_own, after(x_first, sent)]
    for i in range(1, bits):
        x_own = joined(x_own)
        x_own = [x_own, step_d(x_own, i)]
    sent = after(sent, x_own[0])
    back = [along_z(v, k + 1) for k, v in enumerate(sent)]
    back = after(back, x_own[0])
    ge = embed_grad(own, u, inv_norm, back)
    grad_features = dot(ge, weight, LAST)

    small = nd * nb * n_img <= 2048
    near = [along_z(ge, k) for k in range(1, half)]
    own_first = step_d(ge, 0)
    far = [along_z(ge, k) for k in range(half, nz)]
    g_own = over_d(ge, own_first)
    near = after(jnp.concatenate(near), g_own[0], ge)
    near_first = step_d(near, 0)
    g_near = over_d(near, near_first)
    far = after(jnp.concatenate(far), g_own[1], near_first, grad_features)
    far_first = step_d(far, 0)
    adjoint, adjoint_other = caption_sums(both, after(dlogit, far_first), unit)
    adjoint = adjoint + swap(adjoint_other)
    sizes = [n_img, n_img * (half - 1), n_img * half]
    n_own = nz * n_img
    per = nd // 2
    if small:
        x_all = joined(x_own)
        x_other = swap(after(x_all, far))
        plan = [[], []]
        for core in range(2):
            at = 0
            for g, size in enumerate(sizes):
                runs = [(core, i * n_own + at, size) for i in range(nd)]
                if g < 2:
                    plan[0].append(runs)
                else:
                    plan[0].append(runs[:per])
                    plan[1].append(runs[per:])
                at += size
        x_early, x_late = turned([x_all, x_other], plan)
        g_two = [jnp.concatenate(g_own + g_near)]
        g_two.append(swap(g_two[0]))
        g_far = over_d(far, far_first, far_first)
        early = [g_two[0], g_far[0], g_two[1], swap(g_far[0])]
        acc = weight_sum(None, x_early, early)
        late = after(g_far[1], acc, adjoint)
        grad_weight = weight_sum(acc, x_late, [late, swap(late)], 1.0 / nd)
    else:
        g_far = over_d(far, far_first)
        grad_weight = 0.0
        for i, x_part in enumerate(x_own):
            for at in range(per):
                g_part = [
                    g[i][at * m : (at + 1) * m]
                    for m, g in zip(sizes, (g_own, g_near, g_far))
                ]
                grad_weight = grad_weight + dot(
                    x_part[at * n_own : (at + 1) * n_own],
                    jnp.concatenate(g_part),
                    FIRST,
                )
        grad_weight = (grad_weight + swap(grad_weight)) / nd
    return (grad_features[None], adjoint[None], grad_weight)


def solution(mesh):
    placed = (P("dp", "blk", None), P("dp", "blk", None), P("dp", "blk"), P(), P(), P())
    return jax.shard_map(
        on_device,
        mesh=mesh,
        in_specs=placed,
        out_specs=(P("dp", "blk", None), P("dp", "blk", None), P()),
        check_vma=False,
    )
```

```python
import functools

import jax
import jax.numpy as jnp
from jax import lax
from jax.experimental import pallas as pl
from jax.experimental.pallas import tpu as pltpu
from jax.sharding import PartitionSpec as P

FIRST = (((0,), (0,)), ((), ()))
LAST = (((1,), (1,)), ((), ()))
F32 = jnp.float32
BF16 = jnp.bfloat16


def dot(a, b, dims=(((1,), (0,)), ((), ()))):
    return lax.dot_general(a, b, dims, preferred_element_type=F32)


def after(v, *others):
    return lax.optimization_barrier((v, others))[0]


def score_kernel(nz, both, embed, *refs):
    scale, offset = both[0:1, 0:1], both[8:9, 0:1]
    labels, captions, refs = refs[:2], refs[2:4], refs[4:]
    own, unit_own, inv_own, unit, dlogit = refs[:5]
    sent, (caps, sems) = refs[5:-2], refs[-2:]
    n_img, n_cap = embed.shape[0] // nz, captions[0].shape[0]
    copies = []
    for i in range(2):
        here = caps.at[i * n_cap : (i + 1) * n_cap, :]
        copies.append(pltpu.make_async_copy(captions[i], here, sems.at[i]))
        copies[-1].start()
    embed = embed[...]
    inv_norm = lax.rsqrt(jnp.sum(embed * embed, axis=1, keepdims=True) + 1e-06)
    unit_f = embed * inv_norm
    unit_own[...] = unit_f[:n_img]
    inv_own[...] = jnp.broadcast_to(inv_norm[:n_img], inv_own.shape)
    u = unit_f.astype(BF16)
    unit[...] = u
    index = lax.axis_index("blk")
    ids = []
    for k in range(nz):
        first = (index ^ (2 * k)) * n_img
        ids.append(first + lax.broadcasted_iota(jnp.int32, (n_img, 1), 0))
    ids = jnp.concatenate(ids)
    labs = jnp.concatenate([v[...] for v in labels], axis=1)
    sign = jnp.where(labs == ids, 1.0, -1.0).astype(F32)
    for copy in copies:
        copy.wait()
    logits = scale * dot(u, caps[...], LAST) + offset
    d = (-sign * jax.nn.sigmoid(-sign * logits)).astype(BF16)
    dlogit[...] = d
    part = scale * dot(d, caps[...])
    own[...] = part[:n_img]
    for k in range(1, nz):
        sent[k - 1][...] = part[k * n_img : (k + 1) * n_img].astype(BF16)


def scores(nz, both, embed, labels, captions):
    images, depth = embed.shape
    n_img, n_cap = images // nz, captions[0].shape[0]
    caps = 2 * n_cap
    vmem = pl.BlockSpec(memory_space=pltpu.VMEM)
    block = jax.ShapeDtypeStruct((n_img, depth), F32)
    outs = [
        block,
        block,
        jax.ShapeDtypeStruct((n_img, 128), F32),
        jax.ShapeDtypeStruct((images, depth), BF16),
        jax.ShapeDtypeStruct((images, caps), BF16),
    ] + [jax.ShapeDtypeStruct((n_img, depth), BF16)] * (nz - 1)
    return pl.pallas_call(
        functools.partial(score_kernel, nz),
        out_shape=outs,
        in_specs=[vmem] * 4
        + [pl.BlockSpec(memory_space=pl.ANY)] * 2,
        out_specs=[vmem] * len(outs),
        scratch_shapes=[pltpu.VMEM((caps, depth), BF16), pltpu.SemaphoreType.DMA((2,))],
        compiler_params=pltpu.CompilerParams(
            vmem_limit_bytes=12 * 2**20 + 24 * images * depth
        ),
        cost_estimate=pl.CostEstimate(
            flops=4 * images * depth * caps,
            bytes_accessed=2 * depth * (caps + 6 * images),
            transcendentals=images * caps,
        ),
    )(both, embed, *labels, *captions)


def join_kernel(*refs):
    at = 0
    for v in refs[:-1]:
        refs[-1][at : at + v.shape[0], :] = v[...]
        at += v.shape[0]


def joined(vs):
    rows = sum(v.shape[0] for v in vs)
    depth = vs[0].shape[1]
    vmem = pl.BlockSpec(memory_space=pltpu.VMEM)
    return pl.pallas_call(
        join_kernel,
        out_shape=jax.ShapeDtypeStruct((rows, depth), vs[0].dtype),
        in_specs=[vmem] * len(vs),
        out_specs=vmem,
        compiler_params=pltpu.CompilerParams(vmem_limit_bytes=12 * 2**20),
        cost_estimate=pl.CostEstimate(
            flops=0, bytes_accessed=4 * rows * depth, transcendentals=0
        ),
    )(*vs)


def caption_kernel(both, dlogit, unit, own, other):
    scale = both[0:1, 0:1]
    n_cap = own.shape[0]
    own[...] = scale * dot(dlogit[:, :n_cap], unit[...], FIRST)
    other[...] = scale * dot(dlogit[:, n_cap:], unit[...], FIRST)


def caption_sums(both, dlogit, unit):
    images, caps = dlogit.shape
    depth = unit.shape[1]
    vmem = pl.BlockSpec(memory_space=pltpu.VMEM)
    return pl.pallas_call(
        caption_kernel,
        out_shape=[jax.ShapeDtypeStruct((caps // 2, depth), F32)] * 2,
        in_specs=[vmem] * 3,
        out_specs=[vmem] * 2,
        compiler_params=pltpu.CompilerParams(
            vmem_limit_bytes=10 * 2**20 + 8 * images * depth
        ),
        cost_estimate=pl.CostEstimate(
            flops=2 * images * caps * depth,
            bytes_accessed=4 * caps * depth + 2 * images * (depth + caps),
            transcendentals=0,
        ),
    )(both, dlogit, unit)


def embed_grad_kernel(own, unit, inv_norm, *refs):
    back, out = refs[:-1], refs[-1]
    total = own[...]
    for v in back:
        total = total + v[...].astype(F32)
    u = unit[...]
    radial = jnp.sum(u * total, axis=1, keepdims=True)
    out[...] = ((total - u * radial) * inv_norm[:, :1]).astype(BF16)


def embed_grad(own, unit, inv_norm, back):
    vmem = pl.BlockSpec(memory_space=pltpu.VMEM)
    return pl.pallas_call(
        embed_grad_kernel,
        out_shape=jax.ShapeDtypeStruct(own.shape, BF16),
        in_specs=[vmem] * (3 + len(back)),
        out_specs=vmem,
        compiler_params=pltpu.CompilerParams(vmem_limit_bytes=8 * 2**20),
        cost_estimate=pl.CostEstimate(
            flops=8 * own.size, bytes_accessed=12 * own.size, transcendentals=0
        ),
    )(own, unit, inv_norm, *back)


def turn_kernel(plan, *refs):
    ins, outs = refs[: -len(plan)], refs[-len(plan) :]
    for out, pieces in zip(outs, plan):
        col = 0
        for runs in pieces:
            rows = [ins[i][at : at + size, :] for i, at, size in runs]
            rows = jnp.concatenate(rows)
            out[:, col : col + rows.shape[0]] = rows.T
            col += rows.shape[0]


def turned(xs, plan):
    depth = xs[0].shape[1]
    images = [sum(size for runs in pieces for _, _, size in runs) for pieces in plan]
    return pl.pallas_call(
        functools.partial(turn_kernel, plan),
        out_shape=[jax.ShapeDtypeStruct((depth, n), BF16) for n in images],
        in_specs=[pl.BlockSpec(memory_space=pltpu.VMEM)] * len(xs),
        out_specs=[pl.BlockSpec(memory_space=pltpu.VMEM)] * len(plan),
        compiler_params=pltpu.CompilerParams(vmem_limit_bytes=16 * 2**20),
        cost_estimate=pl.CostEstimate(
            flops=0, bytes_accessed=4 * sum(images) * depth, transcendentals=0
        ),
    )(*xs)


def stack(stacked, gs):
    at = 0
    for g in gs:
        stacked[at : at + g.shape[0], :] = g[...]
        at += g.shape[0]


def early_kernel(n, has_acc, x_t, *refs):
    gs, (out, stacked) = refs[has_acc:-2], refs[-2:]
    stack(stacked, gs)
    rows = out.shape[0] // n
    for i in range(n):
        here = slice(i * rows, (i + 1) * rows)
        total = dot(x_t[here, :], stacked[...])
        out[here, :] = refs[0][here, :] + total if has_acc else total


def late_kernel(factor, x_t, acc, *refs):
    gs, (out, stacked, tiles, sems) = refs[:-4], refs[-4:]
    stack(stacked, gs)
    n, rows = tiles.shape[:2]
    copies = []
    for i in range(n):
        here = slice(i * rows, (i + 1) * rows)
        tiles[i] = (acc[here, :] + dot(x_t[here, :], stacked[...])) * factor
        copies.append(pltpu.make_async_copy(tiles.at[i], out.at[here, :], sems.at[i]))
        copies[-1].start()
    for copy in copies:
        copy.wait()


def weight_sum(acc, x_t, gs, factor=None):
    depth, images = x_t.shape
    n = 3
    early, has_acc = factor is None, int(acc is not None)
    vmem = pl.BlockSpec(memory_space=pltpu.VMEM)
    scratch = [pltpu.VMEM((images, depth), BF16)]
    if early:
        kernel = functools.partial(early_kernel, n, has_acc)
    else:
        kernel = functools.partial(late_kernel, factor)
        scratch.append(pltpu.VMEM((n, depth // n, depth), F32))
        scratch.append(pltpu.SemaphoreType.DMA((n,)))
    operands = [x_t] + [acc] * has_acc + gs
    return pl.pallas_call(
        kernel,
        out_shape=jax.ShapeDtypeStruct((depth, depth), F32),
        in_specs=[vmem] * len(operands),
        out_specs=vmem if early else pl.BlockSpec(memory_space=pl.ANY),
        scratch_shapes=scratch,
        compiler_params=pltpu.CompilerParams(vmem_limit_bytes=24 * 2**20),
        cost_estimate=pl.CostEstimate(
            flops=2 * images * depth * depth,
            bytes_accessed=4 * images * depth + 4 * depth * depth * (1 + has_acc),
            transcendentals=0,
        ),
    )(*operands)


def on_device(x, captions, labels, weight, scale, offset):
    x, captions = x[0], captions[0]
    n_img, depth = x.shape
    n_cap = captions.shape[0]
    nd, nb = lax.axis_size("dp"), lax.axis_size("blk")
    nz = nb // 2
    bits = nd.bit_length() - 1

    def along_z(v, k):
        return lax.ppermute(v, "blk", [(i, i ^ (2 * k)) for i in range(nb)])

    def swap(v):
        return lax.ppermute(v, "blk", [(i, i ^ 1) for i in range(nb)])

    def step_d(v, i):
        perm = []
        for j in range(nd):
            for m in range(nb):
                to = j ^ (1 << ((i + m % 2) % bits))
                perm.append((j * nb + m, to * nb + m))
        return lax.ppermute(v, ("dp", "blk"), perm)

    def over_d(v, first, *before):
        v = [v, first]
        for i in range(1, bits):
            v = after(jnp.concatenate(v), before)
            v = [v, step_d(v, i)]
        return v

    half = nz // 2
    xs = [x] + [along_z(x, k) for k in range(1, nz)]
    x_own = joined(xs)
    embed = dot(x_own, weight)
    row = lax.broadcasted_iota(jnp.int32, (16, 128), 0)
    both = jnp.where(row < 8, scale, offset)
    own, u, inv_norm, unit, dlogit, *sent = scores(
        nz,
        both,
        embed,
        [labels, swap(labels)],
        [captions, swap(captions)],
    )
    sent = sent
    back = [along_z(v, k + 1) for k, v in enumerate(sent)]
    x_first = step_d(after(x_own, sent), 0)
    x_own = [x_own, after(x_first, back)]
    for i in range(1, bits):
        x_own = joined(x_own)
        x_own = [x_own, step_d(x_own, i)]
    back = back
    ge = embed_grad(own, u, inv_norm, back)
    grad_features = dot(ge, weight, LAST)

    small = nd * nb * n_img <= 2048
    near = [along_z(ge, k) for k in range(1, half)]
    own_first = step_d(ge, 0)
    far = [along_z(ge, k) for k in range(half, nz)]
    g_own = over_d(ge, own_first)
    near = after(jnp.concatenate(near), g_own[0], ge)
    near_first = step_d(near, 0)
    g_near = over_d(near, near_first)
    far = after(jnp.concatenate(far), near_first, g_own[1], grad_features)
    far_first = step_d(far, 0)
    adjoint, adjoint_other = caption_sums(both, after(dlogit, far_first), unit)
    adjoint = adjoint + swap(adjoint_other)
    sizes = [n_img, n_img * (half - 1), n_img * half]
    n_own = nz * n_img
    per = nd // 2
    if small:
        x_all = joined(x_own)
        x_other = swap(after(x_all, far_first))
        plan = [[], []]
        for core in range(2):
            at = 0
            for g, size in enumerate(sizes):
                runs = [(core, i * n_own + at, size) for i in range(nd)]
                if g < 2:
                    plan[0].append(runs)
                else:
                    plan[0].append(runs[:per])
                    plan[1].append(runs[per:])
                at += size
        x_early, x_late = turned([x_all, x_other], plan)
        g_two = [jnp.concatenate(g_own + g_near)]
        g_two.append(swap(g_two[0]))
        g_far = over_d(far, far_first, far_first)
        early = [g_two[0], g_far[0], g_two[1], swap(g_far[0])]
        acc = weight_sum(None, x_early, early)
        late = after(g_far[1], acc, adjoint)
        grad_weight = weight_sum(acc, x_late, [late, swap(late)], 1.0 / nd)
    else:
        g_far = over_d(far, far_first)
        grad_weight = 0.0
        for i, x_part in enumerate(x_own):
            for at in range(per):
                g_part = [
                    g[i][at * m : (at + 1) * m]
                    for m, g in zip(sizes, (g_own, g_near, g_far))
                ]
                grad_weight = grad_weight + dot(
                    x_part[at * n_own : (at + 1) * n_own],
                    jnp.concatenate(g_part),
                    FIRST,
                )
        grad_weight = (grad_weight + swap(grad_weight)) / nd
    return (grad_features[None], adjoint[None], grad_weight)


def solution(mesh):
    placed = (P("dp", "blk", None), P("dp", "blk", None), P("dp", "blk"), P(), P(), P())
    return jax.shard_map(
        on_device,
        mesh=mesh,
        in_specs=placed,
        out_specs=(P("dp", "blk", None), P("dp", "blk", None), P()),
        check_vma=False,
    )
```

```python
import functools

import jax
import jax.numpy as jnp
from jax import lax
from jax.experimental import pallas as pl
from jax.experimental.pallas import tpu as pltpu
from jax.sharding import PartitionSpec as P

FIRST = (((0,), (0,)), ((), ()))
LAST = (((1,), (1,)), ((), ()))
F32 = jnp.float32
BF16 = jnp.bfloat16


def dot(a, b, dims=(((1,), (0,)), ((), ()))):
    return lax.dot_general(a, b, dims, preferred_element_type=F32)


def after(v, *others):
    return lax.optimization_barrier((v, others))[0]


def score_kernel(nz, both, embed, *refs):
    scale, offset = both[0:1, 0:1], both[8:9, 0:1]
    labels, captions, refs = refs[:2], refs[2:4], refs[4:]
    own, unit_own, inv_own, unit, dlogit = refs[:5]
    sent, (caps, sems) = refs[5:-2], refs[-2:]
    n_img, n_cap = embed.shape[0] // nz, captions[0].shape[0]
    copies = []
    for i in range(2):
        here = caps.at[i * n_cap : (i + 1) * n_cap, :]
        copies.append(pltpu.make_async_copy(captions[i], here, sems.at[i]))
        copies[-1].start()
    embed = embed[...]
    inv_norm = lax.rsqrt(jnp.sum(embed * embed, axis=1, keepdims=True) + 1e-06)
    unit_f = embed * inv_norm
    unit_own[...] = unit_f[:n_img]
    inv_own[...] = jnp.broadcast_to(inv_norm[:n_img], inv_own.shape)
    u = unit_f.astype(BF16)
    unit[...] = u
    index = lax.axis_index("blk")
    ids = []
    for k in range(nz):
        first = (index ^ (2 * k)) * n_img
        ids.append(first + lax.broadcasted_iota(jnp.int32, (n_img, 1), 0))
    ids = jnp.concatenate(ids)
    labs = jnp.concatenate([v[...] for v in labels], axis=1)
    sign = jnp.where(labs == ids, 1.0, -1.0).astype(F32)
    for copy in copies:
        copy.wait()
    logits = scale * dot(u, caps[...], LAST) + offset
    d = (-sign * jax.nn.sigmoid(-sign * logits)).astype(BF16)
    dlogit[...] = d
    part = scale * dot(d, caps[...])
    own[...] = part[:n_img]
    for k in range(1, nz):
        sent[k - 1][...] = part[k * n_img : (k + 1) * n_img].astype(BF16)


def scores(nz, both, embed, labels, captions):
    images, depth = embed.shape
    n_img, n_cap = images // nz, captions[0].shape[0]
    caps = 2 * n_cap
    vmem = pl.BlockSpec(memory_space=pltpu.VMEM)
    block = jax.ShapeDtypeStruct((n_img, depth), F32)
    outs = [
        block,
        block,
        jax.ShapeDtypeStruct((n_img, 128), F32),
        jax.ShapeDtypeStruct((images, depth), BF16),
        jax.ShapeDtypeStruct((images, caps), BF16),
    ] + [jax.ShapeDtypeStruct((n_img, depth), BF16)] * (nz - 1)
    return pl.pallas_call(
        functools.partial(score_kernel, nz),
        out_shape=outs,
        in_specs=[vmem] * 4
        + [pl.BlockSpec(memory_space=pl.ANY)] * 2,
        out_specs=[vmem] * len(outs),
        scratch_shapes=[pltpu.VMEM((caps, depth), BF16), pltpu.SemaphoreType.DMA((2,))],
        compiler_params=pltpu.CompilerParams(
            vmem_limit_bytes=12 * 2**20 + 24 * images * depth
        ),
        cost_estimate=pl.CostEstimate(
            flops=4 * images * depth * caps,
            bytes_accessed=2 * depth * (caps + 6 * images),
            transcendentals=images * caps,
        ),
    )(both, embed, *labels, *captions)


def join_kernel(*refs):
    at = 0
    for v in refs[:-1]:
        refs[-1][at : at + v.shape[0], :] = v[...]
        at += v.shape[0]


def joined(vs):
    rows = sum(v.shape[0] for v in vs)
    depth = vs[0].shape[1]
    vmem = pl.BlockSpec(memory_space=pltpu.VMEM)
    return pl.pallas_call(
        join_kernel,
        out_shape=jax.ShapeDtypeStruct((rows, depth), vs[0].dtype),
        in_specs=[vmem] * len(vs),
        out_specs=vmem,
        compiler_params=pltpu.CompilerParams(vmem_limit_bytes=12 * 2**20),
        cost_estimate=pl.CostEstimate(
            flops=0, bytes_accessed=4 * rows * depth, transcendentals=0
        ),
    )(*vs)


def caption_kernel(both, dlogit, unit, own, other):
    scale = both[0:1, 0:1]
    n_cap = own.shape[0]
    own[...] = scale * dot(dlogit[:, :n_cap], unit[...], FIRST)
    other[...] = scale * dot(dlogit[:, n_cap:], unit[...], FIRST)


def caption_sums(both, dlogit, unit):
    images, caps = dlogit.shape
    depth = unit.shape[1]
    vmem = pl.BlockSpec(memory_space=pltpu.VMEM)
    return pl.pallas_call(
        caption_kernel,
        out_shape=[jax.ShapeDtypeStruct((caps // 2, depth), F32)] * 2,
        in_specs=[vmem] * 3,
        out_specs=[vmem] * 2,
        compiler_params=pltpu.CompilerParams(
            vmem_limit_bytes=10 * 2**20 + 8 * images * depth
        ),
        cost_estimate=pl.CostEstimate(
            flops=2 * images * caps * depth,
            bytes_accessed=4 * caps * depth + 2 * images * (depth + caps),
            transcendentals=0,
        ),
    )(both, dlogit, unit)


def embed_grad_kernel(own, unit, inv_norm, *refs):
    back, out = refs[:-1], refs[-1]
    total = own[...]
    for v in back:
        total = total + v[...].astype(F32)
    u = unit[...]
    radial = jnp.sum(u * total, axis=1, keepdims=True)
    out[...] = ((total - u * radial) * inv_norm[:, :1]).astype(BF16)


def embed_grad(own, unit, inv_norm, back):
    vmem = pl.BlockSpec(memory_space=pltpu.VMEM)
    return pl.pallas_call(
        embed_grad_kernel,
        out_shape=jax.ShapeDtypeStruct(own.shape, BF16),
        in_specs=[vmem] * (3 + len(back)),
        out_specs=vmem,
        compiler_params=pltpu.CompilerParams(vmem_limit_bytes=8 * 2**20),
        cost_estimate=pl.CostEstimate(
            flops=8 * own.size, bytes_accessed=12 * own.size, transcendentals=0
        ),
    )(own, unit, inv_norm, *back)


def turn_kernel(plan, *refs):
    ins, outs = refs[: -len(plan)], refs[-len(plan) :]
    for out, pieces in zip(outs, plan):
        col = 0
        for runs in pieces:
            rows = [ins[i][at : at + size, :] for i, at, size in runs]
            rows = jnp.concatenate(rows)
            out[:, col : col + rows.shape[0]] = rows.T
            col += rows.shape[0]


def turned(xs, plan):
    depth = xs[0].shape[1]
    images = [sum(size for runs in pieces for _, _, size in runs) for pieces in plan]
    return pl.pallas_call(
        functools.partial(turn_kernel, plan),
        out_shape=[jax.ShapeDtypeStruct((depth, n), BF16) for n in images],
        in_specs=[pl.BlockSpec(memory_space=pltpu.VMEM)] * len(xs),
        out_specs=[pl.BlockSpec(memory_space=pltpu.VMEM)] * len(plan),
        compiler_params=pltpu.CompilerParams(vmem_limit_bytes=16 * 2**20),
        cost_estimate=pl.CostEstimate(
            flops=0, bytes_accessed=4 * sum(images) * depth, transcendentals=0
        ),
    )(*xs)


def stack(stacked, gs):
    at = 0
    for g in gs:
        stacked[at : at + g.shape[0], :] = g[...]
        at += g.shape[0]


def early_kernel(n, x_t, *refs):
    gs, (out, stacked) = refs[:-2], refs[-2:]
    stack(stacked, gs)
    rows = out.shape[0] // n
    for i in range(n):
        here = slice(i * rows, (i + 1) * rows)
        out[here, :] = dot(x_t[here, :], stacked[...])


def late_kernel(factor, x_t, acc, *refs):
    gs, (out, stacked, tiles, sems) = refs[:-4], refs[-4:]
    stack(stacked, gs)
    n, rows = tiles.shape[:2]
    copies = []
    for i in range(n):
        here = slice(i * rows, (i + 1) * rows)
        tiles[i] = (acc[here, :] + dot(x_t[here, :], stacked[...])) * factor
        copies.append(pltpu.make_async_copy(tiles.at[i], out.at[here, :], sems.at[i]))
        copies[-1].start()
    for copy in copies:
        copy.wait()


def weight_sum(acc, x_t, gs, factor):
    depth, images = x_t.shape
    n = 3
    early = acc is None
    vmem = pl.BlockSpec(memory_space=pltpu.VMEM)
    scratch = [pltpu.VMEM((images, depth), BF16)]
    if early:
        kernel = functools.partial(early_kernel, n)
    else:
        kernel = functools.partial(late_kernel, factor)
        scratch.append(pltpu.VMEM((n, depth // n, depth), F32))
        scratch.append(pltpu.SemaphoreType.DMA((n,)))
    operands = [x_t] + ([] if early else [acc]) + gs
    return pl.pallas_call(
        kernel,
        out_shape=jax.ShapeDtypeStruct((depth, depth), F32),
        in_specs=[vmem] * len(operands),
        out_specs=vmem if early else pl.BlockSpec(memory_space=pl.ANY),
        scratch_shapes=scratch,
        compiler_params=pltpu.CompilerParams(vmem_limit_bytes=24 * 2**20),
        cost_estimate=pl.CostEstimate(
            flops=2 * images * depth * depth,
            bytes_accessed=4 * images * depth + 4 * depth * depth * (2 - early),
            transcendentals=0,
        ),
    )(*operands)


def on_device(x, captions, labels, weight, scale, offset):
    x, captions = x[0], captions[0]
    n_img, depth = x.shape
    n_cap = captions.shape[0]
    nd, nb = lax.axis_size("dp"), lax.axis_size("blk")
    nz = nb // 2
    bits = nd.bit_length() - 1

    def along_z(v, k):
        return lax.ppermute(v, "blk", [(i, i ^ (2 * k)) for i in range(nb)])

    def swap(v):
        return lax.ppermute(v, "blk", [(i, i ^ 1) for i in range(nb)])

    def step_d(v, i):
        perm = []
        for j in range(nd):
            for m in range(nb):
                to = j ^ (1 << ((i + m % 2) % bits))
                perm.append((j * nb + m, to * nb + m))
        return lax.ppermute(v, ("dp", "blk"), perm)

    def over_d(v, first, *before):
        v = [v, first]
        for i in range(1, bits):
            v = after(jnp.concatenate(v), before)
            v = [v, step_d(v, i)]
        return v

    half = nz // 2

    def over_z(vs):
        out = list(vs)
        for k in [*range(half, nz), *range(1, half)]:
            out[k] = along_z(vs[k], k)
        return out

    xs = over_z([x] * nz)
    x_near, x_far = jnp.concatenate(xs[:half]), jnp.concatenate(xs[half:])
    x_near_first = step_d(x_near, 0)
    x_far_first = step_d(x_far, 0)
    embed = dot(joined(xs), weight)
    row = lax.broadcasted_iota(jnp.int32, (16, 128), 0)
    both = jnp.where(row < 8, scale, offset)
    own, u, inv_norm, unit, dlogit, *sent = scores(
        nz,
        both,
        embed,
        [labels, swap(labels)],
        [captions, swap(captions)],
    )
    sent = sent
    back = over_z([own] + sent)[1:]

    x_near = over_d(x_near, after(x_near_first, sent))
    x_far = over_d(x_far, after(x_far_first, sent))
    back = after(back, x_far, x_near)
    ge = embed_grad(own, u, inv_norm, back)
    grad_features = dot(ge, weight, LAST)

    ges = over_z([ge] * nz)
    near, far = ges[1:half], ges[half:]
    g_own = over_d(ge, step_d(ge, 0))
    near = after(jnp.concatenate(near), g_own[0])
    near_first = step_d(near, 0)
    g_near = over_d(near, near_first)
    far = after(jnp.concatenate(far), near)
    far_first = step_d(far, 0)
    dlogit = after(dlogit, far_first)
    adjoint, adjoint_other = caption_sums(both, dlogit, unit)
    adjoint = adjoint + swap(adjoint_other)
    per = nd // 2
    if nd * nb * n_img <= 2048:
        x_all = [joined(x_near), joined(x_far)]
        x_all += [swap(after(v, near)) for v in x_all]
        plan = [[], []]
        n = half * n_img
        for core in range(2):
            near_at = [(2 * core, i * n) for i in range(nd)]
            far_runs = [(2 * core + 1, i * n, n) for i in range(nd)]
            plan[0] += [
                [(i, at, n_img) for i, at in near_at],
                [(i, at + n_img, n - n_img) for i, at in near_at],
                far_runs[:per],
            ]
            plan[1] += [far_runs[per:]]
        x_early, x_late = turned(x_all, plan)
        g_own = jnp.concatenate(g_own)
        own_swapped = swap(g_own)
        g_far = over_d(far, far_first, own_swapped)
        early = [g_own, jnp.concatenate(g_near), g_far[0]]
        others = [own_swapped, swap(early[1]), swap(after(early[2], g_near[1]))]
        acc = weight_sum(None, x_early, early + others, 1.0)
        late = after(g_far[1], acc)
        grad_weight = weight_sum(acc, x_late, [late, swap(late)], 1.0 / nd)
    else:
        g_far = over_d(far, far_first)
        grad_weight = 0.0
        n = half * n_img
        for i in range(2):
            for at in range(per):
                m = n - n_img
                g_part = [
                    g_own[i][at * n_img : (at + 1) * n_img],
                    g_near[i][at * m : (at + 1) * m],
                    g_far[i][at * n : (at + 1) * n],
                ]
                x_part = [v[i][at * n : (at + 1) * n] for v in (x_near, x_far)]
                grad_weight = grad_weight + dot(
                    jnp.concatenate(x_part), jnp.concatenate(g_part), FIRST
                )
        grad_weight = (grad_weight + swap(grad_weight)) / nd
    return (grad_features[None], adjoint[None], grad_weight)


def solution(mesh):
    placed = (P("dp", "blk", None), P("dp", "blk", None), P("dp", "blk"), P(), P(), P())
    return jax.shard_map(
        on_device,
        mesh=mesh,
        in_specs=placed,
        out_specs=(P("dp", "blk", None), P("dp", "blk", None), P()),
        check_vma=False,
    )
```

```python
import functools

import jax
import jax.numpy as jnp
from jax import lax
from jax.experimental import pallas as pl
from jax.experimental.pallas import tpu as pltpu
from jax.sharding import PartitionSpec as P

FIRST = (((0,), (0,)), ((), ()))
LAST = (((1,), (1,)), ((), ()))
F32 = jnp.float32
BF16 = jnp.bfloat16


def dot(a, b, dims=(((1,), (0,)), ((), ()))):
    return lax.dot_general(a, b, dims, preferred_element_type=F32)


def after(v, *others):
    return lax.optimization_barrier((v, others))[0]


def score_kernel(nz, both, embed, *refs):
    scale, offset = both[0:1, 0:1], both[8:9, 0:1]
    labels, captions, refs = refs[:2], refs[2:4], refs[4:]
    own, unit_own, inv_own, unit, dlogit = refs[:5]
    sent, (caps, sems) = refs[5:-2], refs[-2:]
    n_img, n_cap = embed.shape[0] // nz, captions[0].shape[0]
    copies = []
    for i in range(2):
        here = caps.at[i * n_cap : (i + 1) * n_cap, :]
        copies.append(pltpu.make_async_copy(captions[i], here, sems.at[i]))
        copies[-1].start()
    embed = embed[...]
    inv_norm = lax.rsqrt(jnp.sum(embed * embed, axis=1, keepdims=True) + 1e-06)
    unit_f = embed * inv_norm
    unit_own[...] = unit_f[:n_img]
    inv_own[...] = jnp.broadcast_to(inv_norm[:n_img], inv_own.shape)
    u = unit_f.astype(BF16)
    unit[...] = u
    index = lax.axis_index("blk")
    ids = []
    for k in range(nz):
        first = (index ^ (2 * k)) * n_img
        ids.append(first + lax.broadcasted_iota(jnp.int32, (n_img, 1), 0))
    ids = jnp.concatenate(ids)
    labs = jnp.concatenate([v[...] for v in labels], axis=1)
    sign = jnp.where(labs == ids, 1.0, -1.0).astype(F32)
    for copy in copies:
        copy.wait()
    logits = scale * dot(u, caps[...], LAST) + offset
    d = (-sign * jax.nn.sigmoid(-sign * logits)).astype(BF16)
    dlogit[...] = d
    part = scale * dot(d, caps[...])
    own[...] = part[:n_img]
    for k in range(1, nz):
        sent[k - 1][...] = part[k * n_img : (k + 1) * n_img].astype(BF16)


def scores(nz, both, embed, labels, captions):
    images, depth = embed.shape
    n_img, n_cap = images // nz, captions[0].shape[0]
    caps = 2 * n_cap
    vmem = pl.BlockSpec(memory_space=pltpu.VMEM)
    block = jax.ShapeDtypeStruct((n_img, depth), F32)
    outs = [
        block,
        block,
        jax.ShapeDtypeStruct((n_img, 128), F32),
        jax.ShapeDtypeStruct((images, depth), BF16),
        jax.ShapeDtypeStruct((images, caps), BF16),
    ] + [jax.ShapeDtypeStruct((n_img, depth), BF16)] * (nz - 1)
    return pl.pallas_call(
        functools.partial(score_kernel, nz),
        out_shape=outs,
        in_specs=[vmem] * 4
        + [pl.BlockSpec(memory_space=pl.ANY)] * 2,
        out_specs=[vmem] * len(outs),
        scratch_shapes=[pltpu.VMEM((caps, depth), BF16), pltpu.SemaphoreType.DMA((2,))],
        compiler_params=pltpu.CompilerParams(
            vmem_limit_bytes=12 * 2**20 + 24 * images * depth
        ),
        cost_estimate=pl.CostEstimate(
            flops=4 * images * depth * caps,
            bytes_accessed=2 * depth * (caps + 6 * images),
            transcendentals=images * caps,
        ),
    )(both, embed, *labels, *captions)


def join_kernel(*refs):
    at = 0
    for v in refs[:-1]:
        refs[-1][at : at + v.shape[0], :] = v[...]
        at += v.shape[0]


def joined(vs):
    rows = sum(v.shape[0] for v in vs)
    depth = vs[0].shape[1]
    vmem = pl.BlockSpec(memory_space=pltpu.VMEM)
    return pl.pallas_call(
        join_kernel,
        out_shape=jax.ShapeDtypeStruct((rows, depth), vs[0].dtype),
        in_specs=[vmem] * len(vs),
        out_specs=vmem,
        compiler_params=pltpu.CompilerParams(vmem_limit_bytes=12 * 2**20),
        cost_estimate=pl.CostEstimate(
            flops=0, bytes_accessed=4 * rows * depth, transcendentals=0
        ),
    )(*vs)


def caption_kernel(both, dlogit, unit, own, other):
    scale = both[0:1, 0:1]
    n_cap = own.shape[0]
    own[...] = scale * dot(dlogit[:, :n_cap], unit[...], FIRST)
    other[...] = scale * dot(dlogit[:, n_cap:], unit[...], FIRST)


def caption_sums(both, dlogit, unit):
    images, caps = dlogit.shape
    depth = unit.shape[1]
    vmem = pl.BlockSpec(memory_space=pltpu.VMEM)
    return pl.pallas_call(
        caption_kernel,
        out_shape=[jax.ShapeDtypeStruct((caps // 2, depth), F32)] * 2,
        in_specs=[vmem] * 3,
        out_specs=[vmem] * 2,
        compiler_params=pltpu.CompilerParams(
            vmem_limit_bytes=10 * 2**20 + 8 * images * depth
        ),
        cost_estimate=pl.CostEstimate(
            flops=2 * images * caps * depth,
            bytes_accessed=4 * caps * depth + 2 * images * (depth + caps),
            transcendentals=0,
        ),
    )(both, dlogit, unit)


def embed_grad_kernel(own, unit, inv_norm, *refs):
    back, out = refs[:-1], refs[-1]
    total = own[...]
    for v in back:
        total = total + v[...].astype(F32)
    u = unit[...]
    radial = jnp.sum(u * total, axis=1, keepdims=True)
    out[...] = ((total - u * radial) * inv_norm[:, :1]).astype(BF16)


def embed_grad(own, unit, inv_norm, back):
    vmem = pl.BlockSpec(memory_space=pltpu.VMEM)
    return pl.pallas_call(
        embed_grad_kernel,
        out_shape=jax.ShapeDtypeStruct(own.shape, BF16),
        in_specs=[vmem] * (3 + len(back)),
        out_specs=vmem,
        compiler_params=pltpu.CompilerParams(vmem_limit_bytes=8 * 2**20),
        cost_estimate=pl.CostEstimate(
            flops=8 * own.size, bytes_accessed=12 * own.size, transcendentals=0
        ),
    )(own, unit, inv_norm, *back)


def turn_kernel(plan, *refs):
    ins, outs = refs[: -len(plan)], refs[-len(plan) :]
    for out, pieces in zip(outs, plan):
        col = 0
        for runs in pieces:
            rows = [ins[i][at : at + size, :] for i, at, size in runs]
            rows = jnp.concatenate(rows)
            out[:, col : col + rows.shape[0]] = rows.T
            col += rows.shape[0]


def turned(xs, plan):
    depth = xs[0].shape[1]
    images = [sum(size for runs in pieces for _, _, size in runs) for pieces in plan]
    return pl.pallas_call(
        functools.partial(turn_kernel, plan),
        out_shape=[jax.ShapeDtypeStruct((depth, n), BF16) for n in images],
        in_specs=[pl.BlockSpec(memory_space=pltpu.VMEM)] * len(xs),
        out_specs=[pl.BlockSpec(memory_space=pltpu.VMEM)] * len(plan),
        compiler_params=pltpu.CompilerParams(vmem_limit_bytes=16 * 2**20),
        cost_estimate=pl.CostEstimate(
            flops=0, bytes_accessed=4 * sum(images) * depth, transcendentals=0
        ),
    )(*xs)


def stack(stacked, gs):
    at = 0
    for g in gs:
        stacked[at : at + g.shape[0], :] = g[...]
        at += g.shape[0]


def early_kernel(n, x_t, *refs):
    gs, (out, stacked) = refs[:-2], refs[-2:]
    stack(stacked, gs)
    rows = out.shape[0] // n
    for i in range(n):
        here = slice(i * rows, (i + 1) * rows)
        out[here, :] = dot(x_t[here, :], stacked[...])


def late_kernel(factor, x_t, acc, *refs):
    gs, (out, stacked, tiles, sems) = refs[:-4], refs[-4:]
    stack(stacked, gs)
    n, rows = tiles.shape[:2]
    copies = []
    for i in range(n):
        here = slice(i * rows, (i + 1) * rows)
        tiles[i] = (acc[here, :] + dot(x_t[here, :], stacked[...])) * factor
        copies.append(pltpu.make_async_copy(tiles.at[i], out.at[here, :], sems.at[i]))
        copies[-1].start()
    for copy in copies:
        copy.wait()


def weight_sum(acc, x_t, gs, factor):
    depth, images = x_t.shape
    n = 3
    early = acc is None
    vmem = pl.BlockSpec(memory_space=pltpu.VMEM)
    scratch = [pltpu.VMEM((images, depth), BF16)]
    if early:
        kernel = functools.partial(early_kernel, n)
    else:
        kernel = functools.partial(late_kernel, factor)
        scratch.append(pltpu.VMEM((n, depth // n, depth), F32))
        scratch.append(pltpu.SemaphoreType.DMA((n,)))
    operands = [x_t] + ([] if early else [acc]) + gs
    return pl.pallas_call(
        kernel,
        out_shape=jax.ShapeDtypeStruct((depth, depth), F32),
        in_specs=[vmem] * len(operands),
        out_specs=vmem if early else pl.BlockSpec(memory_space=pl.ANY),
        scratch_shapes=scratch,
        compiler_params=pltpu.CompilerParams(vmem_limit_bytes=24 * 2**20),
        cost_estimate=pl.CostEstimate(
            flops=2 * images * depth * depth,
            bytes_accessed=4 * images * depth + 4 * depth * depth * (2 - early),
            transcendentals=0,
        ),
    )(*operands)


def on_device(x, captions, labels, weight, scale, offset):
    x, captions = x[0], captions[0]
    n_img, depth = x.shape
    n_cap = captions.shape[0]
    nd, nb = lax.axis_size("dp"), lax.axis_size("blk")
    nz = nb // 2
    bits = nd.bit_length() - 1

    def along_z(v, k):
        return lax.ppermute(v, "blk", [(i, i ^ (2 * k)) for i in range(nb)])

    def swap(v):
        return lax.ppermute(v, "blk", [(i, i ^ 1) for i in range(nb)])

    def step_d(v, i):
        perm = []
        for j in range(nd):
            for m in range(nb):
                to = j ^ (1 << ((i + m % 2) % bits))
                perm.append((j * nb + m, to * nb + m))
        return lax.ppermute(v, ("dp", "blk"), perm)

    def over_d(v, first, *before):
        v = [v, first]
        for i in range(1, bits):
            v = after(jnp.concatenate(v), before)
            v = [v, step_d(v, i)]
        return v

    half = nz // 2

    def over_z(vs):
        out = list(vs)
        for k in [*range(half, nz), *range(1, half)]:
            out[k] = along_z(vs[k], k)
        return out

    xs = over_z([x] * nz)
    x_near, x_far = jnp.concatenate(xs[:half]), jnp.concatenate(xs[half:])
    x_near_first = step_d(x_near, 0)
    x_far_first = step_d(x_far, 0)
    embed = dot(joined(xs), weight)
    row = lax.broadcasted_iota(jnp.int32, (16, 128), 0)
    both = jnp.where(row < 8, scale, offset)
    own, u, inv_norm, unit, dlogit, *sent = scores(
        nz,
        both,
        embed,
        [labels, swap(labels)],
        [captions, swap(captions)],
    )
    sent = sent
    back = over_z([own] + sent)[1:]

    x_near = over_d(x_near, after(x_near_first, back))
    x_far = over_d(x_far, after(x_far_first, sent))
    back = after(back, x_far)
    ge = embed_grad(own, u, inv_norm, back)
    grad_features = dot(ge, weight, LAST)

    ges = over_z([ge] * nz)
    near, far = ges[1:half], ges[half:]
    g_own = over_d(ge, step_d(ge, 0))
    near = after(jnp.concatenate(near), g_own[0])
    near_first = step_d(near, 0)
    g_near = over_d(near, near_first)
    far = after(jnp.concatenate(far), near)
    far_first = step_d(far, 0)
    dlogit = after(dlogit, far_first)
    adjoint, adjoint_other = caption_sums(both, dlogit, unit)
    adjoint = adjoint + swap(adjoint_other)
    per = nd // 2
    if nd * nb * n_img <= 2048:
        x_all = [joined(x_near), joined(x_far)]
        x_all += [swap(after(v, near)) for v in x_all]
        plan = [[], []]
        n = half * n_img
        for core in range(2):
            near_at = [(2 * core, i * n) for i in range(nd)]
            far_runs = [(2 * core + 1, i * n, n) for i in range(nd)]
            plan[0] += [
                [(i, at, n_img) for i, at in near_at],
                [(i, at + n_img, n - n_img) for i, at in near_at],
                far_runs[:per],
            ]
            plan[1] += [far_runs[per:]]
        x_early, x_late = turned(x_all, plan)
        g_own = jnp.concatenate(g_own)
        own_swapped = swap(g_own)
        g_far = over_d(far, far_first, own_swapped)
        early = [g_own, jnp.concatenate(g_near), g_far[0]]
        others = [own_swapped, swap(early[1]), swap(after(early[2], g_near[1]))]
        acc = weight_sum(None, x_early, early + others, 1.0)
        late = after(g_far[1], acc)
        grad_weight = weight_sum(acc, x_late, [late, swap(late)], 1.0 / nd)
    else:
        g_far = over_d(far, far_first)
        grad_weight = 0.0
        n = half * n_img
        for i in range(2):
            for at in range(per):
                m = n - n_img
                g_part = [
                    g_own[i][at * n_img : (at + 1) * n_img],
                    g_near[i][at * m : (at + 1) * m],
                    g_far[i][at * n : (at + 1) * n],
                ]
                x_part = [v[i][at * n : (at + 1) * n] for v in (x_near, x_far)]
                grad_weight = grad_weight + dot(
                    jnp.concatenate(x_part), jnp.concatenate(g_part), FIRST
                )
        grad_weight = (grad_weight + swap(grad_weight)) / nd
    return (grad_features[None], adjoint[None], grad_weight)


def solution(mesh):
    placed = (P("dp", "blk", None), P("dp", "blk", None), P("dp", "blk"), P(), P(), P())
    return jax.shard_map(
        on_device,
        mesh=mesh,
        in_specs=placed,
        out_specs=(P("dp", "blk", None), P("dp", "blk", None), P()),
        check_vma=False,
    )
```

```python
import functools

import jax
import jax.numpy as jnp
from jax import lax
from jax.experimental import pallas as pl
from jax.experimental.pallas import tpu as pltpu
from jax.sharding import PartitionSpec as P

FIRST = (((0,), (0,)), ((), ()))
LAST = (((1,), (1,)), ((), ()))
F32 = jnp.float32
BF16 = jnp.bfloat16


def dot(a, b, dims=(((1,), (0,)), ((), ()))):
    return lax.dot_general(a, b, dims, preferred_element_type=F32)


def after(v, *others):
    return lax.optimization_barrier((v, others))[0]


def score_kernel(nz, both, embed, *refs):
    scale, offset = both[0:1, 0:1], both[8:9, 0:1]
    labels, captions, refs = refs[:2], refs[2:4], refs[4:]
    own, unit_own, inv_own, unit, dlogit = refs[:5]
    sent, (caps, sems) = refs[5:-2], refs[-2:]
    n_img, n_cap = embed.shape[0] // nz, captions[0].shape[0]
    copies = []
    for i in range(2):
        here = caps.at[i * n_cap : (i + 1) * n_cap, :]
        copies.append(pltpu.make_async_copy(captions[i], here, sems.at[i]))
        copies[-1].start()
    embed = embed[...]
    inv_norm = lax.rsqrt(jnp.sum(embed * embed, axis=1, keepdims=True) + 1e-06)
    unit_f = embed * inv_norm
    unit_own[...] = unit_f[:n_img]
    inv_own[...] = jnp.broadcast_to(inv_norm[:n_img], inv_own.shape)
    u = unit_f.astype(BF16)
    unit[...] = u
    index = lax.axis_index("blk")
    ids = []
    for k in range(nz):
        first = (index ^ (2 * k)) * n_img
        ids.append(first + lax.broadcasted_iota(jnp.int32, (n_img, 1), 0))
    ids = jnp.concatenate(ids)
    labs = jnp.concatenate([v[...] for v in labels], axis=1)
    sign = jnp.where(labs == ids, 1.0, -1.0).astype(F32)
    for copy in copies:
        copy.wait()
    logits = scale * dot(u, caps[...], LAST) + offset
    d = (-sign * jax.nn.sigmoid(-sign * logits)).astype(BF16)
    dlogit[...] = d
    part = scale * dot(d, caps[...])
    own[...] = part[:n_img]
    for k in range(1, nz):
        sent[k - 1][...] = part[k * n_img : (k + 1) * n_img].astype(BF16)


def scores(nz, both, embed, labels, captions):
    images, depth = embed.shape
    n_img, n_cap = images // nz, captions[0].shape[0]
    caps = 2 * n_cap
    vmem = pl.BlockSpec(memory_space=pltpu.VMEM)
    block = jax.ShapeDtypeStruct((n_img, depth), F32)
    outs = [
        block,
        block,
        jax.ShapeDtypeStruct((n_img, 128), F32),
        jax.ShapeDtypeStruct((images, depth), BF16),
        jax.ShapeDtypeStruct((images, caps), BF16),
    ] + [jax.ShapeDtypeStruct((n_img, depth), BF16)] * (nz - 1)
    return pl.pallas_call(
        functools.partial(score_kernel, nz),
        out_shape=outs,
        in_specs=[vmem] * 4
        + [pl.BlockSpec(memory_space=pl.ANY)] * 2,
        out_specs=[vmem] * len(outs),
        scratch_shapes=[pltpu.VMEM((caps, depth), BF16), pltpu.SemaphoreType.DMA((2,))],
        compiler_params=pltpu.CompilerParams(
            vmem_limit_bytes=12 * 2**20 + 24 * images * depth
        ),
        cost_estimate=pl.CostEstimate(
            flops=4 * images * depth * caps,
            bytes_accessed=2 * depth * (caps + 6 * images),
            transcendentals=images * caps,
        ),
    )(both, embed, *labels, *captions)


def join_kernel(*refs):
    at = 0
    for v in refs[:-1]:
        refs[-1][at : at + v.shape[0], :] = v[...]
        at += v.shape[0]


def joined(vs):
    rows = sum(v.shape[0] for v in vs)
    depth = vs[0].shape[1]
    vmem = pl.BlockSpec(memory_space=pltpu.VMEM)
    return pl.pallas_call(
        join_kernel,
        out_shape=jax.ShapeDtypeStruct((rows, depth), vs[0].dtype),
        in_specs=[vmem] * len(vs),
        out_specs=vmem,
        compiler_params=pltpu.CompilerParams(vmem_limit_bytes=12 * 2**20),
        cost_estimate=pl.CostEstimate(
            flops=0, bytes_accessed=4 * rows * depth, transcendentals=0
        ),
    )(*vs)


def caption_kernel(both, dlogit, unit, own, other):
    scale = both[0:1, 0:1]
    n_cap = own.shape[0]
    own[...] = scale * dot(dlogit[:, :n_cap], unit[...], FIRST)
    other[...] = scale * dot(dlogit[:, n_cap:], unit[...], FIRST)


def caption_sums(both, dlogit, unit):
    images, caps = dlogit.shape
    depth = unit.shape[1]
    vmem = pl.BlockSpec(memory_space=pltpu.VMEM)
    return pl.pallas_call(
        caption_kernel,
        out_shape=[jax.ShapeDtypeStruct((caps // 2, depth), F32)] * 2,
        in_specs=[vmem] * 3,
        out_specs=[vmem] * 2,
        compiler_params=pltpu.CompilerParams(
            vmem_limit_bytes=10 * 2**20 + 8 * images * depth
        ),
        cost_estimate=pl.CostEstimate(
            flops=2 * images * caps * depth,
            bytes_accessed=4 * caps * depth + 2 * images * (depth + caps),
            transcendentals=0,
        ),
    )(both, dlogit, unit)


def embed_grad_kernel(own, unit, inv_norm, *refs):
    back, out = refs[:-1], refs[-1]
    total = own[...]
    for v in back:
        total = total + v[...].astype(F32)
    u = unit[...]
    radial = jnp.sum(u * total, axis=1, keepdims=True)
    out[...] = ((total - u * radial) * inv_norm[:, :1]).astype(BF16)


def embed_grad(own, unit, inv_norm, back):
    vmem = pl.BlockSpec(memory_space=pltpu.VMEM)
    return pl.pallas_call(
        embed_grad_kernel,
        out_shape=jax.ShapeDtypeStruct(own.shape, BF16),
        in_specs=[vmem] * (3 + len(back)),
        out_specs=vmem,
        compiler_params=pltpu.CompilerParams(vmem_limit_bytes=8 * 2**20),
        cost_estimate=pl.CostEstimate(
            flops=8 * own.size, bytes_accessed=12 * own.size, transcendentals=0
        ),
    )(own, unit, inv_norm, *back)


def turn_kernel(plan, *refs):
    ins, outs = refs[: -len(plan)], refs[-len(plan) :]
    for out, pieces in zip(outs, plan):
        col = 0
        for runs in pieces:
            rows = [ins[i][at : at + size, :] for i, at, size in runs]
            rows = jnp.concatenate(rows)
            out[:, col : col + rows.shape[0]] = rows.T
            col += rows.shape[0]


def turned(xs, plan):
    depth = xs[0].shape[1]
    images = [sum(size for runs in pieces for _, _, size in runs) for pieces in plan]
    return pl.pallas_call(
        functools.partial(turn_kernel, plan),
        out_shape=[jax.ShapeDtypeStruct((depth, n), BF16) for n in images],
        in_specs=[pl.BlockSpec(memory_space=pltpu.VMEM)] * len(xs),
        out_specs=[pl.BlockSpec(memory_space=pltpu.VMEM)] * len(plan),
        compiler_params=pltpu.CompilerParams(vmem_limit_bytes=16 * 2**20),
        cost_estimate=pl.CostEstimate(
            flops=0, bytes_accessed=4 * sum(images) * depth, transcendentals=0
        ),
    )(*xs)


def stack(stacked, gs):
    at = 0
    for g in gs:
        stacked[at : at + g.shape[0], :] = g[...]
        at += g.shape[0]


def early_kernel(n, x_t, *refs):
    gs, (out, stacked) = refs[:-2], refs[-2:]
    stack(stacked, gs)
    rows = out.shape[0] // n
    for i in range(n):
        here = slice(i * rows, (i + 1) * rows)
        out[here, :] = dot(x_t[here, :], stacked[...])


def late_kernel(factor, x_t, acc, *refs):
    gs, (out, stacked, tiles, sems) = refs[:-4], refs[-4:]
    stack(stacked, gs)
    n, rows = tiles.shape[:2]
    copies = []
    for i in range(n):
        here = slice(i * rows, (i + 1) * rows)
        tiles[i] = (acc[here, :] + dot(x_t[here, :], stacked[...])) * factor
        copies.append(pltpu.make_async_copy(tiles.at[i], out.at[here, :], sems.at[i]))
        copies[-1].start()
    for copy in copies:
        copy.wait()


def weight_sum(acc, x_t, gs, factor):
    depth, images = x_t.shape
    n = 3
    early = acc is None
    vmem = pl.BlockSpec(memory_space=pltpu.VMEM)
    scratch = [pltpu.VMEM((images, depth), BF16)]
    if early:
        kernel = functools.partial(early_kernel, n)
    else:
        kernel = functools.partial(late_kernel, factor)
        scratch.append(pltpu.VMEM((n, depth // n, depth), F32))
        scratch.append(pltpu.SemaphoreType.DMA((n,)))
    operands = [x_t] + ([] if early else [acc]) + gs
    return pl.pallas_call(
        kernel,
        out_shape=jax.ShapeDtypeStruct((depth, depth), F32),
        in_specs=[vmem] * len(operands),
        out_specs=vmem if early else pl.BlockSpec(memory_space=pl.ANY),
        scratch_shapes=scratch,
        compiler_params=pltpu.CompilerParams(vmem_limit_bytes=24 * 2**20),
        cost_estimate=pl.CostEstimate(
            flops=2 * images * depth * depth,
            bytes_accessed=4 * images * depth + 4 * depth * depth * (2 - early),
            transcendentals=0,
        ),
    )(*operands)


def on_device(x, captions, labels, weight, scale, offset):
    x, captions = x[0], captions[0]
    n_img, depth = x.shape
    n_cap = captions.shape[0]
    nd, nb = lax.axis_size("dp"), lax.axis_size("blk")
    nz = nb // 2
    bits = nd.bit_length() - 1

    def along_z(v, k):
        return lax.ppermute(v, "blk", [(i, i ^ (2 * k)) for i in range(nb)])

    def swap(v):
        return lax.ppermute(v, "blk", [(i, i ^ 1) for i in range(nb)])

    def step_d(v, i):
        perm = []
        for j in range(nd):
            for m in range(nb):
                to = j ^ (1 << ((i + m % 2) % bits))
                perm.append((j * nb + m, to * nb + m))
        return lax.ppermute(v, ("dp", "blk"), perm)

    def over_d(v, first, *before):
        v = [v, first]
        for i in range(1, bits):
            v = after(jnp.concatenate(v), before)
            v = [v, step_d(v, i)]
        return v

    half = nz // 2

    def over_z(vs):
        out = list(vs)
        for k in [*range(half, nz), *range(1, half)]:
            out[k] = along_z(vs[k], k)
        return out

    xs = over_z([x] * nz)
    x_near, x_far = jnp.concatenate(xs[:half]), jnp.concatenate(xs[half:])
    x_near_first = step_d(x_near, 0)
    x_far_first = step_d(x_far, 0)
    embed = dot(joined(xs), weight)
    row = lax.broadcasted_iota(jnp.int32, (16, 128), 0)
    both = jnp.where(row < 8, scale, offset)
    own, u, inv_norm, unit, dlogit, *sent = scores(
        nz,
        both,
        embed,
        [labels, swap(labels)],
        [captions, swap(captions)],
    )
    sent = sent
    back = over_z([own] + sent)[1:]

    x_near = over_d(x_near, after(x_near_first, back))
    x_far = over_d(x_far, after(x_far_first, sent))
    back = after(back[::-1], x_far)
    ge = embed_grad(own, u, inv_norm, back)
    grad_features = dot(ge, weight, LAST)

    ges = over_z([ge] * nz)
    near, far = ges[1:half], ges[half:]
    g_own = over_d(ge, step_d(ge, 0))
    near = after(jnp.concatenate(near), g_own[0])
    near_first = step_d(near, 0)
    g_near = over_d(near, near_first)
    far = after(jnp.concatenate(far), near)
    far_first = step_d(far, 0)
    dlogit = after(dlogit, far_first)
    adjoint, adjoint_other = caption_sums(both, dlogit, unit)
    adjoint = adjoint + swap(adjoint_other)
    per = nd // 2
    if nd * nb * n_img <= 2048:
        x_all = [joined(x_near), joined(x_far)]
        x_all += [swap(after(v, near)) for v in x_all]
        plan = [[], []]
        n = half * n_img
        for core in range(2):
            near_at = [(2 * core, i * n) for i in range(nd)]
            far_runs = [(2 * core + 1, i * n, n) for i in range(nd)]
            plan[0] += [
                [(i, at, n_img) for i, at in near_at],
                [(i, at + n_img, n - n_img) for i, at in near_at],
                far_runs[:per],
            ]
            plan[1] += [far_runs[per:]]
        x_early, x_late = turned(x_all, plan)
        g_own = jnp.concatenate(g_own)
        own_swapped = swap(g_own)
        g_far = over_d(far, far_first, own_swapped)
        early = [g_own, jnp.concatenate(g_near), g_far[0]]
        others = [own_swapped, swap(early[1]), swap(after(early[2], g_near[1]))]
        acc = weight_sum(None, x_early, early + others, 1.0)
        late = after(g_far[1], acc)
        grad_weight = weight_sum(acc, x_late, [late, swap(late)], 1.0 / nd)
    else:
        g_far = over_d(far, far_first)
        grad_weight = 0.0
        n = half * n_img
        for i in range(2):
            for at in range(per):
                m = n - n_img
                g_part = [
                    g_own[i][at * n_img : (at + 1) * n_img],
                    g_near[i][at * m : (at + 1) * m],
                    g_far[i][at * n : (at + 1) * n],
                ]
                x_part = [v[i][at * n : (at + 1) * n] for v in (x_near, x_far)]
                grad_weight = grad_weight + dot(
                    jnp.concatenate(x_part), jnp.concatenate(g_part), FIRST
                )
        grad_weight = (grad_weight + swap(grad_weight)) / nd
    return (grad_features[None], adjoint[None], grad_weight)


def solution(mesh):
    placed = (P("dp", "blk", None), P("dp", "blk", None), P("dp", "blk"), P(), P(), P())
    return jax.shard_map(
        on_device,
        mesh=mesh,
        in_specs=placed,
        out_specs=(P("dp", "blk", None), P("dp", "blk", None), P()),
        check_vma=False,
    )
```

```python
import functools

import jax
import jax.numpy as jnp
from jax import lax
from jax.experimental import pallas as pl
from jax.experimental.pallas import tpu as pltpu
from jax.sharding import PartitionSpec as P

FIRST = (((0,), (0,)), ((), ()))
LAST = (((1,), (1,)), ((), ()))
F32 = jnp.float32
BF16 = jnp.bfloat16


def dot(a, b, dims=(((1,), (0,)), ((), ()))):
    return lax.dot_general(a, b, dims, preferred_element_type=F32)


def after(v, *others):
    return lax.optimization_barrier((v, others))[0]


def score_kernel(nz, both, embed, *refs):
    scale, offset = both[0:1, 0:1], both[8:9, 0:1]
    labels, captions, refs = refs[:2], refs[2:4], refs[4:]
    own, unit_own, inv_own, unit, dlogit = refs[:5]
    sent, (caps, sems) = refs[5:-2], refs[-2:]
    n_img, n_cap = embed.shape[0] // nz, captions[0].shape[0]
    copies = []
    for i in range(2):
        here = caps.at[i * n_cap : (i + 1) * n_cap, :]
        copies.append(pltpu.make_async_copy(captions[i], here, sems.at[i]))
        copies[-1].start()
    embed = embed[...]
    inv_norm = lax.rsqrt(jnp.sum(embed * embed, axis=1, keepdims=True) + 1e-06)
    unit_f = embed * inv_norm
    unit_own[...] = unit_f[:n_img]
    inv_own[...] = jnp.broadcast_to(inv_norm[:n_img], inv_own.shape)
    u = unit_f.astype(BF16)
    unit[...] = u
    index = lax.axis_index("blk")
    ids = []
    for k in range(nz):
        first = (index ^ (2 * k)) * n_img
        ids.append(first + lax.broadcasted_iota(jnp.int32, (n_img, 1), 0))
    ids = jnp.concatenate(ids)
    labs = jnp.concatenate([v[...] for v in labels], axis=1)
    sign = jnp.where(labs == ids, 1.0, -1.0).astype(F32)
    for copy in copies:
        copy.wait()
    logits = scale * dot(u, caps[...], LAST) + offset
    d = (-sign * jax.nn.sigmoid(-sign * logits)).astype(BF16)
    dlogit[...] = d
    part = scale * dot(d, caps[...])
    own[...] = part[:n_img]
    for k in range(1, nz):
        sent[k - 1][...] = part[k * n_img : (k + 1) * n_img].astype(BF16)


def scores(nz, both, embed, labels, captions):
    images, depth = embed.shape
    n_img, n_cap = images // nz, captions[0].shape[0]
    caps = 2 * n_cap
    vmem = pl.BlockSpec(memory_space=pltpu.VMEM)
    block = jax.ShapeDtypeStruct((n_img, depth), F32)
    outs = [
        block,
        block,
        jax.ShapeDtypeStruct((n_img, 128), F32),
        jax.ShapeDtypeStruct((images, depth), BF16),
        jax.ShapeDtypeStruct((images, caps), BF16),
    ] + [jax.ShapeDtypeStruct((n_img, depth), BF16)] * (nz - 1)
    return pl.pallas_call(
        functools.partial(score_kernel, nz),
        out_shape=outs,
        in_specs=[vmem] * 4
        + [pl.BlockSpec(memory_space=pl.ANY)] * 2,
        out_specs=[vmem] * len(outs),
        scratch_shapes=[pltpu.VMEM((caps, depth), BF16), pltpu.SemaphoreType.DMA((2,))],
        compiler_params=pltpu.CompilerParams(
            vmem_limit_bytes=12 * 2**20 + 24 * images * depth
        ),
        cost_estimate=pl.CostEstimate(
            flops=4 * images * depth * caps,
            bytes_accessed=2 * depth * (caps + 6 * images),
            transcendentals=images * caps,
        ),
    )(both, embed, *labels, *captions)


def join_kernel(*refs):
    at = 0
    for v in refs[:-1]:
        refs[-1][at : at + v.shape[0], :] = v[...]
        at += v.shape[0]


def joined(vs):
    rows = sum(v.shape[0] for v in vs)
    depth = vs[0].shape[1]
    vmem = pl.BlockSpec(memory_space=pltpu.VMEM)
    return pl.pallas_call(
        join_kernel,
        out_shape=jax.ShapeDtypeStruct((rows, depth), vs[0].dtype),
        in_specs=[vmem] * len(vs),
        out_specs=vmem,
        compiler_params=pltpu.CompilerParams(vmem_limit_bytes=12 * 2**20),
        cost_estimate=pl.CostEstimate(
            flops=0, bytes_accessed=4 * rows * depth, transcendentals=0
        ),
    )(*vs)


def caption_kernel(both, dlogit, unit, own, other):
    scale = both[0:1, 0:1]
    n_cap = own.shape[0]
    own[...] = scale * dot(dlogit[:, :n_cap], unit[...], FIRST)
    other[...] = scale * dot(dlogit[:, n_cap:], unit[...], FIRST)


def caption_sums(both, dlogit, unit):
    images, caps = dlogit.shape
    depth = unit.shape[1]
    vmem = pl.BlockSpec(memory_space=pltpu.VMEM)
    return pl.pallas_call(
        caption_kernel,
        out_shape=[jax.ShapeDtypeStruct((caps // 2, depth), F32)] * 2,
        in_specs=[vmem] * 3,
        out_specs=[vmem] * 2,
        compiler_params=pltpu.CompilerParams(
            vmem_limit_bytes=10 * 2**20 + 8 * images * depth
        ),
        cost_estimate=pl.CostEstimate(
            flops=2 * images * caps * depth,
            bytes_accessed=4 * caps * depth + 2 * images * (depth + caps),
            transcendentals=0,
        ),
    )(both, dlogit, unit)


def embed_grad_kernel(own, unit, inv_norm, *refs):
    back, out = refs[:-1], refs[-1]
    total = own[...]
    for v in back:
        total = total + v[...].astype(F32)
    u = unit[...]
    radial = jnp.sum(u * total, axis=1, keepdims=True)
    out[...] = ((total - u * radial) * inv_norm[:, :1]).astype(BF16)


def embed_grad(own, unit, inv_norm, back):
    vmem = pl.BlockSpec(memory_space=pltpu.VMEM)
    return pl.pallas_call(
        embed_grad_kernel,
        out_shape=jax.ShapeDtypeStruct(own.shape, BF16),
        in_specs=[vmem] * (3 + len(back)),
        out_specs=vmem,
        compiler_params=pltpu.CompilerParams(vmem_limit_bytes=8 * 2**20),
        cost_estimate=pl.CostEstimate(
            flops=8 * own.size, bytes_accessed=12 * own.size, transcendentals=0
        ),
    )(own, unit, inv_norm, *back)


def turn_kernel(plan, *refs):
    ins, outs = refs[: -len(plan)], refs[-len(plan) :]
    for out, pieces in zip(outs, plan):
        col = 0
        for runs in pieces:
            rows = [ins[i][at : at + size, :] for i, at, size in runs]
            rows = jnp.concatenate(rows)
            out[:, col : col + rows.shape[0]] = rows.T
            col += rows.shape[0]


def turned(xs, plan):
    depth = xs[0].shape[1]
    images = [sum(size for runs in pieces for _, _, size in runs) for pieces in plan]
    return pl.pallas_call(
        functools.partial(turn_kernel, plan),
        out_shape=[jax.ShapeDtypeStruct((depth, n), BF16) for n in images],
        in_specs=[pl.BlockSpec(memory_space=pltpu.VMEM)] * len(xs),
        out_specs=[pl.BlockSpec(memory_space=pltpu.VMEM)] * len(plan),
        compiler_params=pltpu.CompilerParams(vmem_limit_bytes=16 * 2**20),
        cost_estimate=pl.CostEstimate(
            flops=0, bytes_accessed=4 * sum(images) * depth, transcendentals=0
        ),
    )(*xs)


def stack(stacked, gs):
    at = 0
    for g in gs:
        stacked[at : at + g.shape[0], :] = g[...]
        at += g.shape[0]


def early_kernel(n, x_t, *refs):
    gs, (out, stacked) = refs[:-2], refs[-2:]
    stack(stacked, gs)
    rows = out.shape[0] // n
    for i in range(n):
        here = slice(i * rows, (i + 1) * rows)
        out[here, :] = dot(x_t[here, :], stacked[...])


def late_kernel(factor, x_t, acc, *refs):
    gs, (out, stacked, tiles, sems) = refs[:-4], refs[-4:]
    stack(stacked, gs)
    n, rows = tiles.shape[:2]
    copies = []
    for i in range(n):
        here = slice(i * rows, (i + 1) * rows)
        tiles[i] = (acc[here, :] + dot(x_t[here, :], stacked[...])) * factor
        copies.append(pltpu.make_async_copy(tiles.at[i], out.at[here, :], sems.at[i]))
        copies[-1].start()
    for copy in copies:
        copy.wait()


def weight_sum(acc, x_t, gs, factor):
    depth, images = x_t.shape
    n = 3
    early = acc is None
    vmem = pl.BlockSpec(memory_space=pltpu.VMEM)
    scratch = [pltpu.VMEM((images, depth), BF16)]
    if early:
        kernel = functools.partial(early_kernel, n)
    else:
        kernel = functools.partial(late_kernel, factor)
        scratch.append(pltpu.VMEM((n, depth // n, depth), F32))
        scratch.append(pltpu.SemaphoreType.DMA((n,)))
    operands = [x_t] + ([] if early else [acc]) + gs
    return pl.pallas_call(
        kernel,
        out_shape=jax.ShapeDtypeStruct((depth, depth), F32),
        in_specs=[vmem] * len(operands),
        out_specs=vmem if early else pl.BlockSpec(memory_space=pl.ANY),
        scratch_shapes=scratch,
        compiler_params=pltpu.CompilerParams(vmem_limit_bytes=24 * 2**20),
        cost_estimate=pl.CostEstimate(
            flops=2 * images * depth * depth,
            bytes_accessed=4 * images * depth + 4 * depth * depth * (2 - early),
            transcendentals=0,
        ),
    )(*operands)


def on_device(x, captions, labels, weight, scale, offset):
    x, captions = x[0], captions[0]
    n_img, depth = x.shape
    n_cap = captions.shape[0]
    nd, nb = lax.axis_size("dp"), lax.axis_size("blk")
    nz = nb // 2
    bits = nd.bit_length() - 1

    def along_z(v, k):
        return lax.ppermute(v, "blk", [(i, i ^ (2 * k)) for i in range(nb)])

    def swap(v):
        return lax.ppermute(v, "blk", [(i, i ^ 1) for i in range(nb)])

    def step_d(v, i):
        perm = []
        for j in range(nd):
            for m in range(nb):
                to = j ^ (1 << ((i + m % 2) % bits))
                perm.append((j * nb + m, to * nb + m))
        return lax.ppermute(v, ("dp", "blk"), perm)

    def over_d(v, first, *before):
        v = [v, first]
        for i in range(1, bits):
            v = after(jnp.concatenate(v), before)
            v = [v, step_d(v, i)]
        return v

    half = nz // 2

    def over_z(vs):
        out = list(vs)
        for k in [*range(half, nz), *range(1, half)]:
            out[k] = along_z(vs[k], k)
        return out

    xs = over_z([x] * nz)
    x_near, x_far = jnp.concatenate(xs[:half]), jnp.concatenate(xs[half:])
    x_near_first = step_d(x_near, 0)
    x_far_first = step_d(x_far, 0)
    embed = dot(joined(xs), weight)
    row = lax.broadcasted_iota(jnp.int32, (16, 128), 0)
    both = jnp.where(row < 8, scale, offset)
    own, u, inv_norm, unit, dlogit, *sent = scores(
        nz,
        both,
        embed,
        [labels, swap(labels)],
        [captions, swap(captions)],
    )
    sent = sent
    back = over_z([own] + sent)[1:]

    x_near = over_d(x_near, after(x_near_first, back))
    x_far = over_d(x_far, after(x_far_first, sent))
    back = after(back[::-1], x_far)
    ge = embed_grad(own, u, inv_norm, back)
    grad_features = dot(ge, weight, LAST)

    ges = over_z([ge] * nz)
    near, far = ges[1:half], ges[half:]
    g_own = over_d(ge, step_d(ge, 0))
    near = after(jnp.concatenate(near), g_own[0])
    near_first = step_d(near, 0)
    g_near = over_d(near, near_first)
    far = after(jnp.concatenate(far), near)
    far_first = step_d(far, 0)
    dlogit = after(dlogit, near)
    adjoint, adjoint_other = caption_sums(both, dlogit, unit)
    adjoint = adjoint + swap(adjoint_other)
    per = nd // 2
    if nd * nb * n_img <= 2048:
        x_all = [joined(x_near), joined(x_far)]
        x_all += [swap(after(v, near)) for v in x_all]
        plan = [[], []]
        n = half * n_img
        for core in range(2):
            near_at = [(2 * core, i * n) for i in range(nd)]
            far_runs = [(2 * core + 1, i * n, n) for i in range(nd)]
            plan[0] += [
                [(i, at, n_img) for i, at in near_at],
                [(i, at + n_img, n - n_img) for i, at in near_at],
                far_runs[:per],
            ]
            plan[1] += [far_runs[per:]]
        x_early, x_late = turned(x_all, plan)
        g_own = jnp.concatenate(g_own)
        own_swapped = swap(g_own)
        g_far = over_d(far, far_first, own_swapped)
        early = [g_own, jnp.concatenate(g_near), g_far[0]]
        others = [own_swapped, swap(early[1]), swap(after(early[2], g_near[1]))]
        acc = weight_sum(None, x_early, early + others, 1.0)
        late = after(g_far[1], acc)
        grad_weight = weight_sum(acc, x_late, [late, swap(late)], 1.0 / nd)
    else:
        g_far = over_d(far, far_first)
        grad_weight = 0.0
        n = half * n_img
        for i in range(2):
            for at in range(per):
                m = n - n_img
                g_part = [
                    g_own[i][at * n_img : (at + 1) * n_img],
                    g_near[i][at * m : (at + 1) * m],
                    g_far[i][at * n : (at + 1) * n],
                ]
                x_part = [v[i][at * n : (at + 1) * n] for v in (x_near, x_far)]
                grad_weight = grad_weight + dot(
                    jnp.concatenate(x_part), jnp.concatenate(g_part), FIRST
                )
        grad_weight = (grad_weight + swap(grad_weight)) / nd
    return (grad_features[None], adjoint[None], grad_weight)


def solution(mesh):
    placed = (P("dp", "blk", None), P("dp", "blk", None), P("dp", "blk"), P(), P(), P())
    return jax.shard_map(
        on_device,
        mesh=mesh,
        in_specs=placed,
        out_specs=(P("dp", "blk", None), P("dp", "blk", None), P()),
        check_vma=False,
    )
```

```python
import functools

import jax
import jax.numpy as jnp
from jax import lax
from jax.experimental import pallas as pl
from jax.experimental.pallas import tpu as pltpu
from jax.sharding import PartitionSpec as P

FIRST = (((0,), (0,)), ((), ()))
LAST = (((1,), (1,)), ((), ()))
F32 = jnp.float32
BF16 = jnp.bfloat16


def dot(a, b, dims=(((1,), (0,)), ((), ()))):
    return lax.dot_general(a, b, dims, preferred_element_type=F32)


def after(v, *others):
    return lax.optimization_barrier((v, others))[0]


def score_kernel(nz, both, embed, *refs):
    scale, offset = both[0:1, 0:1], both[8:9, 0:1]
    labels, captions, refs = refs[:2], refs[2:4], refs[4:]
    own, unit_own, inv_own, unit, dlogit = refs[:5]
    sent, (caps, sems) = refs[5:-2], refs[-2:]
    n_img, n_cap = embed.shape[0] // nz, captions[0].shape[0]
    copies = []
    for i in range(2):
        here = caps.at[i * n_cap : (i + 1) * n_cap, :]
        copies.append(pltpu.make_async_copy(captions[i], here, sems.at[i]))
        copies[-1].start()
    embed = embed[...]
    inv_norm = lax.rsqrt(jnp.sum(embed * embed, axis=1, keepdims=True) + 1e-06)
    unit_f = embed * inv_norm
    unit_own[...] = unit_f[:n_img]
    inv_own[...] = jnp.broadcast_to(inv_norm[:n_img], inv_own.shape)
    u = unit_f.astype(BF16)
    unit[...] = u
    index = lax.axis_index("blk")
    ids = []
    for k in range(nz):
        first = (index ^ (2 * k)) * n_img
        ids.append(first + lax.broadcasted_iota(jnp.int32, (n_img, 1), 0))
    ids = jnp.concatenate(ids)
    labs = jnp.concatenate([v[...] for v in labels], axis=1)
    sign = jnp.where(labs == ids, 1.0, -1.0).astype(F32)
    for copy in copies:
        copy.wait()
    logits = scale * dot(u, caps[...], LAST) + offset
    d = (-sign * jax.nn.sigmoid(-sign * logits)).astype(BF16)
    dlogit[...] = d
    part = scale * dot(d, caps[...])
    own[...] = part[:n_img]
    for k in range(1, nz):
        sent[k - 1][...] = part[k * n_img : (k + 1) * n_img].astype(BF16)


def scores(nz, both, embed, labels, captions):
    images, depth = embed.shape
    n_img, n_cap = images // nz, captions[0].shape[0]
    caps = 2 * n_cap
    vmem = pl.BlockSpec(memory_space=pltpu.VMEM)
    block = jax.ShapeDtypeStruct((n_img, depth), F32)
    outs = [
        block,
        block,
        jax.ShapeDtypeStruct((n_img, 128), F32),
        jax.ShapeDtypeStruct((images, depth), BF16),
        jax.ShapeDtypeStruct((images, caps), BF16),
    ] + [jax.ShapeDtypeStruct((n_img, depth), BF16)] * (nz - 1)
    return pl.pallas_call(
        functools.partial(score_kernel, nz),
        out_shape=outs,
        in_specs=[vmem] * 4
        + [pl.BlockSpec(memory_space=pl.ANY)] * 2,
        out_specs=[vmem] * len(outs),
        scratch_shapes=[pltpu.VMEM((caps, depth), BF16), pltpu.SemaphoreType.DMA((2,))],
        compiler_params=pltpu.CompilerParams(
            vmem_limit_bytes=12 * 2**20 + 24 * images * depth
        ),
        cost_estimate=pl.CostEstimate(
            flops=4 * images * depth * caps,
            bytes_accessed=2 * depth * (caps + 6 * images),
            transcendentals=images * caps,
        ),
    )(both, embed, *labels, *captions)


def join_kernel(*refs):
    at = 0
    for v in refs[:-1]:
        refs[-1][at : at + v.shape[0], :] = v[...]
        at += v.shape[0]


def joined(vs):
    rows = sum(v.shape[0] for v in vs)
    depth = vs[0].shape[1]
    vmem = pl.BlockSpec(memory_space=pltpu.VMEM)
    return pl.pallas_call(
        join_kernel,
        out_shape=jax.ShapeDtypeStruct((rows, depth), vs[0].dtype),
        in_specs=[vmem] * len(vs),
        out_specs=vmem,
        compiler_params=pltpu.CompilerParams(vmem_limit_bytes=12 * 2**20),
        cost_estimate=pl.CostEstimate(
            flops=0, bytes_accessed=4 * rows * depth, transcendentals=0
        ),
    )(*vs)


def caption_kernel(both, dlogit, unit, own, other):
    scale = both[0:1, 0:1]
    n_cap = own.shape[0]
    own[...] = scale * dot(dlogit[:, :n_cap], unit[...], FIRST)
    other[...] = scale * dot(dlogit[:, n_cap:], unit[...], FIRST)


def caption_sums(both, dlogit, unit):
    images, caps = dlogit.shape
    depth = unit.shape[1]
    vmem = pl.BlockSpec(memory_space=pltpu.VMEM)
    return pl.pallas_call(
        caption_kernel,
        out_shape=[jax.ShapeDtypeStruct((caps // 2, depth), F32)] * 2,
        in_specs=[vmem] * 3,
        out_specs=[vmem] * 2,
        compiler_params=pltpu.CompilerParams(
            vmem_limit_bytes=10 * 2**20 + 8 * images * depth
        ),
        cost_estimate=pl.CostEstimate(
            flops=2 * images * caps * depth,
            bytes_accessed=4 * caps * depth + 2 * images * (depth + caps),
            transcendentals=0,
        ),
    )(both, dlogit, unit)


def embed_grad_kernel(own, unit, inv_norm, *refs):
    back, out = refs[:-1], refs[-1]
    total = own[...]
    for v in back:
        total = total + v[...].astype(F32)
    u = unit[...]
    radial = jnp.sum(u * total, axis=1, keepdims=True)
    out[...] = ((total - u * radial) * inv_norm[:, :1]).astype(BF16)


def embed_grad(own, unit, inv_norm, back):
    vmem = pl.BlockSpec(memory_space=pltpu.VMEM)
    return pl.pallas_call(
        embed_grad_kernel,
        out_shape=jax.ShapeDtypeStruct(own.shape, BF16),
        in_specs=[vmem] * (3 + len(back)),
        out_specs=vmem,
        compiler_params=pltpu.CompilerParams(vmem_limit_bytes=8 * 2**20),
        cost_estimate=pl.CostEstimate(
            flops=8 * own.size, bytes_accessed=12 * own.size, transcendentals=0
        ),
    )(own, unit, inv_norm, *back)


def turn_kernel(plan, *refs):
    ins, outs = refs[: -len(plan)], refs[-len(plan) :]
    for out, pieces in zip(outs, plan):
        col = 0
        for runs in pieces:
            rows = [ins[i][at : at + size, :] for i, at, size in runs]
            rows = jnp.concatenate(rows)
            out[:, col : col + rows.shape[0]] = rows.T
            col += rows.shape[0]


def turned(xs, plan):
    depth = xs[0].shape[1]
    images = [sum(size for runs in pieces for _, _, size in runs) for pieces in plan]
    return pl.pallas_call(
        functools.partial(turn_kernel, plan),
        out_shape=[jax.ShapeDtypeStruct((depth, n), BF16) for n in images],
        in_specs=[pl.BlockSpec(memory_space=pltpu.VMEM)] * len(xs),
        out_specs=[pl.BlockSpec(memory_space=pltpu.VMEM)] * len(plan),
        compiler_params=pltpu.CompilerParams(vmem_limit_bytes=16 * 2**20),
        cost_estimate=pl.CostEstimate(
            flops=0, bytes_accessed=4 * sum(images) * depth, transcendentals=0
        ),
    )(*xs)


def stack(stacked, gs):
    at = 0
    for g in gs:
        stacked[at : at + g.shape[0], :] = g[...]
        at += g.shape[0]


def early_kernel(n, x_t, *refs):
    gs, (out, stacked) = refs[:-2], refs[-2:]
    stack(stacked, gs)
    rows = out.shape[0] // n
    for i in range(n):
        here = slice(i * rows, (i + 1) * rows)
        out[here, :] = dot(x_t[here, :], stacked[...])


def late_kernel(factor, x_t, acc, *refs):
    gs, (out, stacked, tiles, sems) = refs[:-4], refs[-4:]
    stack(stacked, gs)
    n, rows = tiles.shape[:2]
    copies = []
    for i in range(n):
        here = slice(i * rows, (i + 1) * rows)
        tiles[i] = (acc[here, :] + dot(x_t[here, :], stacked[...])) * factor
        copies.append(pltpu.make_async_copy(tiles.at[i], out.at[here, :], sems.at[i]))
        copies[-1].start()
    for copy in copies:
        copy.wait()


def weight_sum(acc, x_t, gs, factor):
    depth, images = x_t.shape
    n = 3
    early = acc is None
    vmem = pl.BlockSpec(memory_space=pltpu.VMEM)
    scratch = [pltpu.VMEM((images, depth), BF16)]
    if early:
        kernel = functools.partial(early_kernel, n)
    else:
        kernel = functools.partial(late_kernel, factor)
        scratch.append(pltpu.VMEM((n, depth // n, depth), F32))
        scratch.append(pltpu.SemaphoreType.DMA((n,)))
    operands = [x_t] + ([] if early else [acc]) + gs
    return pl.pallas_call(
        kernel,
        out_shape=jax.ShapeDtypeStruct((depth, depth), F32),
        in_specs=[vmem] * len(operands),
        out_specs=vmem if early else pl.BlockSpec(memory_space=pl.ANY),
        scratch_shapes=scratch,
        compiler_params=pltpu.CompilerParams(vmem_limit_bytes=24 * 2**20),
        cost_estimate=pl.CostEstimate(
            flops=2 * images * depth * depth,
            bytes_accessed=4 * images * depth + 4 * depth * depth * (2 - early),
            transcendentals=0,
        ),
    )(*operands)


def on_device(x, captions, labels, weight, scale, offset):
    x, captions = x[0], captions[0]
    n_img, depth = x.shape
    n_cap = captions.shape[0]
    nd, nb = lax.axis_size("dp"), lax.axis_size("blk")
    nz = nb // 2
    bits = nd.bit_length() - 1

    def along_z(v, k):
        return lax.ppermute(v, "blk", [(i, i ^ (2 * k)) for i in range(nb)])

    def swap(v):
        return lax.ppermute(v, "blk", [(i, i ^ 1) for i in range(nb)])

    def step_d(v, i):
        perm = []
        for j in range(nd):
            for m in range(nb):
                to = j ^ (1 << ((i + m % 2) % bits))
                perm.append((j * nb + m, to * nb + m))
        return lax.ppermute(v, ("dp", "blk"), perm)

    def over_d(v, first, *before):
        v = [v, first]
        for i in range(1, bits):
            v = after(jnp.concatenate(v), before)
            v = [v, step_d(v, i)]
        return v

    half = nz // 2

    def over_z(vs):
        out = list(vs)
        for k in [*range(half, nz), *range(1, half)]:
            out[k] = along_z(vs[k], k)
        return out

    xs = over_z([x] * nz)
    x_near, x_far = jnp.concatenate(xs[:half]), jnp.concatenate(xs[half:])
    x_near_first = step_d(x_near, 0)
    x_far_first = step_d(x_far, 0)
    embed = dot(joined(xs), weight)
    row = lax.broadcasted_iota(jnp.int32, (16, 128), 0)
    both = jnp.where(row < 8, scale, offset)
    own, u, inv_norm, unit, dlogit, *sent = scores(
        nz,
        both,
        embed,
        [labels, swap(labels)],
        [captions, swap(captions)],
    )
    sent = sent
    back = over_z([own] + sent)[1:]

    x_near = over_d(x_near, after(x_near_first, back))
    x_far = over_d(x_far, after(x_far_first, sent))
    back = after(back[::-1], x_far)
    ge = embed_grad(own, u, inv_norm, back)
    grad_features = dot(ge, weight, LAST)

    ges = over_z([ge] * nz)
    near, far = ges[1:half], ges[half:]
    g_own = over_d(ge, step_d(ge, 0))
    near = after(jnp.concatenate(near), g_own[0])
    near_first = step_d(near, 0)
    g_near = over_d(near, near_first)
    far = after(jnp.concatenate(far), near, grad_features)
    far_first = step_d(far, 0)
    dlogit = after(dlogit, far)
    adjoint, adjoint_other = caption_sums(both, dlogit, unit)
    adjoint = adjoint + swap(adjoint_other)
    per = nd // 2
    if nd * nb * n_img <= 2048:
        x_all = [joined(x_near), joined(x_far)]
        x_all += [swap(after(v, near)) for v in x_all]
        plan = [[], []]
        n = half * n_img
        for core in range(2):
            near_at = [(2 * core, i * n) for i in range(nd)]
            far_runs = [(2 * core + 1, i * n, n) for i in range(nd)]
            plan[0] += [
                [(i, at, n_img) for i, at in near_at],
                [(i, at + n_img, n - n_img) for i, at in near_at],
                far_runs[:per],
            ]
            plan[1] += [far_runs[per:]]
        x_early, x_late = turned(x_all, plan)
        g_own = jnp.concatenate(g_own)
        own_swapped = swap(g_own)
        g_far = over_d(far, far_first, own_swapped)
        early = [g_own, jnp.concatenate(g_near), g_far[0]]
        others = [own_swapped, swap(early[1]), swap(after(early[2], g_near[1]))]
        acc = weight_sum(None, x_early, early + others, 1.0)
        late = after(g_far[1], acc)
        grad_weight = weight_sum(acc, x_late, [late, swap(late)], 1.0 / nd)
    else:
        g_far = over_d(far, far_first)
        grad_weight = 0.0
        n = half * n_img
        for i in range(2):
            for at in range(per):
                m = n - n_img
                g_part = [
                    g_own[i][at * n_img : (at + 1) * n_img],
                    g_near[i][at * m : (at + 1) * m],
                    g_far[i][at * n : (at + 1) * n],
                ]
                x_part = [v[i][at * n : (at + 1) * n] for v in (x_near, x_far)]
                grad_weight = grad_weight + dot(
                    jnp.concatenate(x_part), jnp.concatenate(g_part), FIRST
                )
        grad_weight = (grad_weight + swap(grad_weight)) / nd
    return (grad_features[None], adjoint[None], grad_weight)


def solution(mesh):
    placed = (P("dp", "blk", None), P("dp", "blk", None), P("dp", "blk"), P(), P(), P())
    return jax.shard_map(
        on_device,
        mesh=mesh,
        in_specs=placed,
        out_specs=(P("dp", "blk", None), P("dp", "blk", None), P()),
        check_vma=False,
    )
```

```python
import functools

import jax
import jax.numpy as jnp
from jax import lax
from jax.experimental import pallas as pl
from jax.experimental.pallas import tpu as pltpu
from jax.sharding import PartitionSpec as P

FIRST = (((0,), (0,)), ((), ()))
LAST = (((1,), (1,)), ((), ()))
F32 = jnp.float32
BF16 = jnp.bfloat16


def dot(a, b, dims=(((1,), (0,)), ((), ()))):
    return lax.dot_general(a, b, dims, preferred_element_type=F32)


def after(v, *others):
    return lax.optimization_barrier((v, others))[0]


def score_kernel(nz, both, embed, *refs):
    scale, offset = both[0:1, 0:1], both[8:9, 0:1]
    labels, captions, refs = refs[:2], refs[2:4], refs[4:]
    own, unit_own, inv_own, unit, dlogit = refs[:5]
    sent, (caps, sems) = refs[5:-2], refs[-2:]
    n_img, n_cap = embed.shape[0] // nz, captions[0].shape[0]
    copies = []
    for i in range(2):
        here = caps.at[i * n_cap : (i + 1) * n_cap, :]
        copies.append(pltpu.make_async_copy(captions[i], here, sems.at[i]))
        copies[-1].start()
    embed = embed[...]
    inv_norm = lax.rsqrt(jnp.sum(embed * embed, axis=1, keepdims=True) + 1e-06)
    unit_f = embed * inv_norm
    unit_own[...] = unit_f[:n_img]
    inv_own[...] = jnp.broadcast_to(inv_norm[:n_img], inv_own.shape)
    u = unit_f.astype(BF16)
    unit[...] = u
    index = lax.axis_index("blk")
    ids = []
    for k in range(nz):
        first = (index ^ (2 * k)) * n_img
        ids.append(first + lax.broadcasted_iota(jnp.int32, (n_img, 1), 0))
    ids = jnp.concatenate(ids)
    labs = jnp.concatenate([v[...] for v in labels], axis=1)
    sign = jnp.where(labs == ids, 1.0, -1.0).astype(F32)
    for copy in copies:
        copy.wait()
    logits = scale * dot(u, caps[...], LAST) + offset
    d = (-sign * jax.nn.sigmoid(-sign * logits)).astype(BF16)
    dlogit[...] = d
    part = scale * dot(d, caps[...])
    own[...] = part[:n_img]
    for k in range(1, nz):
        sent[k - 1][...] = part[k * n_img : (k + 1) * n_img].astype(BF16)


def scores(nz, both, embed, labels, captions):
    images, depth = embed.shape
    n_img, n_cap = images // nz, captions[0].shape[0]
    caps = 2 * n_cap
    vmem = pl.BlockSpec(memory_space=pltpu.VMEM)
    block = jax.ShapeDtypeStruct((n_img, depth), F32)
    outs = [
        block,
        block,
        jax.ShapeDtypeStruct((n_img, 128), F32),
        jax.ShapeDtypeStruct((images, depth), BF16),
        jax.ShapeDtypeStruct((images, caps), BF16),
    ] + [jax.ShapeDtypeStruct((n_img, depth), BF16)] * (nz - 1)
    return pl.pallas_call(
        functools.partial(score_kernel, nz),
        out_shape=outs,
        in_specs=[vmem] * 4
        + [pl.BlockSpec(memory_space=pl.ANY)] * 2,
        out_specs=[vmem] * len(outs),
        scratch_shapes=[pltpu.VMEM((caps, depth), BF16), pltpu.SemaphoreType.DMA((2,))],
        compiler_params=pltpu.CompilerParams(
            vmem_limit_bytes=12 * 2**20 + 24 * images * depth
        ),
        cost_estimate=pl.CostEstimate(
            flops=4 * images * depth * caps,
            bytes_accessed=2 * depth * (caps + 6 * images),
            transcendentals=images * caps,
        ),
    )(both, embed, *labels, *captions)


def join_kernel(*refs):
    at = 0
    for v in refs[:-1]:
        refs[-1][at : at + v.shape[0], :] = v[...]
        at += v.shape[0]


def joined(vs):
    rows = sum(v.shape[0] for v in vs)
    depth = vs[0].shape[1]
    vmem = pl.BlockSpec(memory_space=pltpu.VMEM)
    return pl.pallas_call(
        join_kernel,
        out_shape=jax.ShapeDtypeStruct((rows, depth), vs[0].dtype),
        in_specs=[vmem] * len(vs),
        out_specs=vmem,
        compiler_params=pltpu.CompilerParams(vmem_limit_bytes=12 * 2**20),
        cost_estimate=pl.CostEstimate(
            flops=0, bytes_accessed=4 * rows * depth, transcendentals=0
        ),
    )(*vs)


def caption_kernel(both, dlogit, unit, own, other):
    scale = both[0:1, 0:1]
    n_cap = own.shape[0]
    own[...] = scale * dot(dlogit[:, :n_cap], unit[...], FIRST)
    other[...] = scale * dot(dlogit[:, n_cap:], unit[...], FIRST)


def caption_sums(both, dlogit, unit):
    images, caps = dlogit.shape
    depth = unit.shape[1]
    vmem = pl.BlockSpec(memory_space=pltpu.VMEM)
    return pl.pallas_call(
        caption_kernel,
        out_shape=[jax.ShapeDtypeStruct((caps // 2, depth), F32)] * 2,
        in_specs=[vmem] * 3,
        out_specs=[vmem] * 2,
        compiler_params=pltpu.CompilerParams(
            vmem_limit_bytes=10 * 2**20 + 8 * images * depth
        ),
        cost_estimate=pl.CostEstimate(
            flops=2 * images * caps * depth,
            bytes_accessed=4 * caps * depth + 2 * images * (depth + caps),
            transcendentals=0,
        ),
    )(both, dlogit, unit)


def embed_grad_kernel(own, unit, inv_norm, *refs):
    back, out = refs[:-1], refs[-1]
    total = own[...]
    for v in back:
        total = total + v[...].astype(F32)
    u = unit[...]
    radial = jnp.sum(u * total, axis=1, keepdims=True)
    out[...] = ((total - u * radial) * inv_norm[:, :1]).astype(BF16)


def embed_grad(own, unit, inv_norm, back):
    vmem = pl.BlockSpec(memory_space=pltpu.VMEM)
    return pl.pallas_call(
        embed_grad_kernel,
        out_shape=jax.ShapeDtypeStruct(own.shape, BF16),
        in_specs=[vmem] * (3 + len(back)),
        out_specs=vmem,
        compiler_params=pltpu.CompilerParams(vmem_limit_bytes=8 * 2**20),
        cost_estimate=pl.CostEstimate(
            flops=8 * own.size, bytes_accessed=12 * own.size, transcendentals=0
        ),
    )(own, unit, inv_norm, *back)


def turn_kernel(plan, *refs):
    ins, outs = refs[: -len(plan)], refs[-len(plan) :]
    for out, pieces in zip(outs, plan):
        col = 0
        for runs in pieces:
            rows = [ins[i][at : at + size, :] for i, at, size in runs]
            rows = jnp.concatenate(rows)
            out[:, col : col + rows.shape[0]] = rows.T
            col += rows.shape[0]


def turned(xs, plan):
    depth = xs[0].shape[1]
    images = [sum(size for runs in pieces for _, _, size in runs) for pieces in plan]
    return pl.pallas_call(
        functools.partial(turn_kernel, plan),
        out_shape=[jax.ShapeDtypeStruct((depth, n), BF16) for n in images],
        in_specs=[pl.BlockSpec(memory_space=pltpu.VMEM)] * len(xs),
        out_specs=[pl.BlockSpec(memory_space=pltpu.VMEM)] * len(plan),
        compiler_params=pltpu.CompilerParams(vmem_limit_bytes=16 * 2**20),
        cost_estimate=pl.CostEstimate(
            flops=0, bytes_accessed=4 * sum(images) * depth, transcendentals=0
        ),
    )(*xs)


def stack(stacked, gs):
    at = 0
    for g in gs:
        stacked[at : at + g.shape[0], :] = g[...]
        at += g.shape[0]


def early_kernel(n, x_t, *refs):
    gs, (out, stacked) = refs[:-2], refs[-2:]
    stack(stacked, gs)
    rows = out.shape[0] // n
    for i in range(n):
        here = slice(i * rows, (i + 1) * rows)
        out[here, :] = dot(x_t[here, :], stacked[...])


def late_kernel(factor, x_t, acc, *refs):
    gs, (out, stacked, tiles, sems) = refs[:-4], refs[-4:]
    stack(stacked, gs)
    n, rows = tiles.shape[:2]
    copies = []
    for i in range(n):
        here = slice(i * rows, (i + 1) * rows)
        tiles[i] = (acc[here, :] + dot(x_t[here, :], stacked[...])) * factor
        copies.append(pltpu.make_async_copy(tiles.at[i], out.at[here, :], sems.at[i]))
        copies[-1].start()
    for copy in copies:
        copy.wait()


def weight_sum(acc, x_t, gs, factor):
    depth, images = x_t.shape
    n = 3 if acc is None else 6
    early = acc is None
    vmem = pl.BlockSpec(memory_space=pltpu.VMEM)
    scratch = [pltpu.VMEM((images, depth), BF16)]
    if early:
        kernel = functools.partial(early_kernel, n)
    else:
        kernel = functools.partial(late_kernel, factor)
        scratch.append(pltpu.VMEM((n, depth // n, depth), F32))
        scratch.append(pltpu.SemaphoreType.DMA((n,)))
    operands = [x_t] + ([] if early else [acc]) + gs
    return pl.pallas_call(
        kernel,
        out_shape=jax.ShapeDtypeStruct((depth, depth), F32),
        in_specs=[vmem] * len(operands),
        out_specs=vmem if early else pl.BlockSpec(memory_space=pl.ANY),
        scratch_shapes=scratch,
        compiler_params=pltpu.CompilerParams(vmem_limit_bytes=24 * 2**20),
        cost_estimate=pl.CostEstimate(
            flops=2 * images * depth * depth,
            bytes_accessed=4 * images * depth + 4 * depth * depth * (2 - early),
            transcendentals=0,
        ),
    )(*operands)


def on_device(x, captions, labels, weight, scale, offset):
    x, captions = x[0], captions[0]
    n_img, depth = x.shape
    n_cap = captions.shape[0]
    nd, nb = lax.axis_size("dp"), lax.axis_size("blk")
    nz = nb // 2
    bits = nd.bit_length() - 1

    def along_z(v, k):
        return lax.ppermute(v, "blk", [(i, i ^ (2 * k)) for i in range(nb)])

    def swap(v):
        return lax.ppermute(v, "blk", [(i, i ^ 1) for i in range(nb)])

    def step_d(v, i):
        perm = []
        for j in range(nd):
            for m in range(nb):
                to = j ^ (1 << ((i + m % 2) % bits))
                perm.append((j * nb + m, to * nb + m))
        return lax.ppermute(v, ("dp", "blk"), perm)

    def over_d(v, first, *before):
        v = [v, first]
        for i in range(1, bits):
            v = after(jnp.concatenate(v), before)
            v = [v, step_d(v, i)]
        return v

    half = nz // 2

    def over_z(vs):
        out = list(vs)
        for k in [*range(half, nz), *range(1, half)]:
            out[k] = along_z(vs[k], k)
        return out

    xs = over_z([x] * nz)
    x_near, x_far = jnp.concatenate(xs[:half]), jnp.concatenate(xs[half:])
    x_near_first = step_d(x_near, 0)
    x_far_first = step_d(x_far, 0)
    embed = dot(joined(xs), weight)
    row = lax.broadcasted_iota(jnp.int32, (16, 128), 0)
    both = jnp.where(row < 8, scale, offset)
    own, u, inv_norm, unit, dlogit, *sent = scores(
        nz,
        both,
        embed,
        [labels, swap(labels)],
        [captions, swap(captions)],
    )
    sent = sent
    back = over_z([own] + sent)[1:]

    x_near = over_d(x_near, after(x_near_first, back))
    x_far = over_d(x_far, after(x_far_first, sent))
    back = after(back[::-1], x_far)
    ge = embed_grad(own, u, inv_norm, back)
    grad_features = dot(ge, weight, LAST)

    ges = over_z([ge] * nz)
    near, far = ges[1:half], ges[half:]
    g_own = over_d(ge, step_d(ge, 0))
    near = after(jnp.concatenate(near), g_own[0])
    near_first = step_d(near, 0)
    g_near = over_d(near, near_first)
    far = after(jnp.concatenate(far), near, grad_features)
    far_first = step_d(far, 0)
    dlogit = after(dlogit, far)
    adjoint, adjoint_other = caption_sums(both, dlogit, unit)
    adjoint = adjoint + swap(adjoint_other)
    per = nd // 2
    if nd * nb * n_img <= 2048:
        x_all = [joined(x_near), joined(x_far)]
        x_all += [swap(after(v, near)) for v in x_all]
        plan = [[], []]
        n = half * n_img
        for core in range(2):
            near_at = [(2 * core, i * n) for i in range(nd)]
            far_runs = [(2 * core + 1, i * n, n) for i in range(nd)]
            plan[0] += [
                [(i, at, n_img) for i, at in near_at],
                [(i, at + n_img, n - n_img) for i, at in near_at],
                far_runs[:per],
            ]
            plan[1] += [far_runs[per:]]
        x_early, x_late = turned(x_all, plan)
        g_own = jnp.concatenate(g_own)
        own_swapped = swap(g_own)
        g_far = over_d(far, far_first, own_swapped)
        early = [g_own, jnp.concatenate(g_near), g_far[0]]
        others = [own_swapped, swap(early[1]), swap(after(early[2], g_near[1]))]
        acc = weight_sum(None, x_early, early + others, 1.0)
        late = after(g_far[1], acc)
        grad_weight = weight_sum(acc, x_late, [late, swap(late)], 1.0 / nd)
    else:
        g_far = over_d(far, far_first)
        grad_weight = 0.0
        n = half * n_img
        for i in range(2):
            for at in range(per):
                m = n - n_img
                g_part = [
                    g_own[i][at * n_img : (at + 1) * n_img],
                    g_near[i][at * m : (at + 1) * m],
                    g_far[i][at * n : (at + 1) * n],
                ]
                x_part = [v[i][at * n : (at + 1) * n] for v in (x_near, x_far)]
                grad_weight = grad_weight + dot(
                    jnp.concatenate(x_part), jnp.concatenate(g_part), FIRST
                )
        grad_weight = (grad_weight + swap(grad_weight)) / nd
    return (grad_features[None], adjoint[None], grad_weight)


def solution(mesh):
    placed = (P("dp", "blk", None), P("dp", "blk", None), P("dp", "blk"), P(), P(), P())
    return jax.shard_map(
        on_device,
        mesh=mesh,
        in_specs=placed,
        out_specs=(P("dp", "blk", None), P("dp", "blk", None), P()),
        check_vma=False,
    )
```
